32 devices in a mesh: pair: 8 (over z, y), row: 4 (over x, core).
Axes of the slice: x: 2, y: 2, z: 4, core: 2. Of those that a mesh axis runs over, the one named last changes fastest.
Arguments:
- whitened: float32 [4096, 2048], P('row', 'pair'), may hold values from -50 to 50, as said below
- offsets: int32 [4, 4], replicated, may hold values from 0 to 127
Outputs:
- rotated: float32 [4096, 2048], P('row', 'pair')
- right_vectors: float32 [2048, 2048], P('row', 'pair')
The draws below stay inside these ranges and needn't reach their ends.
Inputs may be any that keep to these rules, and one draw needn't show every extreme that they name: whitened has rows and columns of different scales.
All inputs are finite; a program needn't handle non-finite values.
Results may differ from the reference program's by a relative error of at most 0.0003.
Values sent between devices are 32-bit elements; how exact they have to be, the bound alone decides.
No kernel may reach another device: no remote copies, remote signals or barrier semaphores. Data moves between devices by JAX's collectives and lax.ppermute only.
A program may use at most 64 MiB of HBM per device.

```python
import math
import jax
import jax.numpy as jnp
from jax import lax

B = 128
ROUNDS = 4
STEPS = 4
ROWS = 4096
COLS = 2048
N_PAIR = 8


def draw_whitened(key, part):
    keys = jax.random.split(key, 3)
    position = jnp.arange(ROWS, dtype=jnp.float32)
    ramp = 0.5 + position / ROWS
    row_scale = jnp.exp(jax.random.uniform(keys[1], (ROWS,), jnp.float32, math.log(0.3), math.log(3.0))) * ramp
    col_scale = jnp.exp(jax.random.uniform(keys[2], (COLS,), jnp.float32, math.log(0.5), math.log(2.0)))
    base = jnp.clip(jax.random.normal(keys[0], (ROWS, COLS), jnp.float32), -4.0, 4.0)
    return (base * row_scale[:, None] * col_scale[None, :]).astype(jnp.float32)


def plant(entries, rng, smallest, high):
    place = [jax.random.randint(jax.random.fold_in(rng, axis), (), 0, length) for axis, length in enumerate(entries.shape)]
    main_axis = entries.shape.index(max(entries.shape))
    beside = place[:main_axis] + [(place[main_axis] + 1) % entries.shape[main_axis]] + place[main_axis + 1:]
    return entries.at[tuple(place)].set(smallest).at[tuple(beside)].set(high)


def setup_inputs(seed: int = 0) -> dict:
    seeds = jax.random.split(jax.random.key(seed), 3)
    return {
        "whitened": draw_whitened(jax.random.fold_in(seeds[2], 71), 0),
        "offsets": plant(jax.random.randint(seeds[1], (STEPS, ROUNDS), 0, B), jax.random.fold_in(seeds[1], 1), 0, B - 1).astype(jnp.int32),
    }


def pair_rounds(pair_gram, step_offsets):
    full_width = pair_gram.shape[0]
    half_width = full_width // 2
    position = jnp.arange(half_width, dtype=jnp.int32)
    accumulated = jnp.eye(full_width, dtype=pair_gram.dtype)
    for round_index in range(ROUNDS):
        shift_by = step_offsets[round_index]
        permute = (position[None, :] == (position[:, None] + shift_by) % half_width).astype(pair_gram.dtype)
        diagonal = jnp.diagonal(pair_gram)
        first_diag = diagonal[:half_width]
        second = lax.optimization_barrier(jnp.sum(permute * diagonal[half_width:][None, :], axis=1))
        across = lax.optimization_barrier(jnp.sum(pair_gram[:half_width, half_width:] * permute, axis=1))
        half_gap = 0.5 * (second - first_diag)
        radius = jnp.sqrt(half_gap * half_gap + across * across)
        direction = jnp.where(half_gap >= 0, 1.0, -1.0).astype(pair_gram.dtype)
        tangent = -direction * across / (jnp.abs(half_gap) + radius + 1e-06 * (first_diag + second))
        cosine = 1.0 / jnp.sqrt(1.0 + tangent * tangent)
        sine_part = tangent * cosine
        moved_sine = sine_part[:, None] * permute
        cos_second = lax.optimization_barrier(jnp.sum(permute * cosine[:, None], axis=0))
        upper_rows = jnp.concatenate([jnp.diag(cosine), -moved_sine], axis=1)
        lower_rows = jnp.concatenate([moved_sine.T, jnp.diag(cos_second)], axis=1)
        rotation = jnp.concatenate([upper_rows, lower_rows], axis=0)
        pair_gram = jnp.dot(rotation.T, jnp.dot(pair_gram, rotation, precision=lax.Precision.HIGHEST), precision=lax.Precision.HIGHEST)
        accumulated = jnp.dot(accumulated, rotation, precision=lax.Precision.HIGHEST)
    return (pair_gram, accumulated)

def advance(stacked):
    tops = stacked[:, :, :B]
    bottoms = stacked[:, :, B:]
    new_tops = jnp.concatenate([tops[:1], bottoms[:1], tops[1:-1]], axis=0)
    new_bottoms = jnp.concatenate([bottoms[1:], tops[-1:]], axis=0)
    return jnp.concatenate([new_tops, new_bottoms], axis=2)

def reference(whitened, offsets):
    row_count = whitened.shape[0]
    col_count = whitened.shape[1]
    blocks = whitened.reshape(row_count, N_PAIR, 2 * B).transpose(1, 0, 2)
    vectors = jnp.eye(col_count, dtype=whitened.dtype).reshape(col_count, N_PAIR, 2 * B).transpose(1, 0, 2)
    for step_index in range(STEPS):
        grams = jnp.einsum('pmi,pmj->pij', blocks, blocks, precision=lax.Precision.HIGHEST)
        step_offsets = offsets[step_index]

        def solve_one(single):
            return pair_rounds(single, step_offsets)[1]
        rotations = jax.vmap(solve_one)(grams)
        blocks = jnp.einsum('pmi,pij->pmj', blocks, rotations, precision=lax.Precision.HIGHEST)
        vectors = jnp.einsum('pmi,pij->pmj', vectors, rotations, precision=lax.Precision.HIGHEST)
        if step_index + 1 < STEPS:
            blocks = advance(blocks)
            vectors = advance(vectors)
    rotated = blocks.transpose(1, 0, 2).reshape(row_count, col_count)
    right_vectors = vectors.transpose(1, 0, 2).reshape(col_count, col_count)
    return (rotated, right_vectors)
```

```python
import functools

import jax
import jax.numpy as jnp
from jax import lax
from jax.experimental import pallas as pl
from jax.experimental.pallas import tpu as pltpu
from jax.sharding import PartitionSpec as P

B = 128
ROUNDS = 4
STEPS = 4
RECORD = 2 * ROUNDS
CHUNK = 64
AXES = ("pair", "row")
PARAMS = pltpu.CompilerParams(vmem_limit_bytes=40 * 1024 * 1024)
VMEM = pl.BlockSpec(memory_space=pltpu.VMEM)
SMEM = pl.BlockSpec(memory_space=pltpu.SMEM)


def given(slot, part):
    return slot, part


def crossed(slot, part):
    return (slot & ~1) | (part & 1), (part & ~1) | (slot & 1)


def route(source, target, change):
    pairs, rows = lax.axis_size("pair"), lax.axis_size("row")
    line = []
    for slot in range(pairs):
        for part in range(rows):
            a = source(slot, part)
            b = target(*change(slot, part, pairs))
            line.append((a[0] * rows + a[1], b[0] * rows + b[1]))
    return line


def inner(slot, part, pairs):
    return slot ^ 1, part


def outer(slot, part, pairs):
    if slot == 0 or slot == pairs - 1:
        return slot, part
    return (slot + 1 if slot & 1 else slot - 1), part


def send(x, source, target, change):
    return lax.ppermute(x, AXES, route(source, target, change))


def other_part(distance):
    return lambda slot, part, pairs: (slot, part ^ distance)


def back(shift_by):
    return (B - shift_by) & (B - 1)


def eye_mask():
    shape = (B, B)
    return lax.broadcasted_iota(jnp.int32, shape, 0) == lax.broadcasted_iota(jnp.int32, shape, 1)


def diagonal(mask, block):
    return jnp.sum(jnp.where(mask, block, 0.0), axis=0, keepdims=True)


def as_column(mask, row):
    return jnp.sum(jnp.where(mask, jnp.broadcast_to(row, (B, B)), 0.0), axis=1, keepdims=True)


def solve(first, across, second, offs):
    mask = eye_mask()
    angles = []
    held = 0
    for r in range(ROUNDS):
        turn = (held - offs[r]) & (B - 1)
        held = offs[r]
        across = pltpu.roll(across, turn, 1)
        second = pltpu.roll(pltpu.roll(second, turn, 1), turn, 0)
        a = diagonal(mask, first)
        d = diagonal(mask, second)
        c0 = diagonal(mask, across)
        h = 0.5 * (d - a)
        radius = jnp.sqrt(h * h + c0 * c0)
        sg = jnp.where(h >= 0, 1.0, -1.0)
        t = -sg * c0 / (jnp.abs(h) + radius + 1e-06 * (a + d))
        c = 1.0 / jnp.sqrt(1.0 + t * t)
        s = t * c
        angles.append((c, s))
        cc, sc = as_column(mask, c), as_column(mask, s)
        below = across.T
        first1 = first * c + across * s
        across1 = across * c - first * s
        below1 = below * c + second * s
        second1 = second * c - below * s
        first = cc * first1 + sc * below1
        across = cc * across1 + sc * second1
        second = cc * second1 - sc * across1
    second = pltpu.roll(pltpu.roll(second, held, 1), held, 0)
    return angles, first, second


def rotate(first, second, angles, offs):
    held = 0
    for r in range(ROUNDS):
        c, s = angles[r]
        second = pltpu.roll(second, (held - offs[r]) & (B - 1), 1)
        held = offs[r]
        first, second = c * first + s * second, c * second - s * first
    return first, pltpu.roll(second, held, 1)


def rotate_back(first, second, angles, offs):
    held = 0
    for r in reversed(range(ROUNDS)):
        c, s = angles[r]
        second = pltpu.roll(second, (held - offs[r]) & (B - 1), 1)
        held = offs[r]
        first, second = c * first - s * second, s * first + c * second
    return first, pltpu.roll(second, held, 1)


def read_record(rows):
    return [(rows[r : r + 1], rows[ROUNDS + r : ROUNDS + r + 1]) for r in range(ROUNDS)]


def write_record(ref, at, angles):
    for r, (c, s) in enumerate(angles):
        ref[at + r : at + r + 1, :] = c
        ref[at + ROUNDS + r : at + ROUNDS + r + 1, :] = s


def tree_sum(parts):
    parts = list(parts)
    while len(parts) > 1:
        parts = [parts[i] + parts[i + 1] for i in range(0, len(parts), 2)]
    return parts[0]


def rotate_rows(rows, angles, offs, take, put):
    @pl.loop(0, rows // CHUNK)
    def _(i):
        at = pl.ds(pl.multiple_of(i * CHUNK, CHUNK), CHUNK)
        put(at, *rotate(*take(at), angles, offs))


def step_offsets(offs_ref, step):
    return [offs_ref[step, r] for r in range(ROUNDS)]


def transposed_dot(left, right):
    return lax.dot_general(
        left,
        right,
        (((0,), (0,)), ((), ())),
        precision=lax.Precision.HIGHEST,
        preferred_element_type=jnp.float32,
    )


def whole_gram_kernel(x_ref, out_ref):
    gram = transposed_dot(x_ref[...], x_ref[...])
    out_ref[0:B, :] = gram[:B, :B]
    out_ref[B : 2 * B, :] = gram[:B, B:]
    out_ref[2 * B : 3 * B, :] = gram[B:, B:]


def whole_gram(x):
    return pl.pallas_call(
        whole_gram_kernel,
        out_shape=jax.ShapeDtypeStruct((3 * B, B), jnp.float32),
        in_specs=[VMEM],
        out_specs=VMEM,
        compiler_params=PARAMS,
    )(x)


def cross_gram_kernel(rows, u_ref, w_ref, out_ref):
    out_ref[...] = transposed_dot(u_ref[:rows, :], w_ref[:rows, :])


def cross_gram(rows, u, w):
    return pl.pallas_call(
        functools.partial(cross_gram_kernel, rows),
        out_shape=jax.ShapeDtypeStruct((B, B), jnp.float32),
        in_specs=[VMEM, VMEM],
        out_specs=VMEM,
        compiler_params=PARAMS,
    )(u, w)


def first_kernel(count, offs_ref, place_ref, *refs):
    parts, (x_ref, in_ref, out_ref) = refs[:count], refs[count:]
    rows = x_ref.shape[0]
    offs = step_offsets(offs_ref, 0)
    gram = tree_sum([p[...] for p in parts])
    angles, first, second = solve(gram[:B], gram[B : 2 * B], gram[2 * B :], offs)
    slot = place_ref[0]
    swap = jnp.logical_and((slot & 1) == 0, slot != 0)

    def finish(first_ref, second_ref):
        first_ref[rows : rows + B, :] = first
        second_ref[rows : rows + B, :] = second
        write_record(first_ref, rows + B, angles)
        write_record(second_ref, rows + B, angles)

        def put(at, t, b):
            first_ref[at, :] = t
            second_ref[at, :] = b

        rotate_rows(rows, angles, offs, lambda at: (x_ref[at, :B], x_ref[at, B:]), put)

    @pl.when(swap)
    def _():
        finish(in_ref, out_ref)

    @pl.when(jnp.logical_not(swap))
    def _():
        finish(out_ref, in_ref)


def first_step(offsets, place, parts, x):
    message = jax.ShapeDtypeStruct((x.shape[0] + B + RECORD, B), jnp.float32)
    return pl.pallas_call(
        functools.partial(first_kernel, len(parts)),
        out_shape=(message, message),
        in_specs=[SMEM, SMEM] + [VMEM] * (len(parts) + 1),
        out_specs=(VMEM, VMEM),
        compiler_params=PARAMS,
    )(offsets, place, *parts, x)


def cross_solve(rows, parts, odd, u_ref, w_ref, offs):
    gram = tree_sum([p[...] for p in parts])
    across = jnp.where(odd, gram, gram.T)
    gu, gw = u_ref[rows : rows + B, :], w_ref[rows : rows + B, :]
    return solve(jnp.where(odd, gu, gw), across, jnp.where(odd, gw, gu), offs)


def middle_kernel(step, rows, count, offs_ref, place_ref, *refs):
    parts, (u_ref, w_ref, in_ref, out_ref) = refs[:count], refs[count:]
    offs = step_offsets(offs_ref, step)
    slot = place_ref[0]
    odd = (slot & 1) == 1
    angles, first, second = cross_solve(rows, parts, odd, u_ref, w_ref, offs)
    past = u_ref.shape[0] - rows - B
    base = rows + B

    def finish(top_ref, low_ref, first_ref, second_ref):
        first_ref[rows : rows + B, :] = first
        second_ref[rows : rows + B, :] = second
        for ref in (first_ref, second_ref):
            write_record(ref, base, angles)
            ref[base + RECORD : base + RECORD + past, :] = top_ref[base : base + past, :]
            ref[base + RECORD + past : base + RECORD + 2 * past, :] = low_ref[base : base + past, :]

        def put(at, t, b):
            first_ref[at, :] = t
            second_ref[at, :] = b

        rotate_rows(rows, angles, offs, lambda at: (top_ref[at, :], low_ref[at, :]), put)

    @pl.when(odd)
    def _():
        finish(u_ref, w_ref, out_ref, in_ref)

    @pl.when(jnp.logical_and(jnp.logical_not(odd), slot != 0))
    def _():
        finish(w_ref, u_ref, in_ref, out_ref)

    @pl.when(slot == 0)
    def _():
        finish(w_ref, u_ref, out_ref, in_ref)


def middle_step(step, rows, offsets, place, parts, u, w):
    past = u.shape[0] - rows - B
    message = jax.ShapeDtypeStruct((rows + B + RECORD + 2 * past, B), jnp.float32)
    return pl.pallas_call(
        functools.partial(middle_kernel, step, rows, len(parts)),
        out_shape=(message, message),
        in_specs=[SMEM, SMEM] + [VMEM] * (len(parts) + 2),
        out_specs=(VMEM, VMEM),
        compiler_params=PARAMS,
    )(offsets, place, *parts, u, w)


def came_from(slot, is_first, pairs):
    if is_first:
        return jnp.where(slot == 0, 0, slot - 1), slot != 1
    last = slot == pairs - 1
    return jnp.where(last, slot, slot + 1), last


def vectors_kernel(rows, offs_ref, place_ref, u_ref, w_ref, out_ref):
    slot, pairs, part = place_ref[0], place_ref[1], place_ref[2]
    odd = (slot & 1) == 1
    held_slots = out_ref.shape[0] // (2 * B)
    base = rows + B
    past = u_ref.shape[0] - base
    out_ref[...] = jnp.zeros_like(out_ref)
    unit = jnp.where(eye_mask(), 1.0, 0.0)

    def descend(block, node, was_first, step, history, columns):
        zero = jnp.zeros_like(block)

        def turned():
            return rotate_back(
                jnp.where(was_first, block, zero),
                jnp.where(was_first, zero, block),
                read_record(history[:RECORD]),
                step_offsets(offs_ref, step),
            )

        if step == 0:

            @pl.when(node // held_slots == part)
            def _():
                at = pl.multiple_of((node - part * held_slots) * (2 * B), 2 * B)
                top, low = turned()
                out_ref[pl.ds(at, B), columns] += top.T
                out_ref[pl.ds(at + B, B), columns] += low.T

            return
        top, low = turned()
        half = (history.shape[0] - RECORD) // 2
        older = (history[RECORD : RECORD + half], history[RECORD + half :])
        descend(top, *came_from(node, True, pairs), step - 1, older[0], columns)
        descend(low, *came_from(node, False, pairs), step - 1, older[1], columns)

    hu, hw = u_ref[base : base + past, :], w_ref[base : base + past, :]
    top_history, low_history = jnp.where(odd, hu, hw), jnp.where(odd, hw, hu)
    descend(unit, *came_from(slot, True, pairs), STEPS - 2, top_history, slice(0, B))
    descend(unit, *came_from(slot, False, pairs), STEPS - 2, low_history, slice(B, 2 * B))


def vectors_before_last(rows, height, offsets, place, u, w):
    return pl.pallas_call(
        functools.partial(vectors_kernel, rows),
        out_shape=jax.ShapeDtypeStruct((height, 2 * B), jnp.float32),
        in_specs=[SMEM, SMEM, VMEM, VMEM],
        out_specs=VMEM,
        compiler_params=PARAMS,
    )(offsets, place, u, w)


def last_kernel(rows, count, offs_ref, place_ref, *refs):
    parts, (u_ref, w_ref, v_ref, x_out, v_out) = refs[:count], refs[count:]
    offs = step_offsets(offs_ref, STEPS - 1)
    odd = (place_ref[0] & 1) == 1
    angles, _, _ = cross_solve(rows, parts, odd, u_ref, w_ref, offs)

    def put(ref):
        def store(at, t, b):
            ref[at, :B] = t
            ref[at, B:] = b

        return store

    @pl.when(odd)
    def _():
        rotate_rows(rows, angles, offs, lambda at: (u_ref[at, :], w_ref[at, :]), put(x_out))

    @pl.when(jnp.logical_not(odd))
    def _():
        rotate_rows(rows, angles, offs, lambda at: (w_ref[at, :], u_ref[at, :]), put(x_out))

    rotate_rows(
        v_ref.shape[0], angles, offs, lambda at: (v_ref[at, :B], v_ref[at, B:]), put(v_out)
    )


def last_step(rows, offsets, place, parts, u, w, v):
    return pl.pallas_call(
        functools.partial(last_kernel, rows, len(parts)),
        out_shape=(
            jax.ShapeDtypeStruct((rows, 2 * B), jnp.float32),
            jax.ShapeDtypeStruct(v.shape, jnp.float32),
        ),
        in_specs=[SMEM, SMEM] + [VMEM] * (len(parts) + 3),
        out_specs=(VMEM, VMEM),
        compiler_params=PARAMS,
    )(offsets, place, *parts, u, w, v)


def in_stages(partial, layout):
    distance, count = 1, lax.axis_size("row")
    while 2 * distance < count:
        partial = partial + send(partial, layout, layout, other_part(distance))
        distance *= 2
    if distance < count:
        return [partial, send(partial, layout, layout, other_part(distance))]
    return [partial]


def at_once(partial, layout):
    others = range(1, lax.axis_size("row"))
    return [partial] + [send(partial, layout, layout, other_part(d)) for d in others]


def body(whitened, offsets):
    rows, width = whitened.shape
    pairs, parts = lax.axis_size("pair"), lax.axis_size("row")
    pair, row = lax.axis_index("pair"), lax.axis_index("row")
    place = {
        layout: jnp.stack([layout(pair, row)[0], jnp.int32(pairs), layout(pair, row)[1]])
        for layout in (given, crossed)
    }
    height = pairs * width // parts

    terms = in_stages(whole_gram(whitened), given)
    near, far = first_step(offsets, place[given], terms, whitened)
    before = given
    for step in range(1, STEPS):
        layout = given if step == STEPS - 1 else crossed
        u = send(near, before, layout, inner)
        w = send(far, before, layout, outer)
        cross = cross_gram(rows, u, w)
        if step < STEPS - 1:
            terms = at_once(cross, layout)
            near, far = middle_step(step, rows, offsets, place[layout], terms, u, w)
        before = layout
    terms = in_stages(cross, given)
    vectors = vectors_before_last(rows, height, offsets, place[given], u, w)
    return last_step(rows, offsets, place[given], terms, u, w, vectors)


def solution(mesh):
    in_specs = (P("row", "pair"), P())
    out_specs = (P("row", "pair"), P("row", "pair"))
    return jax.shard_map(body, mesh=mesh, in_specs=in_specs, out_specs=out_specs, check_vma=False)
```

```python
import functools

import jax
import jax.numpy as jnp
from jax import lax
from jax.experimental import pallas as pl
from jax.experimental.pallas import tpu as pltpu
from jax.sharding import PartitionSpec as P

B = 128
ROUNDS = 4
STEPS = 4
RECORD = 2 * ROUNDS
AXES = ("pair", "row")
PARAMS = pltpu.CompilerParams(vmem_limit_bytes=40 * 1024 * 1024)
VMEM = pl.BlockSpec(memory_space=pltpu.VMEM)
SMEM = pl.BlockSpec(memory_space=pltpu.SMEM)


def given(slot, part):
    return slot, part


def crossed(slot, part):
    return (slot & ~1) | (part & 1), (part & ~1) | (slot & 1)


def route(source, target, change):
    pairs, rows = lax.axis_size("pair"), lax.axis_size("row")
    line = []
    for slot in range(pairs):
        for part in range(rows):
            a = source(slot, part)
            b = target(*change(slot, part, pairs))
            line.append((a[0] * rows + a[1], b[0] * rows + b[1]))
    return line


def inner(slot, part, pairs):
    return slot ^ 1, part


def outer(slot, part, pairs):
    if slot == 0 or slot == pairs - 1:
        return slot, part
    return (slot + 1 if slot & 1 else slot - 1), part


def send(x, source, target, change):
    return lax.ppermute(x, AXES, route(source, target, change))


def other_part(distance):
    return lambda slot, part, pairs: (slot, part ^ distance)


def eye_mask():
    shape = (B, B)
    return lax.broadcasted_iota(jnp.int32, shape, 0) == lax.broadcasted_iota(jnp.int32, shape, 1)


def identity_halves():
    unit = jnp.where(eye_mask(), 1.0, 0.0)
    return [(unit, jnp.zeros_like(unit)), (jnp.zeros_like(unit), unit)]


def diagonal(mask, block):
    return jnp.sum(jnp.where(mask, block, 0.0), axis=0, keepdims=True)


def as_column(mask, row):
    return jnp.sum(jnp.where(mask, jnp.broadcast_to(row, (B, B)), 0.0), axis=1, keepdims=True)


def solve(first, across, second, offs):
    mask = eye_mask()
    angles = []
    turns = identity_halves()
    held = 0
    for r in range(ROUNDS):
        turn = (held - offs[r]) & (B - 1)
        held = offs[r]
        across = pltpu.roll(across, turn, 1)
        second = pltpu.roll(pltpu.roll(second, turn, 1), turn, 0)
        turns = [(top, pltpu.roll(low, turn, 1)) for top, low in turns]
        a = diagonal(mask, first)
        d = diagonal(mask, second)
        c0 = diagonal(mask, across)
        h = 0.5 * (d - a)
        radius = jnp.sqrt(h * h + c0 * c0)
        sg = jnp.where(h >= 0, 1.0, -1.0)
        t = -sg * c0 / (jnp.abs(h) + radius + 1e-06 * (a + d))
        c = 1.0 / jnp.sqrt(1.0 + t * t)
        s = t * c
        angles.append((c, s))
        cc, sc = as_column(mask, c), as_column(mask, s)
        below = across.T
        first1 = first * c + across * s
        across1 = across * c - first * s
        below1 = below * c + second * s
        second1 = second * c - below * s
        first = cc * first1 + sc * below1
        across = cc * across1 + sc * second1
        second = cc * second1 - sc * across1
        turns = [(c * top + s * low, c * low - s * top) for top, low in turns]
    second = pltpu.roll(pltpu.roll(second, held, 1), held, 0)
    turns = [(top, pltpu.roll(low, held, 1)) for top, low in turns]
    rotation = jnp.concatenate([jnp.concatenate(t, axis=1) for t in turns], axis=0)
    return angles, rotation, first, second


def rotate_back(first, second, angles, offs):
    held = 0
    for r in reversed(range(ROUNDS)):
        c, s = angles[r]
        second = pltpu.roll(second, (held - offs[r]) & (B - 1), 1)
        held = offs[r]
        first, second = c * first - s * second, s * first + c * second
    return first, pltpu.roll(second, held, 1)


def read_record(rows):
    return [(rows[r : r + 1], rows[ROUNDS + r : ROUNDS + r + 1]) for r in range(ROUNDS)]


def write_record(ref, at, angles):
    for r, (c, s) in enumerate(angles):
        ref[at + r : at + r + 1, :] = c
        ref[at + ROUNDS + r : at + ROUNDS + r + 1, :] = s


def tree_sum(parts):
    parts = list(parts)
    while len(parts) > 1:
        parts = [parts[i] + parts[i + 1] for i in range(0, len(parts), 2)]
    return parts[0]


def split(x):
    high = x.astype(jnp.bfloat16)
    return high, (x - high.astype(jnp.float32)).astype(jnp.bfloat16)


def product(x, rotation):
    xh, xl = split(x)
    rh, rl = split(rotation)

    def dot(a, b):
        return jnp.dot(a, b, preferred_element_type=jnp.float32)

    return (dot(xl, rh) + dot(xh, rl)) + dot(xh, rh)


def step_offsets(offs_ref, step):
    return [offs_ref[step, r] for r in range(ROUNDS)]


def transposed_dot(left, right):
    return lax.dot_general(
        left,
        right,
        (((0,), (0,)), ((), ())),
        precision=lax.Precision.HIGHEST,
        preferred_element_type=jnp.float32,
    )


def whole_gram_kernel(x_ref, out_ref):
    gram = transposed_dot(x_ref[...], x_ref[...])
    out_ref[0:B, :] = gram[:B, :B]
    out_ref[B : 2 * B, :] = gram[:B, B:]
    out_ref[2 * B : 3 * B, :] = gram[B:, B:]


def whole_gram(x):
    return pl.pallas_call(
        whole_gram_kernel,
        out_shape=jax.ShapeDtypeStruct((3 * B, B), jnp.float32),
        in_specs=[VMEM],
        out_specs=VMEM,
        compiler_params=PARAMS,
    )(x)


def cross_gram_kernel(rows, u_ref, w_ref, out_ref):
    out_ref[...] = transposed_dot(u_ref[:rows, :], w_ref[:rows, :])


def cross_gram(rows, u, w):
    return pl.pallas_call(
        functools.partial(cross_gram_kernel, rows),
        out_shape=jax.ShapeDtypeStruct((B, B), jnp.float32),
        in_specs=[VMEM, VMEM],
        out_specs=VMEM,
        compiler_params=PARAMS,
    )(u, w)


def first_kernel(count, offs_ref, place_ref, *refs):
    parts, (x_ref, in_ref, out_ref) = refs[:count], refs[count:]
    rows = x_ref.shape[0]
    offs = step_offsets(offs_ref, 0)
    gram = tree_sum([p[...] for p in parts])
    angles, rotation, first, second = solve(gram[:B], gram[B : 2 * B], gram[2 * B :], offs)
    slot = place_ref[0]
    swap = jnp.logical_and((slot & 1) == 0, slot != 0)

    def finish(first_ref, second_ref):
        first_ref[rows : rows + B, :] = first
        second_ref[rows : rows + B, :] = second
        write_record(first_ref, rows + B, angles)
        write_record(second_ref, rows + B, angles)

        x = product(x_ref[...], rotation)
        first_ref[:rows, :] = x[:, :B]
        second_ref[:rows, :] = x[:, B:]

    @pl.when(swap)
    def _():
        finish(in_ref, out_ref)

    @pl.when(jnp.logical_not(swap))
    def _():
        finish(out_ref, in_ref)


def first_step(offsets, place, parts, x):
    message = jax.ShapeDtypeStruct((x.shape[0] + B + RECORD, B), jnp.float32)
    return pl.pallas_call(
        functools.partial(first_kernel, len(parts)),
        out_shape=(message, message),
        in_specs=[SMEM, SMEM] + [VMEM] * (len(parts) + 1),
        out_specs=(VMEM, VMEM),
        compiler_params=PARAMS,
    )(offsets, place, *parts, x)


def cross_solve(rows, parts, odd, u_ref, w_ref, offs):
    gram = tree_sum([p[...] for p in parts])
    across = jnp.where(odd, gram, gram.T)
    gu, gw = u_ref[rows : rows + B, :], w_ref[rows : rows + B, :]
    return solve(jnp.where(odd, gu, gw), across, jnp.where(odd, gw, gu), offs)


def middle_kernel(step, rows, count, offs_ref, place_ref, *refs):
    parts, (u_ref, w_ref, in_ref, out_ref) = refs[:count], refs[count:]
    offs = step_offsets(offs_ref, step)
    slot = place_ref[0]
    odd = (slot & 1) == 1
    angles, rotation, first, second = cross_solve(rows, parts, odd, u_ref, w_ref, offs)
    past = u_ref.shape[0] - rows - B
    base = rows + B

    def finish(top_ref, low_ref, first_ref, second_ref):
        first_ref[rows : rows + B, :] = first
        second_ref[rows : rows + B, :] = second
        for ref in (first_ref, second_ref):
            write_record(ref, base, angles)
            ref[base + RECORD : base + RECORD + past, :] = top_ref[base : base + past, :]
            ref[base + RECORD + past : base + RECORD + 2 * past, :] = low_ref[base : base + past, :]

        x = product(jnp.concatenate([top_ref[:rows, :], low_ref[:rows, :]], axis=1), rotation)
        first_ref[:rows, :] = x[:, :B]
        second_ref[:rows, :] = x[:, B:]

    @pl.when(odd)
    def _():
        finish(u_ref, w_ref, out_ref, in_ref)

    @pl.when(jnp.logical_and(jnp.logical_not(odd), slot != 0))
    def _():
        finish(w_ref, u_ref, in_ref, out_ref)

    @pl.when(slot == 0)
    def _():
        finish(w_ref, u_ref, out_ref, in_ref)


def middle_step(step, rows, offsets, place, parts, u, w):
    past = u.shape[0] - rows - B
    message = jax.ShapeDtypeStruct((rows + B + RECORD + 2 * past, B), jnp.float32)
    return pl.pallas_call(
        functools.partial(middle_kernel, step, rows, len(parts)),
        out_shape=(message, message),
        in_specs=[SMEM, SMEM] + [VMEM] * (len(parts) + 2),
        out_specs=(VMEM, VMEM),
        compiler_params=PARAMS,
    )(offsets, place, *parts, u, w)


def came_from(slot, is_first, pairs):
    if is_first:
        return jnp.where(slot == 0, 0, slot - 1), slot != 1
    last = slot == pairs - 1
    return jnp.where(last, slot, slot + 1), last


def vectors_kernel(rows, offs_ref, place_ref, u_ref, w_ref, out_ref):
    slot, pairs, part = place_ref[0], place_ref[1], place_ref[2]
    odd = (slot & 1) == 1
    held_slots = out_ref.shape[0] // (2 * B)
    base = rows + B
    past = u_ref.shape[0] - base
    out_ref[...] = jnp.zeros_like(out_ref)
    unit = jnp.where(eye_mask(), 1.0, 0.0)

    def descend(block, node, was_first, step, history, columns):
        zero = jnp.zeros_like(block)

        def turned():
            return rotate_back(
                jnp.where(was_first, block, zero),
                jnp.where(was_first, zero, block),
                read_record(history[:RECORD]),
                step_offsets(offs_ref, step),
            )

        if step == 0:

            @pl.when(node // held_slots == part)
            def _():
                at = pl.multiple_of((node - part * held_slots) * (2 * B), 2 * B)
                top, low = turned()
                out_ref[pl.ds(at, B), columns] += top.T
                out_ref[pl.ds(at + B, B), columns] += low.T

            return
        top, low = turned()
        half = (history.shape[0] - RECORD) // 2
        older = (history[RECORD : RECORD + half], history[RECORD + half :])
        descend(top, *came_from(node, True, pairs), step - 1, older[0], columns)
        descend(low, *came_from(node, False, pairs), step - 1, older[1], columns)

    hu, hw = u_ref[base : base + past, :], w_ref[base : base + past, :]
    top_history, low_history = jnp.where(odd, hu, hw), jnp.where(odd, hw, hu)
    descend(unit, *came_from(slot, True, pairs), STEPS - 2, top_history, slice(0, B))
    descend(unit, *came_from(slot, False, pairs), STEPS - 2, low_history, slice(B, 2 * B))


def vectors_before_last(rows, height, offsets, place, u, w):
    return pl.pallas_call(
        functools.partial(vectors_kernel, rows),
        out_shape=jax.ShapeDtypeStruct((height, 2 * B), jnp.float32),
        in_specs=[SMEM, SMEM, VMEM, VMEM],
        out_specs=VMEM,
        compiler_params=PARAMS,
    )(offsets, place, u, w)


def last_kernel(rows, count, offs_ref, place_ref, *refs):
    parts, (u_ref, w_ref, v_ref, x_out, v_out) = refs[:count], refs[count:]
    offs = step_offsets(offs_ref, STEPS - 1)
    odd = (place_ref[0] & 1) == 1
    _, rotation, _, _ = cross_solve(rows, parts, odd, u_ref, w_ref, offs)

    @pl.when(odd)
    def _():
        x_out[...] = product(jnp.concatenate([u_ref[:rows, :], w_ref[:rows, :]], axis=1), rotation)

    @pl.when(jnp.logical_not(odd))
    def _():
        x_out[...] = product(jnp.concatenate([w_ref[:rows, :], u_ref[:rows, :]], axis=1), rotation)

    v_out[...] = product(v_ref[...], rotation)


def last_step(rows, offsets, place, parts, u, w, v):
    return pl.pallas_call(
        functools.partial(last_kernel, rows, len(parts)),
        out_shape=(
            jax.ShapeDtypeStruct((rows, 2 * B), jnp.float32),
            jax.ShapeDtypeStruct(v.shape, jnp.float32),
        ),
        in_specs=[SMEM, SMEM] + [VMEM] * (len(parts) + 3),
        out_specs=(VMEM, VMEM),
        compiler_params=PARAMS,
    )(offsets, place, *parts, u, w, v)


def in_stages(partial, layout):
    distance, count = 1, lax.axis_size("row")
    while 2 * distance < count:
        partial = partial + send(partial, layout, layout, other_part(distance))
        distance *= 2
    if distance < count:
        return [partial, send(partial, layout, layout, other_part(distance))]
    return [partial]


def at_once(partial, layout):
    others = range(1, lax.axis_size("row"))
    return [partial] + [send(partial, layout, layout, other_part(d)) for d in others]


def body(whitened, offsets):
    rows, width = whitened.shape
    pairs, parts = lax.axis_size("pair"), lax.axis_size("row")
    pair, row = lax.axis_index("pair"), lax.axis_index("row")
    place = {
        layout: jnp.stack([layout(pair, row)[0], jnp.int32(pairs), layout(pair, row)[1]])
        for layout in (given, crossed)
    }
    height = pairs * width // parts

    terms = in_stages(whole_gram(whitened), given)
    near, far = first_step(offsets, place[given], terms, whitened)
    before = given
    for step in range(1, STEPS):
        layout = given if step == STEPS - 1 else crossed
        u = send(near, before, layout, inner)
        w = send(far, before, layout, outer)
        cross = cross_gram(rows, u, w)
        if step < STEPS - 1:
            terms = at_once(cross, layout)
            near, far = middle_step(step, rows, offsets, place[layout], terms, u, w)
        before = layout
    terms = in_stages(cross, given)
    vectors = vectors_before_last(rows, height, offsets, place[given], u, w)
    return last_step(rows, offsets, place[given], terms, u, w, vectors)


def solution(mesh):
    in_specs = (P("row", "pair"), P())
    out_specs = (P("row", "pair"), P("row", "pair"))
    return jax.shard_map(body, mesh=mesh, in_specs=in_specs, out_specs=out_specs, check_vma=False)
```

```python
import functools

import jax
import jax.numpy as jnp
from jax import lax
from jax.experimental import pallas as pl
from jax.experimental.pallas import tpu as pltpu
from jax.sharding import PartitionSpec as P

B = 128
ROUNDS = 4
STEPS = 4
RECORD = 2 * ROUNDS
AXES = ("pair", "row")
PARAMS = pltpu.CompilerParams(vmem_limit_bytes=40 * 1024 * 1024)
VMEM = pl.BlockSpec(memory_space=pltpu.VMEM)
SMEM = pl.BlockSpec(memory_space=pltpu.SMEM)


def given(slot, part):
    return slot, part


def crossed(slot, part):
    return (slot & ~1) | (part & 1), (part & ~1) | (slot & 1)


def route(source, target, change):
    pairs, rows = lax.axis_size("pair"), lax.axis_size("row")
    line = []
    for slot in range(pairs):
        for part in range(rows):
            a = source(slot, part)
            b = target(*change(slot, part, pairs))
            line.append((a[0] * rows + a[1], b[0] * rows + b[1]))
    return line


def inner(slot, part, pairs):
    return slot ^ 1, part


def outer(slot, part, pairs):
    if slot == 0 or slot == pairs - 1:
        return slot, part
    return (slot + 1 if slot & 1 else slot - 1), part


def send(x, source, target, change):
    return lax.ppermute(x, AXES, route(source, target, change))


def other_part(distance):
    return lambda slot, part, pairs: (slot, part ^ distance)


def eye_mask():
    shape = (B, B)
    return lax.broadcasted_iota(jnp.int32, shape, 0) == lax.broadcasted_iota(jnp.int32, shape, 1)


def identity_halves():
    unit = jnp.where(eye_mask(), 1.0, 0.0)
    return [(unit, jnp.zeros_like(unit)), (jnp.zeros_like(unit), unit)]


def diagonal(mask, block):
    return jnp.sum(jnp.where(mask, block, 0.0), axis=0, keepdims=True)


def as_column(mask, row):
    return jnp.sum(jnp.where(mask, jnp.broadcast_to(row, (B, B)), 0.0), axis=1, keepdims=True)


def solve(first, across, second, offs):
    mask = eye_mask()
    angles = []
    turns = identity_halves()
    held = 0
    for r in range(ROUNDS):
        turn = (held - offs[r]) & (B - 1)
        held = offs[r]
        across = pltpu.roll(across, turn, 1)
        second = pltpu.roll(pltpu.roll(second, turn, 1), turn, 0)
        turns = [(top, pltpu.roll(low, turn, 1)) for top, low in turns]
        a = diagonal(mask, first)
        d = diagonal(mask, second)
        c0 = diagonal(mask, across)
        h = 0.5 * (d - a)
        radius = jnp.sqrt(h * h + c0 * c0)
        sg = jnp.where(h >= 0, 1.0, -1.0)
        t = -sg * c0 / (jnp.abs(h) + radius + 1e-06 * (a + d))
        c = 1.0 / jnp.sqrt(1.0 + t * t)
        s = t * c
        angles.append((c, s))
        cc, sc = as_column(mask, c), as_column(mask, s)
        below = across.T
        first1 = first * c + across * s
        across1 = across * c - first * s
        below1 = below * c + second * s
        second1 = second * c - below * s
        first = cc * first1 + sc * below1
        across = cc * across1 + sc * second1
        second = cc * second1 - sc * across1
        turns = [(c * top + s * low, c * low - s * top) for top, low in turns]
    second = pltpu.roll(pltpu.roll(second, held, 1), held, 0)
    turns = [(top, pltpu.roll(low, held, 1)) for top, low in turns]
    rotation = jnp.concatenate([jnp.concatenate(t, axis=1) for t in turns], axis=0)
    return angles, rotation, first, second


def rotate(first, second, angles, offs):
    held = 0
    for r in range(ROUNDS):
        c, s = angles[r]
        second = pltpu.roll(second, (held - offs[r]) & (B - 1), 1)
        held = offs[r]
        first, second = c * first + s * second, c * second - s * first
    return first, pltpu.roll(second, held, 1)


def rotate_back(first, second, angles, offs):
    held = 0
    for r in reversed(range(ROUNDS)):
        c, s = angles[r]
        second = pltpu.roll(second, (held - offs[r]) & (B - 1), 1)
        held = offs[r]
        first, second = c * first - s * second, s * first + c * second
    return first, pltpu.roll(second, held, 1)


def read_record(rows):
    return [(rows[r : r + 1], rows[ROUNDS + r : ROUNDS + r + 1]) for r in range(ROUNDS)]


def write_record(ref, at, angles):
    for r, (c, s) in enumerate(angles):
        ref[at + r : at + r + 1, :] = c
        ref[at + ROUNDS + r : at + ROUNDS + r + 1, :] = s


def tree_sum(parts):
    parts = list(parts)
    while len(parts) > 1:
        parts = [parts[i] + parts[i + 1] for i in range(0, len(parts), 2)]
    return parts[0]


def split(x):
    high = x.astype(jnp.bfloat16)
    return high, (x - high.astype(jnp.float32)).astype(jnp.bfloat16)


def product(x, rotation):
    xh, xl = split(x)
    rh, rl = split(rotation)

    def dot(a, b):
        return jnp.dot(a, b, preferred_element_type=jnp.float32)

    return (dot(xl, rh) + dot(xh, rl)) + dot(xh, rh)


def step_offsets(offs_ref, step):
    return [offs_ref[step, r] for r in range(ROUNDS)]


def transposed_dot(left, right):
    return lax.dot_general(
        left,
        right,
        (((0,), (0,)), ((), ())),
        precision=lax.Precision.HIGHEST,
        preferred_element_type=jnp.float32,
    )


def whole_gram_kernel(x_ref, out_ref):
    gram = transposed_dot(x_ref[...], x_ref[...])
    out_ref[0:B, :] = gram[:B, :B]
    out_ref[B : 2 * B, :] = gram[:B, B:]
    out_ref[2 * B : 3 * B, :] = gram[B:, B:]


def whole_gram(x):
    return pl.pallas_call(
        whole_gram_kernel,
        out_shape=jax.ShapeDtypeStruct((3 * B, B), jnp.float32),
        in_specs=[VMEM],
        out_specs=VMEM,
        compiler_params=PARAMS,
    )(x)


def cross_gram_kernel(rows, u_ref, w_ref, out_ref):
    out_ref[...] = transposed_dot(u_ref[:rows, :], w_ref[:rows, :])


def cross_gram(rows, u, w):
    return pl.pallas_call(
        functools.partial(cross_gram_kernel, rows),
        out_shape=jax.ShapeDtypeStruct((B, B), jnp.float32),
        in_specs=[VMEM, VMEM],
        out_specs=VMEM,
        compiler_params=PARAMS,
    )(u, w)


def joined_gram_kernel(place_ref, u_ref, w_ref, x_ref, gram_ref):
    rows = x_ref.shape[0]
    u, w = u_ref[:rows, :], w_ref[:rows, :]
    odd = (place_ref[0] & 1) == 1

    @pl.when(odd)
    def _():
        x_ref[:, :B] = u
        x_ref[:, B:] = w

    @pl.when(jnp.logical_not(odd))
    def _():
        x_ref[:, :B] = w
        x_ref[:, B:] = u

    gram_ref[...] = transposed_dot(u, w)


def joined_gram(rows, place, u, w):
    return pl.pallas_call(
        joined_gram_kernel,
        out_shape=(
            jax.ShapeDtypeStruct((rows, 2 * B), jnp.float32),
            jax.ShapeDtypeStruct((B, B), jnp.float32),
        ),
        in_specs=[SMEM, VMEM, VMEM],
        out_specs=(VMEM, VMEM),
        compiler_params=PARAMS,
    )(place, u, w)


def write_messages(near_ref, far_ref, near_base, far_base, slot, first, second, angles, past):
    swap = jnp.logical_and((slot & 1) == 0, slot != 0)
    near_ref[near_base : near_base + B, :] = jnp.where(swap, first, second)
    far_ref[far_base : far_base + B, :] = jnp.where(swap, second, first)
    for ref, at in ((near_ref, near_base + B), (far_ref, far_base + B)):
        write_record(ref, at, angles)
        at += RECORD
        for history in past:
            ref[at : at + history.shape[0], :] = history
            at += history.shape[0]


def write_blocks(near_ref, far_ref, rows, slot, x):
    swap = jnp.logical_and((slot & 1) == 0, slot != 0)

    @pl.when(swap)
    def _():
        near_ref[:rows, :] = x[:, :B]
        far_ref[:rows, :] = x[:, B:]

    @pl.when(jnp.logical_not(swap))
    def _():
        far_ref[:rows, :] = x[:, :B]
        near_ref[:rows, :] = x[:, B:]


def first_kernel(count, offs_ref, place_ref, *refs):
    parts, (x_ref, near_ref, far_ref) = refs[:count], refs[count:]
    rows = x_ref.shape[0]
    gram = tree_sum([p[...] for p in parts])
    offs = step_offsets(offs_ref, 0)
    angles, rotation, first, second = solve(gram[:B], gram[B : 2 * B], gram[2 * B :], offs)
    slot = place_ref[0]
    write_messages(near_ref, far_ref, rows, rows, slot, first, second, angles, ())
    write_blocks(near_ref, far_ref, rows, slot, product(x_ref[...], rotation))


def first_step(offsets, place, parts, x):
    message = jax.ShapeDtypeStruct((x.shape[0] + B + RECORD, B), jnp.float32)
    return pl.pallas_call(
        functools.partial(first_kernel, len(parts)),
        out_shape=(message, message),
        in_specs=[SMEM, SMEM] + [VMEM] * (len(parts) + 1),
        out_specs=(VMEM, VMEM),
        compiler_params=PARAMS,
    )(offsets, place, *parts, x)


def half_rotation(angles, offs, take_first):
    halves = [rotate(top, low, angles, offs) for top, low in identity_halves()]
    return jnp.concatenate([jnp.where(take_first, top, low) for top, low in halves], axis=0)


def arrive_kernel(step, offs_ref, place_ref, u_ref, w_ref, xw_ref, x_ref, gram_ref):
    rows = xw_ref.shape[0]
    slot, pairs = place_ref[0], place_ref[1]
    odd = (slot & 1) == 1
    takes_first = jnp.logical_or(jnp.logical_not(odd), slot == pairs - 1)
    angles = read_record(w_ref[B : B + RECORD, :])
    w = product(xw_ref[...], half_rotation(angles, step_offsets(offs_ref, step), takes_first))
    u = u_ref[:rows, :]

    @pl.when(odd)
    def _():
        x_ref[:, :B] = u
        x_ref[:, B:] = w

    @pl.when(jnp.logical_not(odd))
    def _():
        x_ref[:, :B] = w
        x_ref[:, B:] = u

    gram_ref[...] = transposed_dot(u, w)


def arrive(step, offsets, place, u, w, xw):
    return pl.pallas_call(
        functools.partial(arrive_kernel, step),
        out_shape=(
            jax.ShapeDtypeStruct(xw.shape, jnp.float32),
            jax.ShapeDtypeStruct((B, B), jnp.float32),
        ),
        in_specs=[SMEM, SMEM] + [VMEM] * 3,
        out_specs=(VMEM, VMEM),
        compiler_params=PARAMS,
    )(offsets, place, u, w, xw)


def cross_solve(u_base, w_base, parts, odd, u_ref, w_ref, offs):
    gram = tree_sum([p[...] for p in parts])
    across = jnp.where(odd, gram, gram.T)
    gu, gw = u_ref[u_base : u_base + B, :], w_ref[w_base : w_base + B, :]
    return solve(jnp.where(odd, gu, gw), across, jnp.where(odd, gw, gu), offs)


def older(odd, u_base, w_base, u_ref, w_ref):
    hu, hw = u_ref[u_base + B :, :], w_ref[w_base + B :, :]
    return jnp.where(odd, hu, hw), jnp.where(odd, hw, hu)


def middle_kernel(step, bases, sent, count, offs_ref, place_ref, *refs):
    parts, (u_ref, w_ref, x_ref, near_ref, far_ref) = refs[:count], refs[count:]
    rows = x_ref.shape[0]
    slot = place_ref[0]
    odd = (slot & 1) == 1
    offs = step_offsets(offs_ref, step)
    angles, rotation, first, second = cross_solve(*bases, parts, odd, u_ref, w_ref, offs)
    past = older(odd, *bases, u_ref, w_ref)
    far_base = 0 if sent else rows
    write_messages(near_ref, far_ref, rows, far_base, slot, first, second, angles, past)
    if not sent:
        write_blocks(near_ref, far_ref, rows, slot, product(x_ref[...], rotation))
        return
    takes_first = jnp.logical_and(jnp.logical_not(odd), slot != 0)
    half = jnp.where(takes_first, rotation[:, :B], rotation[:, B:])
    near_ref[:rows, :] = product(x_ref[...], half)


def middle_step(step, bases, sent, offsets, place, parts, u, w, x):
    rows = x.shape[0]
    small = B + RECORD + 2 * (u.shape[0] - bases[0] - B)
    near = jax.ShapeDtypeStruct((rows + small, B), jnp.float32)
    far = jax.ShapeDtypeStruct((small, B), jnp.float32) if sent else near
    return pl.pallas_call(
        functools.partial(middle_kernel, step, bases, sent, len(parts)),
        out_shape=(near, far),
        in_specs=[SMEM, SMEM] + [VMEM] * (len(parts) + 3),
        out_specs=(VMEM, VMEM),
        compiler_params=PARAMS,
    )(offsets, place, *parts, u, w, x)


def came_from(slot, is_first, pairs):
    if is_first:
        return jnp.where(slot == 0, 0, slot - 1), slot != 1
    last = slot == pairs - 1
    return jnp.where(last, slot, slot + 1), last


def vectors_kernel(rows, offs_ref, place_ref, u_ref, w_ref, out_ref):
    slot, pairs, part = place_ref[0], place_ref[1], place_ref[2]
    odd = (slot & 1) == 1
    held_slots = out_ref.shape[0] // (2 * B)
    unit = jnp.where(eye_mask(), 1.0, 0.0)
    zero = jnp.zeros_like(unit)
    pasts = older(odd, rows, rows, u_ref, w_ref)
    nodes = [
        (unit, *came_from(slot, is_first, pairs), past, at)
        for is_first, past, at in ((True, pasts[0], 0), (False, pasts[1], B))
    ]
    for step in reversed(range(STEPS - 1)):
        offs = step_offsets(offs_ref, step)
        below = []
        for block, node, was_first, past, at in nodes:
            top, low = rotate_back(
                jnp.where(was_first, block, zero),
                jnp.where(was_first, zero, block),
                read_record(past[:RECORD]),
                offs,
            )
            if step == 0:
                below.append((top, low, node, at))
                continue
            half = (past.shape[0] - RECORD) // 2
            top_past, low_past = past[RECORD : RECORD + half], past[RECORD + half :]
            below.append((top, *came_from(node, True, pairs), top_past, at))
            below.append((low, *came_from(node, False, pairs), low_past, at))
        nodes = below
    out_ref[...] = jnp.zeros_like(out_ref)
    for top, low, node, column in nodes:

        @pl.when(node // held_slots == part)
        def _():
            at = pl.multiple_of((node - part * held_slots) * (2 * B), 2 * B)
            out_ref[pl.ds(at, B), column : column + B] += top.T
            out_ref[pl.ds(at + B, B), column : column + B] += low.T


def vectors_before_last(rows, height, offsets, place, u, w):
    return pl.pallas_call(
        functools.partial(vectors_kernel, rows),
        out_shape=jax.ShapeDtypeStruct((height, 2 * B), jnp.float32),
        in_specs=[SMEM, SMEM, VMEM, VMEM],
        out_specs=VMEM,
        compiler_params=PARAMS,
    )(offsets, place, u, w)


def last_kernel(rows, count, offs_ref, place_ref, *refs):
    parts, (u_ref, w_ref, v_ref, x_out, v_out) = refs[:count], refs[count:]
    offs = step_offsets(offs_ref, STEPS - 1)
    odd = (place_ref[0] & 1) == 1
    _, rotation, _, _ = cross_solve(rows, rows, parts, odd, u_ref, w_ref, offs)

    @pl.when(odd)
    def _():
        x_out[...] = product(jnp.concatenate([u_ref[:rows, :], w_ref[:rows, :]], axis=1), rotation)

    @pl.when(jnp.logical_not(odd))
    def _():
        x_out[...] = product(jnp.concatenate([w_ref[:rows, :], u_ref[:rows, :]], axis=1), rotation)

    v_out[...] = product(v_ref[...], rotation)


def last_step(rows, offsets, place, parts, u, w, v):
    return pl.pallas_call(
        functools.partial(last_kernel, rows, len(parts)),
        out_shape=(
            jax.ShapeDtypeStruct((rows, 2 * B), jnp.float32),
            jax.ShapeDtypeStruct(v.shape, jnp.float32),
        ),
        in_specs=[SMEM, SMEM] + [VMEM] * (len(parts) + 3),
        out_specs=(VMEM, VMEM),
        compiler_params=PARAMS,
    )(offsets, place, *parts, u, w, v)


def in_stages(partial, layout):
    distance, count = 1, lax.axis_size("row")
    while 2 * distance < count:
        partial = partial + send(partial, layout, layout, other_part(distance))
        distance *= 2
    if distance < count:
        return [partial, send(partial, layout, layout, other_part(distance))]
    return [partial]


def at_once(partial, layout):
    others = range(1, lax.axis_size("row"))
    return [partial] + [send(partial, layout, layout, other_part(d)) for d in others]


def body(whitened, offsets):
    rows, width = whitened.shape
    pairs, parts = lax.axis_size("pair"), lax.axis_size("row")
    pair, row = lax.axis_index("pair"), lax.axis_index("row")
    place = {
        layout: jnp.stack([layout(pair, row)[0], jnp.int32(pairs), layout(pair, row)[1]])
        for layout in (given, crossed)
    }
    height = pairs * width // parts

    terms = in_stages(whole_gram(whitened), given)
    near, far = first_step(offsets, place[given], terms, whitened)
    u = send(near, given, crossed, inner)
    w = send(far, given, crossed, outer)
    x, cross = joined_gram(rows, place[crossed], u, w)
    ahead = send(x, crossed, crossed, outer)
    terms = at_once(cross, crossed)
    near, far = middle_step(1, (rows, rows), True, offsets, place[crossed], terms, u, w, x)
    u = send(near, crossed, crossed, inner)
    w = send(far, crossed, crossed, outer)
    x, cross = arrive(1, offsets, place[crossed], u, w, ahead)
    terms = at_once(cross, crossed)
    near, far = middle_step(2, (rows, 0), False, offsets, place[crossed], terms, u, w, x)
    u = send(near, crossed, given, inner)
    w = send(far, crossed, given, outer)
    terms = in_stages(cross_gram(rows, u, w), given)
    vectors = vectors_before_last(rows, height, offsets, place[given], u, w)
    return last_step(rows, offsets, place[given], terms, u, w, vectors)


def solution(mesh):
    in_specs = (P("row", "pair"), P())
    out_specs = (P("row", "pair"), P("row", "pair"))
    return jax.shard_map(body, mesh=mesh, in_specs=in_specs, out_specs=out_specs, check_vma=False)
```

```python
import functools

import jax
import jax.numpy as jnp
from jax import lax
from jax.experimental import pallas as pl
from jax.experimental.pallas import tpu as pltpu
from jax.sharding import PartitionSpec as P

B = 128
ROUNDS = 4
STEPS = 4
RECORD = 2 * ROUNDS
HALF = B // 2
PACKED = HALF + 8
AXES = ("pair", "row")
PARAMS = pltpu.CompilerParams(vmem_limit_bytes=40 * 1024 * 1024)
VMEM = pl.BlockSpec(memory_space=pltpu.VMEM)


def given(slot, part):
    return slot, part


def crossed(slot, part):
    return (slot & ~1) | (part & 1), (part & ~1) | (slot & 1)


def route(source, target, change, swap=True):
    pairs, rows = lax.axis_size("pair"), lax.axis_size("row")
    line = []
    for slot in range(pairs):
        for part in range(rows):
            a = source(slot, part)
            b = target(*change(slot, part, pairs))
            if swap and a == b:
                b = a[0], a[1] ^ (rows // 2)
            line.append((a[0] * rows + a[1], b[0] * rows + b[1]))
    return line


def inner(slot, part, pairs):
    return slot ^ 1, part


def outer(slot, part, pairs):
    if slot == 0 or slot == pairs - 1:
        return slot, part
    return (slot + 1 if slot & 1 else slot - 1), part


def send(x, source, target, change, swap=True):
    return lax.ppermute(x, AXES, route(source, target, change, swap))


def other_part(distance):
    return lambda slot, part, pairs: (slot, part ^ distance)


def eye_mask():
    shape = (B, B)
    return lax.broadcasted_iota(jnp.int32, shape, 0) == lax.broadcasted_iota(jnp.int32, shape, 1)


def identity_halves():
    unit = jnp.where(eye_mask(), 1.0, 0.0)
    return [(unit, jnp.zeros_like(unit)), (jnp.zeros_like(unit), unit)]


def diagonal(mask, block):
    return jnp.sum(jnp.where(mask, block, 0.0), axis=0, keepdims=True)


def as_column(mask, row):
    return jnp.sum(jnp.where(mask, jnp.broadcast_to(row, (B, B)), 0.0), axis=1, keepdims=True)


def solve(first, across, second, offs):
    mask = eye_mask()
    angles = []
    turns = identity_halves()
    held = 0
    for r in range(ROUNDS):
        turn = (held - offs[r]) & (B - 1)
        held = offs[r]
        across = pltpu.roll(across, turn, 1)
        second = pltpu.roll(pltpu.roll(second, turn, 1), turn, 0)
        turns = [(top, pltpu.roll(low, turn, 1)) for top, low in turns]
        a = diagonal(mask, first)
        d = diagonal(mask, second)
        c0 = diagonal(mask, across)
        h = 0.5 * (d - a)
        radius = jnp.sqrt(h * h + c0 * c0)
        sg = jnp.where(h >= 0, 1.0, -1.0)
        t = -sg * c0 / (jnp.abs(h) + radius + 1e-06 * (a + d))
        c = 1.0 / jnp.sqrt(1.0 + t * t)
        s = t * c
        angles.append((c, s))
        cc, sc = as_column(mask, c), as_column(mask, s)
        below = across.T
        first1 = first * c + across * s
        across1 = across * c - first * s
        below1 = below * c + second * s
        second1 = second * c - below * s
        first = cc * first1 + sc * below1
        across = cc * across1 + sc * second1
        second = cc * second1 - sc * across1
        turns = [(c * top + s * low, c * low - s * top) for top, low in turns]
    second = pltpu.roll(pltpu.roll(second, held, 1), held, 0)
    turns = [(top, pltpu.roll(low, held, 1)) for top, low in turns]
    rotation = jnp.concatenate([jnp.concatenate(t, axis=1) for t in turns], axis=0)
    return angles, rotation, first, second


def rotate(first, second, angles, offs):
    held = 0
    for r in range(ROUNDS):
        c, s = angles[r]
        second = pltpu.roll(second, (held - offs[r]) & (B - 1), 1)
        held = offs[r]
        first, second = c * first + s * second, c * second - s * first
    return first, pltpu.roll(second, held, 1)


def rotate_back(first, second, angles, offs):
    held = 0
    for r in reversed(range(ROUNDS)):
        c, s = angles[r]
        second = pltpu.roll(second, (held - offs[r]) & (B - 1), 1)
        held = offs[r]
        first, second = c * first - s * second, s * first + c * second
    return first, pltpu.roll(second, held, 1)


def read_record(rows):
    return [(rows[r : r + 1], rows[ROUNDS + r : ROUNDS + r + 1]) for r in range(ROUNDS)]


def write_record(ref, at, angles):
    for r, (c, s) in enumerate(angles):
        ref[at + r : at + r + 1, :] = c
        ref[at + ROUNDS + r : at + ROUNDS + r + 1, :] = s


def index(shape, axis):
    return lax.broadcasted_iota(jnp.int32, shape, axis)


def pack(block):
    shape = (HALF, B)
    low = jnp.logical_and(index(shape, 1) < HALF, index(shape, 0) > index(shape, 1))
    rows = jnp.where(low, pltpu.roll(block[HALF:], HALF, 1), block[:HALF])
    return jnp.concatenate([rows, jnp.broadcast_to(diagonal(eye_mask(), block), (8, B))], axis=0)


def unpack(packed):
    rows, diag = packed[:HALF], packed[HALF : HALF + 1]
    turned = jnp.concatenate([rows, rows], axis=0).T
    shape = (HALF, B)
    i, j = index(shape, 0), index(shape, 1)
    left = j < HALF
    top = jnp.where(jnp.logical_and(left, i > j), turned[:HALF], rows)
    right = jnp.where(i > j - HALF, pltpu.roll(rows, HALF, 1), turned[:HALF])
    right = jnp.where(i == j - HALF, jnp.broadcast_to(diag, shape), right)
    return jnp.concatenate([top, jnp.where(left, turned[HALF:], right)], axis=0)


def pack_two(first, second):
    rows, cols = index((B, B), 0), index((B, B), 1)
    return [
        jnp.where(rows <= cols, first, second),
        jnp.broadcast_to(diagonal(eye_mask(), second), (8, B)),
    ]


def unpack_two(block, diag):
    rows, cols = index((B, B), 0), index((B, B), 1)
    turned = block.T
    second = jnp.where(rows > cols, block, turned)
    second = jnp.where(rows == cols, jnp.broadcast_to(diag, (B, B)), second)
    return jnp.where(rows <= cols, block, turned), second


def tree_sum(parts):
    parts = list(parts)
    while len(parts) > 1:
        parts = [parts[i] + parts[i + 1] for i in range(0, len(parts), 2)]
    return parts[0]


def split(x):
    high = x.astype(jnp.bfloat16)
    return high, (x - high.astype(jnp.float32)).astype(jnp.bfloat16)


def product(x, rotation):
    xh, xl = split(x)
    rh, rl = split(rotation)

    def dot(a, b):
        return jnp.dot(a, b, preferred_element_type=jnp.float32)

    return (dot(xl, rh) + dot(xh, rl)) + dot(xh, rh)


def step_offsets(offs_ref, step):
    return [offs_ref[step, r] for r in range(ROUNDS)]


def transposed_dot(left, right):
    return lax.dot_general(
        left,
        right,
        (((0,), (0,)), ((), ())),
        precision=lax.Precision.HIGHEST,
        preferred_element_type=jnp.float32,
    )


JOINED, RAW, EITHER = range(3)


def call(kernel, out_shapes, arrays):
    return pl.pallas_call(
        kernel,
        out_shape=tuple(jax.ShapeDtypeStruct(shape, jnp.float32) for shape in out_shapes),
        in_specs=[VMEM] * len(arrays),
        out_specs=tuple(VMEM for _ in out_shapes),
        compiler_params=PARAMS,
    )(*arrays)


class Place:
    def __init__(self, layout):
        pair, row = lax.axis_index("pair"), lax.axis_index("row")
        self.pairs = lax.axis_size("pair")
        self.slot, self.part = layout(pair, row)
        self.odd = (self.slot & 1) == 1
        self.edge = jnp.logical_or(self.slot == 0, self.slot == self.pairs - 1)
        self.stays = jnp.logical_and(self.edge, ((pair ^ row) & 1) == 0)


def whole_gram_kernel(x_ref, out_ref):
    gram = transposed_dot(x_ref[...], x_ref[...])
    packed, diag = pack_two(gram[:B, :B], gram[B:, B:])
    out_ref[:B, :] = gram[:B, B:]
    out_ref[B : 2 * B, :] = packed
    out_ref[2 * B :, :] = diag


def whole_gram(x):
    return call(whole_gram_kernel, [(2 * B + 8, B)], (x,))[0]


def base_of(way, rows):
    return rows if way == JOINED else 0


def older(odd, mu, mw):
    hu, hw = mu[PACKED:], mw[PACKED:]
    return jnp.where(odd, hu, hw), jnp.where(odd, hw, hu)


def cross_solve(across, odd, mu, mw, offs):
    gu, gw = unpack(mu[:PACKED]), unpack(mw[:PACKED])
    return solve(jnp.where(odd, gu, gw), across, jnp.where(odd, gw, gu), offs)


def turn_kernel(step, goes, layout, count, offs_ref, *refs):
    parts, refs = refs[:count], list(refs[count:])
    place = Place(layout)
    odd = place.odd
    offs = step_offsets(offs_ref, step)
    if step == 0:
        gram = tree_sum([p[...] for p in parts])
        first, second = unpack_two(gram[B : 2 * B], gram[2 * B : 2 * B + 1])
        angles, rotation, first, second = solve(first, gram[:B], second, offs)
        past = ()
    else:
        mu, mw = refs.pop(0)[...], refs.pop(0)[...]
        across = tree_sum([p[...] for p in parts])
        angles, rotation, first, second = cross_solve(across, odd, mu, mw, offs)
        past = older(odd, mu, mw)
    x_ref = refs.pop(0)
    rows = x_ref.shape[0]
    swap = jnp.logical_and(jnp.logical_not(odd), place.slot != 0)
    blocks = []
    for way, near in zip(goes, (True, False)):
        message = refs.pop(0)
        base = base_of(way, rows)
        gives_first = swap if near else jnp.logical_not(swap)
        message[base : base + PACKED, :] = pack(jnp.where(gives_first, first, second))
        at = base + PACKED
        write_record(message, at, angles)
        at += RECORD
        for history in past:
            message[at : at + history.shape[0], :] = history
            at += history.shape[0]
        if way != RAW:
            blocks.append((message if way == JOINED else refs.pop(0), gives_first))
    if len(blocks) == 1:
        (block_ref, gives_first), = blocks
        half = jnp.where(gives_first, rotation[:, :B], rotation[:, B:])
        block_ref[:rows, :] = product(x_ref[...], half)
        return
    x = product(x_ref[...], rotation)
    for block_ref, gives_first in blocks:

        @pl.when(gives_first)
        def _():
            block_ref[:rows, :] = x[:, :B]

        @pl.when(jnp.logical_not(gives_first))
        def _():
            block_ref[:rows, :] = x[:, B:]


def turn(step, goes, layout, offsets, parts, messages, x):
    rows = x.shape[0]
    small = PACKED + RECORD
    if step:
        small += 2 * (messages[0].shape[0] - PACKED)
    shapes = []
    for way in goes:
        shapes.append((base_of(way, rows) + small, B))
        if way == EITHER:
            shapes.append((rows, B))
    kernel = functools.partial(turn_kernel, step, goes, layout, len(parts))
    return call(kernel, shapes, (offsets, *parts, *messages, x))


def half_rotation(angles, offs, take_first):
    halves = [rotate(top, low, angles, offs) for top, low in identity_halves()]
    return jnp.concatenate([jnp.where(take_first, top, low) for top, low in halves], axis=0)


def arrive_kernel(step, came, source, offs_ref, u_ref, w_ref, own_ref, *refs):
    *refs, x_ref, gram_ref, mu_ref, mw_ref = refs
    rows = x_ref.shape[0]
    place = Place(crossed)
    odd = place.odd
    own = place.edge if source is crossed else place.stays
    u_base, w_base = (base_of(way, rows) for way in came)
    mu_ref[...] = u_ref[u_base:, :]
    mw_ref[...] = jnp.where(own, own_ref[w_base:, :], w_ref[w_base:, :])

    def put(first, block):
        @pl.when(first)
        def _():
            x_ref[:, :B] = block

        @pl.when(jnp.logical_not(first))
        def _():
            x_ref[:, B:] = block

    put(odd, u_ref[:rows, :])
    if came[1] == RAW:
        takes_first = jnp.logical_or(jnp.logical_not(odd), place.slot == place.pairs - 1)
        offs = step_offsets(offs_ref, step)
        angles = read_record(mw_ref[PACKED : PACKED + RECORD, :])
        put(jnp.logical_not(odd), product(refs[0][...], half_rotation(angles, offs, takes_first)))
    else:

        @pl.when(own)
        def _():
            put(jnp.logical_not(odd), own_ref[:rows, :])

        @pl.when(jnp.logical_not(own))
        def _():
            put(jnp.logical_not(odd), w_ref[:rows, :])

    gram_ref[...] = transposed_dot(x_ref[:, :B], x_ref[:, B:])


def arrive(step, rows, came, source, offsets, messages, raw=()):
    kernel = functools.partial(arrive_kernel, step, came, source)
    small = messages[0].shape[0] - base_of(came[0], rows)
    shapes = [(rows, 2 * B), (B, B), (small, B), (small, B)]
    return call(kernel, shapes, (offsets, *messages, *raw))


def last_gram_kernel(rows, u_ref, w_ref, own_ref, out_ref):
    own = Place(given).stays

    @pl.when(own)
    def _():
        out_ref[...] = transposed_dot(u_ref[:rows, :], own_ref[:rows, :])

    @pl.when(jnp.logical_not(own))
    def _():
        out_ref[...] = transposed_dot(u_ref[:rows, :], w_ref[:rows, :])


def last_gram(rows, messages):
    return call(functools.partial(last_gram_kernel, rows), [(B, B)], messages)[0]


def settle_kernel(u_ref, w_ref, own_ref, x_ref, mu_ref, mw_ref):
    rows = x_ref.shape[0]
    place = Place(given)
    odd, own = place.odd, place.stays
    u, w = u_ref[...], jnp.where(own, own_ref[...], w_ref[...])
    x_ref[:, :B] = jnp.where(odd, u[:rows], w[:rows])
    x_ref[:, B:] = jnp.where(odd, w[:rows], u[:rows])
    mu_ref[...] = u[rows:]
    mw_ref[...] = w[rows:]


def settle(rows, messages):
    small = messages[0].shape[0] - rows
    shapes = [(rows, 2 * B), (small, B), (small, B)]
    return call(settle_kernel, shapes, messages)


def came_from(slot, is_first, pairs):
    if is_first:
        return jnp.where(slot == 0, 0, slot - 1), slot != 1
    last = slot == pairs - 1
    return jnp.where(last, slot, slot + 1), last


def vectors_kernel(offs_ref, mu_ref, mw_ref, out_ref):
    place = Place(given)
    slot, pairs, part, odd = place.slot, place.pairs, place.part, place.odd
    held_slots = out_ref.shape[0] // (2 * B)
    unit = jnp.where(eye_mask(), 1.0, 0.0)
    zero = jnp.zeros_like(unit)
    pasts = older(odd, mu_ref[...], mw_ref[...])
    nodes = [
        (unit, *came_from(slot, is_first, pairs), past, at)
        for is_first, past, at in ((True, pasts[0], 0), (False, pasts[1], B))
    ]
    for step in reversed(range(STEPS - 1)):
        offs = step_offsets(offs_ref, step)
        below = []
        for block, node, was_first, past, at in nodes:
            top, low = rotate_back(
                jnp.where(was_first, block, zero),
                jnp.where(was_first, zero, block),
                read_record(past[:RECORD]),
                offs,
            )
            if step == 0:
                below.append((top, low, node, at))
                continue
            half = (past.shape[0] - RECORD) // 2
            top_past, low_past = past[RECORD : RECORD + half], past[RECORD + half :]
            below.append((top, *came_from(node, True, pairs), top_past, at))
            below.append((low, *came_from(node, False, pairs), low_past, at))
        nodes = below
    out_ref[...] = jnp.zeros_like(out_ref)
    for top, low, node, column in nodes:

        @pl.when(node // held_slots == part)
        def _():
            at = pl.multiple_of((node - part * held_slots) * (2 * B), 2 * B)
            out_ref[pl.ds(at, B), column : column + B] += top.T
            out_ref[pl.ds(at + B, B), column : column + B] += low.T


def vectors_before_last(height, offsets, messages):
    return call(vectors_kernel, [(height, 2 * B)], (offsets, *messages))[0]


def last_kernel(count, offs_ref, *refs):
    parts, (mu_ref, mw_ref, x_ref, v_ref, x_out, v_out) = refs[:count], refs[count:]
    odd = Place(given).odd
    gram = tree_sum([p[...] for p in parts])
    across = jnp.where(odd, gram, gram.T)
    offs = step_offsets(offs_ref, STEPS - 1)
    _, rotation, _, _ = cross_solve(across, odd, mu_ref[...], mw_ref[...], offs)
    x_out[...] = product(x_ref[...], rotation)
    v_out[...] = product(v_ref[...], rotation)


def last_step(offsets, parts, messages, x, v):
    kernel = functools.partial(last_kernel, len(parts))
    return call(kernel, [x.shape, v.shape], (offsets, *parts, *messages, x, v))


def in_stages(partial, layout):
    distance, count = 1, lax.axis_size("row")
    while 2 * distance < count:
        partial = partial + send(partial, layout, layout, other_part(distance))
        distance *= 2
    if distance < count:
        return [partial, send(partial, layout, layout, other_part(distance))]
    return [partial]


def at_once(partial, layout):
    others = range(1, lax.axis_size("row"))
    return [partial] + [send(partial, layout, layout, other_part(d)) for d in others]


def body(whitened, offsets):
    rows, width = whitened.shape
    height = lax.axis_size("pair") * width // lax.axis_size("row")

    terms = in_stages(whole_gram(whitened), given)
    ways = (JOINED, JOINED)
    near, far = turn(0, ways, given, offsets, terms, (), whitened)
    w = send(far, given, crossed, outer)
    u = send(near, given, crossed, inner)
    x, cross, mu, mw = arrive(0, rows, ways, given, offsets, (u, w, far))

    raw = send(x, crossed, crossed, outer, swap=False)
    terms = at_once(cross, crossed)
    ways = (JOINED, RAW)
    near, far = turn(1, ways, crossed, offsets, terms, (mu, mw), x)
    w = send(far, crossed, crossed, outer)
    u = send(near, crossed, crossed, inner)
    x, cross, mu, mw = arrive(1, rows, ways, crossed, offsets, (u, w, far), (raw,))

    terms = at_once(cross, crossed)
    near, far = turn(2, (JOINED, JOINED), crossed, offsets, terms, (mu, mw), x)
    w = send(far, crossed, given, outer)
    u = send(near, crossed, given, inner)
    terms = in_stages(last_gram(rows, (u, w, far)), given)
    x, mu, mw = settle(rows, (u, w, far))
    vectors = vectors_before_last(height, offsets, (mu, mw))
    return last_step(offsets, terms, (mu, mw), x, vectors)


def solution(mesh):
    in_specs = (P("row", "pair"), P())
    out_specs = (P("row", "pair"), P("row", "pair"))
    return jax.shard_map(body, mesh=mesh, in_specs=in_specs, out_specs=out_specs, check_vma=False)
```

```python
import functools

import jax
import jax.numpy as jnp
from jax import lax
from jax.experimental import pallas as pl
from jax.experimental.pallas import tpu as pltpu
from jax.sharding import PartitionSpec as P

B = 128
ROUNDS = 4
STEPS = 4
RECORD = 2 * ROUNDS
HALF = B // 2
PACKED = HALF + 8
AXES = ("pair", "row")
PARAMS = pltpu.CompilerParams(vmem_limit_bytes=40 * 1024 * 1024)
VMEM = pl.BlockSpec(memory_space=pltpu.VMEM)


def given(slot, part):
    return slot, part


def crossed(slot, part):
    return (slot & ~1) | (part & 1), (part & ~1) | (slot & 1)


def route(source, target, change, swap=True):
    pairs, rows = lax.axis_size("pair"), lax.axis_size("row")
    line = []
    for slot in range(pairs):
        for part in range(rows):
            a = source(slot, part)
            b = target(*change(slot, part, pairs))
            if swap and a == b:
                b = a[0], a[1] ^ (rows // 2)
            line.append((a[0] * rows + a[1], b[0] * rows + b[1]))
    return line


def inner(slot, part, pairs):
    return slot ^ 1, part


def outer(slot, part, pairs):
    if slot == 0 or slot == pairs - 1:
        return slot, part
    return (slot + 1 if slot & 1 else slot - 1), part


def send(x, source, target, change, swap=True):
    return lax.ppermute(x, AXES, route(source, target, change, swap))


def other_part(distance):
    return lambda slot, part, pairs: (slot, part ^ distance)


def eye_mask():
    shape = (B, B)
    return lax.broadcasted_iota(jnp.int32, shape, 0) == lax.broadcasted_iota(jnp.int32, shape, 1)


def identity_halves():
    unit = jnp.where(eye_mask(), 1.0, 0.0)
    return [(unit, jnp.zeros_like(unit)), (jnp.zeros_like(unit), unit)]


def diagonal(mask, block):
    return jnp.sum(jnp.where(mask, block, 0.0), axis=0, keepdims=True)


def as_column(mask, row):
    return jnp.sum(jnp.where(mask, jnp.broadcast_to(row, (B, B)), 0.0), axis=1, keepdims=True)


def solve(first, across, second, offs):
    mask = eye_mask()
    angles = []
    turns = identity_halves()
    held = 0
    for r in range(ROUNDS):
        turn = (held - offs[r]) & (B - 1)
        held = offs[r]
        across = pltpu.roll(across, turn, 1)
        second = pltpu.roll(pltpu.roll(second, turn, 1), turn, 0)
        turns = [(top, pltpu.roll(low, turn, 1)) for top, low in turns]
        a = diagonal(mask, first)
        d = diagonal(mask, second)
        c0 = diagonal(mask, across)
        h = 0.5 * (d - a)
        radius = jnp.sqrt(h * h + c0 * c0)
        sg = jnp.where(h >= 0, 1.0, -1.0)
        t = -sg * c0 / (jnp.abs(h) + radius + 1e-06 * (a + d))
        c = 1.0 / jnp.sqrt(1.0 + t * t)
        s = t * c
        angles.append((c, s))
        cc, sc = as_column(mask, c), as_column(mask, s)
        below = across.T
        first1 = first * c + across * s
        across1 = across * c - first * s
        below1 = below * c + second * s
        second1 = second * c - below * s
        first = cc * first1 + sc * below1
        across = cc * across1 + sc * second1
        second = cc * second1 - sc * across1
        turns = [(c * top + s * low, c * low - s * top) for top, low in turns]
    second = pltpu.roll(pltpu.roll(second, held, 1), held, 0)
    turns = [(top, pltpu.roll(low, held, 1)) for top, low in turns]
    rotation = jnp.concatenate([jnp.concatenate(t, axis=1) for t in turns], axis=0)
    return angles, rotation, first, second


def rotate(first, second, angles, offs):
    held = 0
    for r in range(ROUNDS):
        c, s = angles[r]
        second = pltpu.roll(second, (held - offs[r]) & (B - 1), 1)
        held = offs[r]
        first, second = c * first + s * second, c * second - s * first
    return first, pltpu.roll(second, held, 1)


def rotate_back(first, second, angles, offs):
    held = 0
    for r in reversed(range(ROUNDS)):
        c, s = angles[r]
        second = pltpu.roll(second, (held - offs[r]) & (B - 1), 1)
        held = offs[r]
        first, second = c * first - s * second, s * first + c * second
    return first, pltpu.roll(second, held, 1)


def read_record(rows):
    return [(rows[r : r + 1], rows[ROUNDS + r : ROUNDS + r + 1]) for r in range(ROUNDS)]


def write_record(ref, at, angles):
    for r, (c, s) in enumerate(angles):
        ref[at + r : at + r + 1, :] = c
        ref[at + ROUNDS + r : at + ROUNDS + r + 1, :] = s


def index(shape, axis):
    return lax.broadcasted_iota(jnp.int32, shape, axis)


def pack(block):
    shape = (HALF, B)
    low = jnp.logical_and(index(shape, 1) < HALF, index(shape, 0) > index(shape, 1))
    rows = jnp.where(low, pltpu.roll(block[HALF:], HALF, 1), block[:HALF])
    return jnp.concatenate([rows, jnp.broadcast_to(diagonal(eye_mask(), block), (8, B))], axis=0)


def unpack(packed):
    rows, diag = packed[:HALF], packed[HALF : HALF + 1]
    turned = jnp.concatenate([rows, rows], axis=0).T
    shape = (HALF, B)
    i, j = index(shape, 0), index(shape, 1)
    left = j < HALF
    top = jnp.where(jnp.logical_and(left, i > j), turned[:HALF], rows)
    right = jnp.where(i > j - HALF, pltpu.roll(rows, HALF, 1), turned[:HALF])
    right = jnp.where(i == j - HALF, jnp.broadcast_to(diag, shape), right)
    return jnp.concatenate([top, jnp.where(left, turned[HALF:], right)], axis=0)


def pack_two(first, second):
    rows, cols = index((B, B), 0), index((B, B), 1)
    return [
        jnp.where(rows <= cols, first, second),
        jnp.broadcast_to(diagonal(eye_mask(), second), (8, B)),
    ]


def unpack_two(block, diag):
    rows, cols = index((B, B), 0), index((B, B), 1)
    turned = block.T
    second = jnp.where(rows > cols, block, turned)
    second = jnp.where(rows == cols, jnp.broadcast_to(diag, (B, B)), second)
    return jnp.where(rows <= cols, block, turned), second


def tree_sum(parts):
    parts = list(parts)
    while len(parts) > 1:
        parts = [parts[i] + parts[i + 1] for i in range(0, len(parts), 2)]
    return parts[0]


def split(x):
    high = x.astype(jnp.bfloat16)
    return high, (x - high.astype(jnp.float32)).astype(jnp.bfloat16)


def product(x, rotation):
    xh, xl = split(x)
    rh, rl = split(rotation)

    def dot(a, b):
        return jnp.dot(a, b, preferred_element_type=jnp.float32)

    return (dot(xl, rh) + dot(xh, rl)) + dot(xh, rh)


def step_offsets(offs_ref, step):
    return [offs_ref[step, r] for r in range(ROUNDS)]


def transposed_dot(left, right):
    return lax.dot_general(
        left,
        right,
        (((0,), (0,)), ((), ())),
        precision=lax.Precision.HIGHEST,
        preferred_element_type=jnp.float32,
    )


JOINED, RAW, EITHER = range(3)


def call(kernel, out_shapes, arrays):
    return pl.pallas_call(
        kernel,
        out_shape=tuple(jax.ShapeDtypeStruct(shape, jnp.float32) for shape in out_shapes),
        in_specs=[VMEM] * len(arrays),
        out_specs=tuple(VMEM for _ in out_shapes),
        compiler_params=PARAMS,
    )(*arrays)


class Place:
    def __init__(self, layout):
        pair, row = lax.axis_index("pair"), lax.axis_index("row")
        self.pairs = lax.axis_size("pair")
        self.slot, self.part = layout(pair, row)
        self.odd = (self.slot & 1) == 1
        self.edge = jnp.logical_or(self.slot == 0, self.slot == self.pairs - 1)
        self.same = ((pair ^ row) & 1) == 0
        self.stays = jnp.logical_and(self.edge, self.same)


def whole_gram_kernel(x_ref, out_ref):
    gram = transposed_dot(x_ref[...], x_ref[...])
    packed, diag = pack_two(gram[:B, :B], gram[B:, B:])
    out_ref[:B, :] = gram[:B, B:]
    out_ref[B : 2 * B, :] = packed
    out_ref[2 * B :, :] = diag


def whole_gram(x):
    return call(whole_gram_kernel, [(2 * B + 8, B)], (x,))[0]


def base_of(way, rows):
    return rows if way == JOINED else 0


def older(odd, mu, mw):
    hu, hw = mu[PACKED:], mw[PACKED:]
    return jnp.where(odd, hu, hw), jnp.where(odd, hw, hu)


def cross_solve(across, odd, mu, mw, offs):
    gu, gw = unpack(mu[:PACKED]), unpack(mw[:PACKED])
    return solve(jnp.where(odd, gu, gw), across, jnp.where(odd, gw, gu), offs)


def turn_kernel(step, goes, layout, count, offs_ref, *refs):
    parts, refs = refs[:count], list(refs[count:])
    place = Place(layout)
    odd = place.odd
    offs = step_offsets(offs_ref, step)
    if step == 0:
        gram = tree_sum([p[...] for p in parts])
        first, second = unpack_two(gram[B : 2 * B], gram[2 * B : 2 * B + 1])
        angles, rotation, first, second = solve(first, gram[:B], second, offs)
        past = ()
    else:
        mu, mw = refs.pop(0)[...], refs.pop(0)[...]
        across = tree_sum([p[...] for p in parts])
        angles, rotation, first, second = cross_solve(across, odd, mu, mw, offs)
        past = older(odd, mu, mw)
    x_ref = refs.pop(0)
    rows = x_ref.shape[0]
    swap = jnp.logical_and(jnp.logical_not(odd), place.slot != 0)
    blocks = []
    for way, near in zip(goes, (True, False)):
        message = refs.pop(0)
        base = base_of(way, rows)
        gives_first = swap if near else jnp.logical_not(swap)
        message[base : base + PACKED, :] = pack(jnp.where(gives_first, first, second))
        at = base + PACKED
        write_record(message, at, angles)
        at += RECORD
        for history in past:
            message[at : at + history.shape[0], :] = history
            at += history.shape[0]
        if way != RAW:
            blocks.append((message if way == JOINED else refs.pop(0), gives_first))
    if len(blocks) == 1:
        (block_ref, gives_first), = blocks
        half = jnp.where(gives_first, rotation[:, :B], rotation[:, B:])
        block_ref[:rows, :] = product(x_ref[...], half)
        return
    x = product(x_ref[...], rotation)
    for block_ref, gives_first in blocks:

        @pl.when(gives_first)
        def _():
            block_ref[:rows, :] = x[:, :B]

        @pl.when(jnp.logical_not(gives_first))
        def _():
            block_ref[:rows, :] = x[:, B:]


def turn(step, goes, layout, offsets, parts, messages, x):
    rows = x.shape[0]
    small = PACKED + RECORD
    if step:
        small += 2 * (messages[0].shape[0] - PACKED)
    shapes = []
    for way in goes:
        shapes.append((base_of(way, rows) + small, B))
        if way == EITHER:
            shapes.append((rows, B))
    kernel = functools.partial(turn_kernel, step, goes, layout, len(parts))
    return call(kernel, shapes, (offsets, *parts, *messages, x))


def half_rotation(angles, offs, take_first):
    halves = [rotate(top, low, angles, offs) for top, low in identity_halves()]
    return jnp.concatenate([jnp.where(take_first, top, low) for top, low in halves], axis=0)


def arrive_kernel(step, came, source, offs_ref, u_ref, w_ref, own_ref, *refs):
    *refs, x_ref, gram_ref, mu_ref, mw_ref = refs
    rows = x_ref.shape[0]
    place = Place(crossed)
    odd = place.odd
    own = place.edge if source is crossed else place.stays
    u_base, w_base = (base_of(way, rows) for way in came)
    mu_ref[...] = u_ref[u_base:, :]
    mw_ref[...] = jnp.where(own, own_ref[w_base:, :], w_ref[w_base:, :])

    def put(first, block):
        @pl.when(first)
        def _():
            x_ref[:, :B] = block

        @pl.when(jnp.logical_not(first))
        def _():
            x_ref[:, B:] = block

    if came[0] == JOINED:
        put(odd, u_ref[:rows, :])
    else:
        put(odd, refs[0][...])
    if came[1] == RAW:
        takes_first = jnp.logical_or(jnp.logical_not(odd), place.slot == place.pairs - 1)
        offs = step_offsets(offs_ref, step)
        angles = read_record(mw_ref[PACKED : PACKED + RECORD, :])
        put(jnp.logical_not(odd), product(refs[0][...], half_rotation(angles, offs, takes_first)))
    else:

        @pl.when(own)
        def _():
            put(jnp.logical_not(odd), own_ref[:rows, :])

        @pl.when(jnp.logical_not(own))
        def _():
            put(jnp.logical_not(odd), w_ref[:rows, :])

    gram_ref[...] = transposed_dot(x_ref[:, :B], x_ref[:, B:])


def ready_kernel(step, offs_ref, u_ref, block_ref, raw_ref, out_ref):
    place = Place(crossed)

    @pl.when(place.same)
    def _():
        takes_first = jnp.logical_and(place.odd, place.slot != 1)
        angles = read_record(u_ref[PACKED : PACKED + RECORD, :])
        half = half_rotation(angles, step_offsets(offs_ref, step), takes_first)
        out_ref[...] = product(raw_ref[...], half)

    @pl.when(jnp.logical_not(place.same))
    def _():
        out_ref[...] = block_ref[...]


def ready(step, offsets, u, block, raw):
    kernel = functools.partial(ready_kernel, step)
    return call(kernel, [block.shape], (offsets, u, block, raw))[0]


def arrive(step, rows, came, source, offsets, messages, raw=()):
    kernel = functools.partial(arrive_kernel, step, came, source)
    small = messages[0].shape[0] - base_of(came[0], rows)
    shapes = [(rows, 2 * B), (B, B), (small, B), (small, B)]
    return call(kernel, shapes, (offsets, *messages, *raw))


def last_gram_kernel(rows, u_ref, w_ref, own_ref, out_ref):
    own = Place(given).stays

    @pl.when(own)
    def _():
        out_ref[...] = transposed_dot(u_ref[:rows, :], own_ref[:rows, :])

    @pl.when(jnp.logical_not(own))
    def _():
        out_ref[...] = transposed_dot(u_ref[:rows, :], w_ref[:rows, :])


def last_gram(rows, messages):
    return call(functools.partial(last_gram_kernel, rows), [(B, B)], messages)[0]


def settle_kernel(u_ref, w_ref, own_ref, x_ref, mu_ref, mw_ref):
    rows = x_ref.shape[0]
    place = Place(given)
    odd, own = place.odd, place.stays
    u, w = u_ref[...], jnp.where(own, own_ref[...], w_ref[...])
    x_ref[:, :B] = jnp.where(odd, u[:rows], w[:rows])
    x_ref[:, B:] = jnp.where(odd, w[:rows], u[:rows])
    mu_ref[...] = u[rows:]
    mw_ref[...] = w[rows:]


def settle(rows, messages):
    small = messages[0].shape[0] - rows
    shapes = [(rows, 2 * B), (small, B), (small, B)]
    return call(settle_kernel, shapes, messages)


def came_from(slot, is_first, pairs):
    if is_first:
        return jnp.where(slot == 0, 0, slot - 1), slot != 1
    last = slot == pairs - 1
    return jnp.where(last, slot, slot + 1), last


def vectors_kernel(offs_ref, mu_ref, mw_ref, out_ref):
    place = Place(given)
    slot, pairs, part, odd = place.slot, place.pairs, place.part, place.odd
    held_slots = out_ref.shape[0] // (2 * B)
    unit = jnp.where(eye_mask(), 1.0, 0.0)
    zero = jnp.zeros_like(unit)
    pasts = older(odd, mu_ref[...], mw_ref[...])
    nodes = [
        (unit, *came_from(slot, is_first, pairs), past, at)
        for is_first, past, at in ((True, pasts[0], 0), (False, pasts[1], B))
    ]
    for step in reversed(range(STEPS - 1)):
        offs = step_offsets(offs_ref, step)
        below = []
        for block, node, was_first, past, at in nodes:
            top, low = rotate_back(
                jnp.where(was_first, block, zero),
                jnp.where(was_first, zero, block),
                read_record(past[:RECORD]),
                offs,
            )
            if step == 0:
                below.append((top, low, node, at))
                continue
            half = (past.shape[0] - RECORD) // 2
            top_past, low_past = past[RECORD : RECORD + half], past[RECORD + half :]
            below.append((top, *came_from(node, True, pairs), top_past, at))
            below.append((low, *came_from(node, False, pairs), low_past, at))
        nodes = below
    out_ref[...] = jnp.zeros_like(out_ref)
    for top, low, node, column in nodes:

        @pl.when(node // held_slots == part)
        def _():
            at = pl.multiple_of((node - part * held_slots) * (2 * B), 2 * B)
            out_ref[pl.ds(at, B), column : column + B] += top.T
            out_ref[pl.ds(at + B, B), column : column + B] += low.T


def vectors_before_last(height, offsets, messages):
    return call(vectors_kernel, [(height, 2 * B)], (offsets, *messages))[0]


def last_kernel(count, offs_ref, *refs):
    parts, (mu_ref, mw_ref, x_ref, v_ref, x_out, v_out) = refs[:count], refs[count:]
    odd = Place(given).odd
    gram = tree_sum([p[...] for p in parts])
    across = jnp.where(odd, gram, gram.T)
    offs = step_offsets(offs_ref, STEPS - 1)
    _, rotation, _, _ = cross_solve(across, odd, mu_ref[...], mw_ref[...], offs)
    x_out[...] = product(x_ref[...], rotation)
    v_out[...] = product(v_ref[...], rotation)


def last_step(offsets, parts, messages, x, v):
    kernel = functools.partial(last_kernel, len(parts))
    return call(kernel, [x.shape, v.shape], (offsets, *parts, *messages, x, v))


def in_stages(partial, layout):
    distance, count = 1, lax.axis_size("row")
    while 2 * distance < count:
        partial = partial + send(partial, layout, layout, other_part(distance))
        distance *= 2
    if distance < count:
        return [partial, send(partial, layout, layout, other_part(distance))]
    return [partial]


def at_once(partial, layout):
    others = range(1, lax.axis_size("row"))
    return [partial] + [send(partial, layout, layout, other_part(d)) for d in others]


def body(whitened, offsets):
    rows, width = whitened.shape
    height = lax.axis_size("pair") * width // lax.axis_size("row")

    raw = send(whitened, given, crossed, inner)
    terms = in_stages(whole_gram(whitened), given)
    ways = (EITHER, JOINED)
    near, block, far = turn(0, ways, given, offsets, terms, (), whitened)
    w = send(far, given, crossed, outer)
    u = send(near, given, crossed, inner)
    block = send(block, given, given, other_part(1))
    block = ready(0, offsets, u, block, raw)
    x, cross, mu, mw = arrive(0, rows, ways, given, offsets, (u, w, far), (block,))

    raw = send(x, crossed, crossed, outer, swap=False)
    terms = at_once(cross, crossed)
    ways = (JOINED, RAW)
    near, far = turn(1, ways, crossed, offsets, terms, (mu, mw), x)
    w = send(far, crossed, crossed, outer)
    u = send(near, crossed, crossed, inner)
    x, cross, mu, mw = arrive(1, rows, ways, crossed, offsets, (u, w, far), (raw,))

    terms = at_once(cross, crossed)
    near, far = turn(2, (JOINED, JOINED), crossed, offsets, terms, (mu, mw), x)
    w = send(far, crossed, given, outer)
    u = send(near, crossed, given, inner)
    terms = in_stages(last_gram(rows, (u, w, far)), given)
    x, mu, mw = settle(rows, (u, w, far))
    vectors = vectors_before_last(height, offsets, (mu, mw))
    return last_step(offsets, terms, (mu, mw), x, vectors)


def solution(mesh):
    in_specs = (P("row", "pair"), P())
    out_specs = (P("row", "pair"), P("row", "pair"))
    return jax.shard_map(body, mesh=mesh, in_specs=in_specs, out_specs=out_specs, check_vma=False)
```

```python
import functools

import jax
import jax.numpy as jnp
from jax import lax
from jax.experimental import pallas as pl
from jax.experimental.pallas import tpu as pltpu
from jax.sharding import PartitionSpec as P

B = 128
ROUNDS = 4
STEPS = 4
RECORD = 2 * ROUNDS
HALF = B // 2
PACKED = HALF + 8
AXES = ("pair", "row")
PARAMS = pltpu.CompilerParams(vmem_limit_bytes=40 * 1024 * 1024)
VMEM = pl.BlockSpec(memory_space=pltpu.VMEM)


def given(slot, part):
    return slot, part


def crossed(slot, part):
    return (slot & ~1) | (part & 1), (part & ~1) | (slot & 1)


def route(source, target, change, swap=True):
    pairs, rows = lax.axis_size("pair"), lax.axis_size("row")
    line = []
    for slot in range(pairs):
        for part in range(rows):
            a = source(slot, part)
            b = target(*change(slot, part, pairs))
            if swap and a == b:
                b = a[0], a[1] ^ (rows // 2)
            line.append((a[0] * rows + a[1], b[0] * rows + b[1]))
    return line


def inner(slot, part, pairs):
    return slot ^ 1, part


def outer(slot, part, pairs):
    if slot == 0 or slot == pairs - 1:
        return slot, part
    return (slot + 1 if slot & 1 else slot - 1), part


def send(x, source, target, change, swap=True):
    return lax.ppermute(x, AXES, route(source, target, change, swap))


def other_part(distance):
    return lambda slot, part, pairs: (slot, part ^ distance)


def eye_mask():
    shape = (B, B)
    return lax.broadcasted_iota(jnp.int32, shape, 0) == lax.broadcasted_iota(jnp.int32, shape, 1)


def identity_halves():
    unit = jnp.where(eye_mask(), 1.0, 0.0)
    return [(unit, jnp.zeros_like(unit)), (jnp.zeros_like(unit), unit)]


def diagonal(mask, block):
    return jnp.sum(jnp.where(mask, block, 0.0), axis=0, keepdims=True)


def as_column(mask, row):
    return jnp.sum(jnp.where(mask, jnp.broadcast_to(row, (B, B)), 0.0), axis=1, keepdims=True)


def solve(first, across, second, offs):
    mask = eye_mask()
    distance = (index((B, B), 1) - index((B, B), 0)) & (B - 1)
    angles = []
    turns = identity_halves()
    a, d = diagonal(mask, first), diagonal(mask, second)
    held = 0
    for r in range(ROUNDS):
        turn, ahead = (held - offs[r]) & (B - 1), (offs[r] - held) & (B - 1)
        held = offs[r]
        c0 = pltpu.roll(diagonal(distance == ahead, across), turn, 1)
        d = pltpu.roll(d, turn, 1)
        across = pltpu.roll(across, turn, 1)
        second = pltpu.roll(pltpu.roll(second, turn, 1), turn, 0)
        turns = [(top, pltpu.roll(low, turn, 1)) for top, low in turns]
        h = 0.5 * (d - a)
        radius = jnp.sqrt(h * h + c0 * c0)
        sg = jnp.where(h >= 0, 1.0, -1.0)
        t = -sg * c0 / (jnp.abs(h) + radius + 1e-06 * (a + d))
        c = 1.0 / jnp.sqrt(1.0 + t * t)
        s = t * c
        angles.append((c, s))
        cc, sc = as_column(mask, c), as_column(mask, s)
        below = across.T
        first1 = first * c + across * s
        across1 = across * c - first * s
        below1 = below * c + second * s
        second1 = second * c - below * s
        first = cc * first1 + sc * below1
        across = cc * across1 + sc * second1
        second = cc * second1 - sc * across1
        a, d = c * (a * c + c0 * s) + s * (c0 * c + d * s), c * (d * c - c0 * s) - s * (c0 * c - a * s)
        turns = [(c * top + s * low, c * low - s * top) for top, low in turns]
    second = pltpu.roll(pltpu.roll(second, held, 1), held, 0)
    turns = [(top, pltpu.roll(low, held, 1)) for top, low in turns]
    rotation = jnp.concatenate([jnp.concatenate(t, axis=1) for t in turns], axis=0)
    return angles, rotation, first, second


def rotate(first, second, angles, offs):
    held = 0
    for r in range(ROUNDS):
        c, s = angles[r]
        second = pltpu.roll(second, (held - offs[r]) & (B - 1), 1)
        held = offs[r]
        first, second = c * first + s * second, c * second - s * first
    return first, pltpu.roll(second, held, 1)


def rotate_back(first, second, angles, offs):
    held = 0
    for r in reversed(range(ROUNDS)):
        c, s = angles[r]
        second = pltpu.roll(second, (held - offs[r]) & (B - 1), 1)
        held = offs[r]
        first, second = c * first - s * second, s * first + c * second
    return first, pltpu.roll(second, held, 1)


def read_record(rows):
    return [(rows[r : r + 1], rows[ROUNDS + r : ROUNDS + r + 1]) for r in range(ROUNDS)]


def write_record(ref, at, angles):
    for r, (c, s) in enumerate(angles):
        ref[at + r : at + r + 1, :] = c
        ref[at + ROUNDS + r : at + ROUNDS + r + 1, :] = s


def index(shape, axis):
    return lax.broadcasted_iota(jnp.int32, shape, axis)


def pack(block):
    shape = (HALF, B)
    low = jnp.logical_and(index(shape, 1) < HALF, index(shape, 0) > index(shape, 1))
    rows = jnp.where(low, pltpu.roll(block[HALF:], HALF, 1), block[:HALF])
    return jnp.concatenate([rows, jnp.broadcast_to(diagonal(eye_mask(), block), (8, B))], axis=0)


def unpack(packed):
    rows, diag = packed[:HALF], packed[HALF : HALF + 1]
    turned = jnp.concatenate([rows, rows], axis=0).T
    shape = (HALF, B)
    i, j = index(shape, 0), index(shape, 1)
    left = j < HALF
    top = jnp.where(jnp.logical_and(left, i > j), turned[:HALF], rows)
    right = jnp.where(i > j - HALF, pltpu.roll(rows, HALF, 1), turned[:HALF])
    right = jnp.where(i == j - HALF, jnp.broadcast_to(diag, shape), right)
    return jnp.concatenate([top, jnp.where(left, turned[HALF:], right)], axis=0)


def pack_two(first, second):
    rows, cols = index((B, B), 0), index((B, B), 1)
    return [
        jnp.where(rows <= cols, first, second),
        jnp.broadcast_to(diagonal(eye_mask(), second), (8, B)),
    ]


def unpack_two(block, diag):
    rows, cols = index((B, B), 0), index((B, B), 1)
    turned = block.T
    second = jnp.where(rows > cols, block, turned)
    second = jnp.where(rows == cols, jnp.broadcast_to(diag, (B, B)), second)
    return jnp.where(rows <= cols, block, turned), second


def tree_sum(parts):
    parts = list(parts)
    while len(parts) > 1:
        parts = [parts[i] + parts[i + 1] for i in range(0, len(parts), 2)]
    return parts[0]


def split(x):
    high = x.astype(jnp.bfloat16)
    return high, (x - high.astype(jnp.float32)).astype(jnp.bfloat16)


def product(x, rotation):
    xh, xl = split(x)
    rh, rl = split(rotation)

    def dot(a, b):
        return jnp.dot(a, b, preferred_element_type=jnp.float32)

    return (dot(xl, rh) + dot(xh, rl)) + dot(xh, rh)


def step_offsets(offs_ref, step):
    return [offs_ref[step, r] for r in range(ROUNDS)]


def transposed_dot(left, right):
    lh, ll = split(left)
    rh, rl = split(right)

    def dot(a, b):
        dims = (((0,), (0,)), ((), ()))
        return lax.dot_general(a, b, dims, preferred_element_type=jnp.float32)

    return (dot(ll, rh) + dot(lh, rl)) + dot(lh, rh)


JOINED, RAW, EITHER = range(3)


def call(kernel, out_shapes, arrays):
    return pl.pallas_call(
        kernel,
        out_shape=tuple(jax.ShapeDtypeStruct(shape, jnp.float32) for shape in out_shapes),
        in_specs=[VMEM] * len(arrays),
        out_specs=tuple(VMEM for _ in out_shapes),
        compiler_params=PARAMS,
    )(*arrays)


class Place:
    def __init__(self, layout):
        pair, row = lax.axis_index("pair"), lax.axis_index("row")
        self.pairs = lax.axis_size("pair")
        self.slot, self.part = layout(pair, row)
        self.odd = (self.slot & 1) == 1
        self.edge = jnp.logical_or(self.slot == 0, self.slot == self.pairs - 1)
        self.gives_first = (
            jnp.logical_and(jnp.logical_not(self.odd), self.slot != 0),
            jnp.logical_or(self.odd, self.slot == 0),
        )
        self.same = ((pair ^ row) & 1) == 0
        self.stays = jnp.logical_and(self.edge, self.same)


def whole_gram_kernel(x_ref, out_ref):
    x = x_ref[...]
    gram = transposed_dot(x, x)
    squares = jnp.sum(x * x, axis=0, keepdims=True)
    mask = eye_mask()
    first = jnp.where(mask, jnp.broadcast_to(squares[:, :B], (B, B)), gram[:B, :B])
    second = jnp.where(mask, jnp.broadcast_to(squares[:, B:], (B, B)), gram[B:, B:])
    packed, diag = pack_two(first, second)
    out_ref[:B, :] = gram[:B, B:]
    out_ref[B : 2 * B, :] = packed
    out_ref[2 * B :, :] = diag


def whole_gram(x):
    return call(whole_gram_kernel, [(2 * B + 8, B)], (x,))[0]


def base_of(way, rows, message):
    return rows + (message.shape[0] if way == JOINED else 0)


def older(odd, mu, mw):
    hu, hw = mu[PACKED:], mw[PACKED:]
    return jnp.where(odd, hu, hw), jnp.where(odd, hw, hu)


def cross_solve(across, odd, mu, mw, offs):
    gu, gw = unpack(mu[:PACKED]), unpack(mw[:PACKED])
    return solve(jnp.where(odd, gu, gw), across, jnp.where(odd, gw, gu), offs)


def solve_kernel(step, layout, count, offs_ref, *refs):
    parts, refs = refs[:count], refs[count:]
    place = Place(layout)
    odd = place.odd
    offs = step_offsets(offs_ref, step)
    if step == 0:
        rotation_ref, *messages = refs
        gram = tree_sum([p[...] for p in parts])
        first, second = unpack_two(gram[B : 2 * B], gram[2 * B : 2 * B + 1])
        angles, rotation, first, second = solve(first, gram[:B], second, offs)
        past = ()
    else:
        mu_ref, mw_ref, rotation_ref, *messages = refs
        mu, mw = mu_ref[...], mw_ref[...]
        gram = tree_sum([p[...] for p in parts])
        angles, rotation, first, second = cross_solve(gram, odd, mu, mw, offs)
        past = older(odd, mu, mw)
    rotation_ref[...] = rotation
    packed = pack(first), pack(second)
    for message, gives_first in zip(messages, place.gives_first):
        message[:PACKED, :] = jnp.where(gives_first, *packed)
        write_record(message, PACKED, angles)
        at = PACKED + RECORD
        for history in past:
            message[at : at + history.shape[0], :] = history
            at += history.shape[0]


def solved(step, layout, offsets, parts, messages=()):
    small = PACKED + RECORD
    if step:
        small += 2 * (messages[0].shape[0] - PACKED)
    kernel = functools.partial(solve_kernel, step, layout, len(parts))
    shapes = [(2 * B, 2 * B), (small, B), (small, B)]
    return call(kernel, shapes, (offsets, *parts, *messages))


def turn_kernel(ways, layout, ordered, rotation_ref, near_ref, far_ref, *refs):
    count = 1 if ordered else 2
    xs, outs = refs[:count], list(refs[count:])
    place = Place(layout)
    rows = outs[0].shape[0] - base_excess(ways, near_ref)
    x = jnp.concatenate([x_ref[:rows, :] for x_ref in xs], axis=1)
    rotation = rotation_ref[...]
    if not ordered:
        swapped = jnp.concatenate([rotation[B:], rotation[:B]], axis=0)
        rotation = jnp.where(place.odd, rotation, swapped)
    if len(outs) == 1:
        rotation = jnp.where(place.gives_first[0], rotation[:, :B], rotation[:, B:])
    x = product(x, rotation)
    messages = [m for m, way in zip((near_ref, far_ref), ways) if way != RAW]
    sides = [g for g, way in zip(place.gives_first, ways) if way != RAW]
    kept = [way for way in ways if way != RAW]
    for out, message, gives_first, way in zip(outs, messages, sides, kept):
        if way == JOINED:
            out[rows:, :] = message[...]
        if len(outs) == 1:
            out[:rows, :] = x
            continue

        @pl.when(gives_first)
        def _():
            out[:rows, :] = x[:, :B]

        @pl.when(jnp.logical_not(gives_first))
        def _():
            out[:rows, :] = x[:, B:]


def base_excess(ways, message):
    way = next(w for w in ways if w != RAW)
    return message.shape[0] if way == JOINED else 0


def turned(rows, ways, layout, rotation, near, far, *xs):
    shapes = [(base_of(way, rows, near), B) for way in ways if way != RAW]
    kernel = functools.partial(turn_kernel, ways, layout, len(xs) == 1)
    return call(kernel, shapes, (rotation, near, far, *xs))


def half_rotation(angles, offs, take_first):
    halves = [rotate(top, low, angles, offs) for top, low in identity_halves()]
    return jnp.concatenate([jnp.where(take_first, top, low) for top, low in halves], axis=0)


def arrive_kernel(block_ref, u_ref, w_ref, own_ref, x_ref, gram_ref, mw_ref):
    rows = x_ref.shape[0]
    place = Place(crossed)
    own = place.stays
    mw_ref[...] = jnp.where(own, own_ref[rows:, :], w_ref[rows:, :])

    def put(first, block):
        @pl.when(first)
        def _():
            x_ref[:, :B] = block

        @pl.when(jnp.logical_not(first))
        def _():
            x_ref[:, B:] = block

    put(place.odd, block_ref[...])
    even = jnp.logical_not(place.odd)

    @pl.when(own)
    def _():
        put(even, own_ref[:rows, :])

    @pl.when(jnp.logical_not(own))
    def _():
        put(even, w_ref[:rows, :])

    gram_ref[...] = transposed_dot(x_ref[:, :B], x_ref[:, B:])


def arrive(block, u, w, own):
    rows = block.shape[0]
    shapes = [(rows, 2 * B), (B, B), u.shape]
    return call(arrive_kernel, shapes, (block, u, w, own))


def arrive_raw_kernel(step, offs_ref, u_ref, w_ref, own_ref, raw_ref, *refs):
    block_ref, gram_ref, mu_ref, mw_ref = refs
    rows = raw_ref.shape[0]
    place = Place(crossed)
    own = place.edge
    mu_ref[...] = u_ref[rows:, :]
    mw_ref[...] = jnp.where(own, own_ref[...], w_ref[...])
    at = slice(PACKED, PACKED + RECORD)
    angles = read_record(jnp.where(own, own_ref[at, :], w_ref[at, :]))
    takes_first = jnp.logical_or(jnp.logical_not(place.odd), place.slot == place.pairs - 1)
    half = half_rotation(angles, step_offsets(offs_ref, step), takes_first)
    block = product(raw_ref[...], half)
    block_ref[...] = block
    gram = transposed_dot(u_ref[:rows, :], block)
    gram_ref[...] = jnp.where(place.odd, gram, gram.T)


def arrive_raw(step, offsets, u, w, own, raw):
    rows = raw.shape[0]
    kernel = functools.partial(arrive_raw_kernel, step)
    shapes = [(rows, B), (B, B), w.shape, w.shape]
    return call(kernel, shapes, (offsets, u, w, own, raw))


def ready_kernel(step, offs_ref, u_ref, block_ref, raw_ref, out_ref):
    place = Place(crossed)

    @pl.when(place.same)
    def _():
        takes_first = jnp.logical_and(place.odd, place.slot != 1)
        angles = read_record(u_ref[PACKED : PACKED + RECORD, :])
        half = half_rotation(angles, step_offsets(offs_ref, step), takes_first)
        out_ref[...] = product(raw_ref[...], half)

    @pl.when(jnp.logical_not(place.same))
    def _():
        out_ref[...] = block_ref[...]


def ready(step, offsets, u, block, raw):
    kernel = functools.partial(ready_kernel, step)
    return call(kernel, [block.shape], (offsets, u, block, raw))[0]


def last_gram_kernel(rows, u_ref, w_ref, own_ref, out_ref):
    own = Place(given).stays

    @pl.when(own)
    def _():
        out_ref[...] = transposed_dot(u_ref[:rows, :], own_ref[:rows, :])

    @pl.when(jnp.logical_not(own))
    def _():
        out_ref[...] = transposed_dot(u_ref[:rows, :], w_ref[:rows, :])


def last_gram(rows, messages):
    return call(functools.partial(last_gram_kernel, rows), [(B, B)], messages)[0]


def settle_kernel(u_ref, w_ref, own_ref, x_ref, mu_ref, mw_ref):
    rows = x_ref.shape[0]
    place = Place(given)
    odd, own = place.odd, place.stays
    u, w = u_ref[...], jnp.where(own, own_ref[...], w_ref[...])
    x_ref[:, :B] = jnp.where(odd, u[:rows], w[:rows])
    x_ref[:, B:] = jnp.where(odd, w[:rows], u[:rows])
    mu_ref[...] = u[rows:]
    mw_ref[...] = w[rows:]


def settle(rows, messages):
    small = messages[0].shape[0] - rows
    shapes = [(rows, 2 * B), (small, B), (small, B)]
    return call(settle_kernel, shapes, messages)


def came_from(slot, is_first, pairs):
    if is_first:
        return jnp.where(slot == 0, 0, slot - 1), slot != 1
    last = slot == pairs - 1
    return jnp.where(last, slot, slot + 1), last


def vectors_kernel(offs_ref, mu_ref, mw_ref, out_ref):
    place = Place(given)
    slot, pairs, part, odd = place.slot, place.pairs, place.part, place.odd
    held_slots = out_ref.shape[0] // (2 * B)
    unit = jnp.where(eye_mask(), 1.0, 0.0)
    zero = jnp.zeros_like(unit)
    pasts = older(odd, mu_ref[...], mw_ref[...])
    nodes = [
        (unit, *came_from(slot, is_first, pairs), past, at)
        for is_first, past, at in ((True, pasts[0], 0), (False, pasts[1], B))
    ]
    for step in reversed(range(STEPS - 1)):
        offs = step_offsets(offs_ref, step)
        below = []
        for block, node, was_first, past, at in nodes:
            top, low = rotate_back(
                jnp.where(was_first, block, zero),
                jnp.where(was_first, zero, block),
                read_record(past[:RECORD]),
                offs,
            )
            if step == 0:
                below.append((top, low, node, at))
                continue
            half = (past.shape[0] - RECORD) // 2
            top_past, low_past = past[RECORD : RECORD + half], past[RECORD + half :]
            below.append((top, *came_from(node, True, pairs), top_past, at))
            below.append((low, *came_from(node, False, pairs), low_past, at))
        nodes = below
    out_ref[...] = jnp.zeros_like(out_ref)
    for top, low, node, column in nodes:

        @pl.when(node // held_slots == part)
        def _():
            at = pl.multiple_of((node - part * held_slots) * (2 * B), 2 * B)
            out_ref[pl.ds(at, B), column : column + B] += top.T
            out_ref[pl.ds(at + B, B), column : column + B] += low.T


def vectors_before_last(height, offsets, messages):
    return call(vectors_kernel, [(height, 2 * B)], (offsets, *messages))[0]


def last_kernel(count, offs_ref, *refs):
    parts, (mu_ref, mw_ref, x_ref, v_ref, x_out, v_out) = refs[:count], refs[count:]
    odd = Place(given).odd
    gram = tree_sum([p[...] for p in parts])
    across = jnp.where(odd, gram, gram.T)
    offs = step_offsets(offs_ref, STEPS - 1)
    _, rotation, _, _ = cross_solve(across, odd, mu_ref[...], mw_ref[...], offs)
    x_out[...] = product(x_ref[...], rotation)
    v_out[...] = product(v_ref[...], rotation)


def last_step(offsets, parts, messages, x, v):
    kernel = functools.partial(last_kernel, len(parts))
    return call(kernel, [x.shape, v.shape], (offsets, *parts, *messages, x, v))


def in_stages(partial, layout):
    distance, count = 1, lax.axis_size("row")
    while 2 * distance < count:
        partial = partial + send(partial, layout, layout, other_part(distance))
        distance *= 2
    if distance < count:
        return [partial, send(partial, layout, layout, other_part(distance))]
    return [partial]


def at_once(partial, layout):
    others = range(1, lax.axis_size("row"))
    return [partial] + [send(partial, layout, layout, other_part(d)) for d in others]


def body(whitened, offsets):
    rows, width = whitened.shape
    height = lax.axis_size("pair") * width // lax.axis_size("row")

    raw = send(whitened, given, crossed, inner)
    terms = in_stages(whole_gram(whitened), given)
    rotation, near, far = solved(0, given, offsets, terms)
    u = send(near, given, crossed, inner)
    block, far = turned(rows, (EITHER, JOINED), given, rotation, near, far, whitened)
    w = send(far, given, crossed, outer)
    block = send(block, given, given, other_part(1))
    block = ready(0, offsets, u, block, raw)
    x, cross, mw = arrive(block, u, w, far)

    raw = send(x, crossed, crossed, outer, swap=False)
    terms = at_once(cross, crossed)
    rotation, near, far = solved(1, crossed, offsets, terms, (u, mw))
    w = send(far, crossed, crossed, outer)
    (near,) = turned(rows, (JOINED, RAW), crossed, rotation, near, far, x)
    u = send(near, crossed, crossed, inner)
    block, cross, mu, mw = arrive_raw(1, offsets, u, w, far, raw)

    terms = at_once(cross, crossed)
    rotation, near, far = solved(2, crossed, offsets, terms, (mu, mw))
    near, far = turned(rows, (JOINED, JOINED), crossed, rotation, near, far, u, block)
    w = send(far, crossed, given, outer)
    u = send(near, crossed, given, inner)
    terms = in_stages(last_gram(rows, (u, w, far)), given)
    x, mu, mw = settle(rows, (u, w, far))
    vectors = vectors_before_last(height, offsets, (mu, mw))
    return last_step(offsets, terms, (mu, mw), x, vectors)


def solution(mesh):
    in_specs = (P("row", "pair"), P())
    out_specs = (P("row", "pair"), P("row", "pair"))
    return jax.shard_map(body, mesh=mesh, in_specs=in_specs, out_specs=out_specs, check_vma=False)
```

```python
import functools

import jax
import jax.numpy as jnp
from jax import lax
from jax.experimental import pallas as pl
from jax.experimental.pallas import tpu as pltpu
from jax.sharding import PartitionSpec as P

B = 128
ROUNDS = 4
STEPS = 4
RECORD = 2 * ROUNDS
PIECES = 4
HALF = B // 2
PACKED = HALF + 8
AXES = ("pair", "row")
PARAMS = pltpu.CompilerParams(vmem_limit_bytes=40 * 1024 * 1024)
VMEM = pl.BlockSpec(memory_space=pltpu.VMEM)


def given(slot, part):
    return slot, part


def crossed(slot, part):
    return (slot & ~1) | (part & 1), (part & ~1) | (slot & 1)


def route(source, target, change, swap=True):
    pairs, rows = lax.axis_size("pair"), lax.axis_size("row")
    line = []
    for slot in range(pairs):
        for part in range(rows):
            a = source(slot, part)
            b = target(*change(slot, part, pairs))
            if swap and a == b:
                b = a[0], a[1] ^ (rows // 2)
            line.append((a[0] * rows + a[1], b[0] * rows + b[1]))
    return line


def inner(slot, part, pairs):
    return slot ^ 1, part


def outer(slot, part, pairs):
    if slot == 0 or slot == pairs - 1:
        return slot, part
    return (slot + 1 if slot & 1 else slot - 1), part


def send(x, source, target, change, swap=True):
    return lax.ppermute(x, AXES, route(source, target, change, swap))


def other_part(distance):
    return lambda slot, part, pairs: (slot, part ^ distance)


def eye_mask():
    shape = (B, B)
    return lax.broadcasted_iota(jnp.int32, shape, 0) == lax.broadcasted_iota(jnp.int32, shape, 1)


def identity_halves():
    unit = jnp.where(eye_mask(), 1.0, 0.0)
    return [(unit, jnp.zeros_like(unit)), (jnp.zeros_like(unit), unit)]


def diagonal(mask, block):
    return jnp.sum(jnp.where(mask, block, 0.0), axis=0, keepdims=True)


def as_column(mask, row):
    return jnp.sum(jnp.where(mask, jnp.broadcast_to(row, (B, B)), 0.0), axis=1, keepdims=True)


def solve(first, across, second, offs):
    mask = eye_mask()
    distance = (index((B, B), 1) - index((B, B), 0)) & (B - 1)
    angles = []
    turns = identity_halves()
    a, d = diagonal(mask, first), diagonal(mask, second)
    held = 0
    for r in range(ROUNDS):
        turn, ahead = (held - offs[r]) & (B - 1), (offs[r] - held) & (B - 1)
        held = offs[r]
        c0 = pltpu.roll(diagonal(distance == ahead, across), turn, 1)
        d = pltpu.roll(d, turn, 1)
        across = pltpu.roll(across, turn, 1)
        second = pltpu.roll(pltpu.roll(second, turn, 1), turn, 0)
        turns = [(top, pltpu.roll(low, turn, 1)) for top, low in turns]
        h = 0.5 * (d - a)
        radius = jnp.sqrt(h * h + c0 * c0)
        sg = jnp.where(h >= 0, 1.0, -1.0)
        t = -sg * c0 / (jnp.abs(h) + radius + 1e-06 * (a + d))
        c = lax.rsqrt(1.0 + t * t)
        s = t * c
        angles.append((c, s))
        cc, sc = as_column(mask, c), as_column(mask, s)
        below = across.T
        first1 = first * c + across * s
        across1 = across * c - first * s
        below1 = below * c + second * s
        second1 = second * c - below * s
        first = cc * first1 + sc * below1
        across = cc * across1 + sc * second1
        second = cc * second1 - sc * across1
        moved = s * (s * (d - a) + 2.0 * (c * c0))
        a, d = a + moved, d - moved
        turns = [(c * top + s * low, c * low - s * top) for top, low in turns]
    first = jnp.where(mask, jnp.broadcast_to(a, (B, B)), first)
    second = jnp.where(mask, jnp.broadcast_to(d, (B, B)), second)
    second = pltpu.roll(pltpu.roll(second, held, 1), held, 0)
    turns = [(top, pltpu.roll(low, held, 1)) for top, low in turns]
    rotation = jnp.concatenate([jnp.concatenate(t, axis=1) for t in turns], axis=0)
    return angles, rotation, first, second


def rotate(first, second, angles, offs):
    held = 0
    for r in range(ROUNDS):
        c, s = angles[r]
        second = pltpu.roll(second, (held - offs[r]) & (B - 1), 1)
        held = offs[r]
        first, second = c * first + s * second, c * second - s * first
    return first, pltpu.roll(second, held, 1)


def rotate_back(first, second, angles, offs):
    held = 0
    for r in reversed(range(ROUNDS)):
        c, s = angles[r]
        second = pltpu.roll(second, (held - offs[r]) & (B - 1), 1)
        held = offs[r]
        first, second = c * first - s * second, s * first + c * second
    return first, pltpu.roll(second, held, 1)


def read_record(rows):
    return [(rows[r : r + 1], rows[ROUNDS + r : ROUNDS + r + 1]) for r in range(ROUNDS)]


def write_record(ref, at, angles):
    for r, (c, s) in enumerate(angles):
        ref[at + r : at + r + 1, :] = c
        ref[at + ROUNDS + r : at + ROUNDS + r + 1, :] = s


def index(shape, axis):
    return lax.broadcasted_iota(jnp.int32, shape, axis)


def pack(block):
    shape = (HALF, B)
    low = jnp.logical_and(index(shape, 1) < HALF, index(shape, 0) > index(shape, 1))
    rows = jnp.where(low, pltpu.roll(block[HALF:], HALF, 1), block[:HALF])
    return jnp.concatenate([rows, jnp.broadcast_to(diagonal(eye_mask(), block), (8, B))], axis=0)


def unpack(packed):
    rows, diag = packed[:HALF], packed[HALF : HALF + 1]
    turned = jnp.concatenate([rows, rows], axis=0).T
    shape = (HALF, B)
    i, j = index(shape, 0), index(shape, 1)
    left = j < HALF
    top = jnp.where(jnp.logical_and(left, i > j), turned[:HALF], rows)
    right = jnp.where(i > j - HALF, pltpu.roll(rows, HALF, 1), turned[:HALF])
    right = jnp.where(i == j - HALF, jnp.broadcast_to(diag, shape), right)
    return jnp.concatenate([top, jnp.where(left, turned[HALF:], right)], axis=0)


def pack_two(first, second):
    rows, cols = index((B, B), 0), index((B, B), 1)
    return [
        jnp.where(rows <= cols, first, second),
        jnp.broadcast_to(diagonal(eye_mask(), second), (8, B)),
    ]


def unpack_two(block, diag):
    rows, cols = index((B, B), 0), index((B, B), 1)
    turned = block.T
    second = jnp.where(rows > cols, block, turned)
    second = jnp.where(rows == cols, jnp.broadcast_to(diag, (B, B)), second)
    return jnp.where(rows <= cols, block, turned), second


def tree_sum(parts):
    parts = list(parts)
    while len(parts) > 1:
        parts = [parts[i] + parts[i + 1] for i in range(0, len(parts), 2)]
    return parts[0]


def split(x):
    high = x.astype(jnp.bfloat16)
    return high, (x - high.astype(jnp.float32)).astype(jnp.bfloat16)


def product(x, rotation):
    xh, xl = split(x)
    rh, rl = split(rotation)

    def dot(a, b):
        return jnp.dot(a, b, preferred_element_type=jnp.float32)

    return (dot(xl, rh) + dot(xh, rl)) + dot(xh, rh)


def step_offsets(offs_ref, step):
    return [offs_ref[step, r] for r in range(ROUNDS)]


def transposed_dot(left, right):
    lh, ll = split(left)
    rh, rl = split(right)

    def dot(a, b):
        dims = (((0,), (0,)), ((), ()))
        return lax.dot_general(a, b, dims, preferred_element_type=jnp.float32)

    return (dot(ll, rh) + dot(lh, rl)) + dot(lh, rh)


JOINED, RAW, EITHER = range(3)


def call(kernel, out_shapes, arrays):
    return pl.pallas_call(
        kernel,
        out_shape=tuple(jax.ShapeDtypeStruct(shape, jnp.float32) for shape in out_shapes),
        in_specs=[VMEM] * len(arrays),
        out_specs=tuple(VMEM for _ in out_shapes),
        compiler_params=PARAMS,
    )(*arrays)


class Place:
    def __init__(self, layout):
        pair, row = lax.axis_index("pair"), lax.axis_index("row")
        self.pairs = lax.axis_size("pair")
        self.slot, self.part = layout(pair, row)
        self.odd = (self.slot & 1) == 1
        self.edge = jnp.logical_or(self.slot == 0, self.slot == self.pairs - 1)
        self.gives_first = (
            jnp.logical_and(jnp.logical_not(self.odd), self.slot != 0),
            jnp.logical_or(self.odd, self.slot == 0),
        )
        self.same = ((pair ^ row) & 1) == 0
        self.stays = jnp.logical_and(self.edge, self.same)


def whole_gram_kernel(x_ref, out_ref):
    x = x_ref[...]
    gram = transposed_dot(x, x)
    squares = jnp.sum(x * x, axis=0, keepdims=True)
    mask = eye_mask()
    first = jnp.where(mask, jnp.broadcast_to(squares[:, :B], (B, B)), gram[:B, :B])
    second = jnp.where(mask, jnp.broadcast_to(squares[:, B:], (B, B)), gram[B:, B:])
    packed, diag = pack_two(first, second)
    out_ref[:B, :] = gram[:B, B:]
    out_ref[B : 2 * B, :] = packed
    out_ref[2 * B :, :] = diag


def whole_gram(x):
    return call(whole_gram_kernel, [(2 * B + 8, B)], (x,))[0]


def base_of(way, rows, message):
    return rows + (message.shape[0] if way == JOINED else 0)


def older(odd, mu, mw):
    hu, hw = mu[PACKED:], mw[PACKED:]
    return jnp.where(odd, hu, hw), jnp.where(odd, hw, hu)


def cross_solve(across, odd, mu, mw, offs):
    gu, gw = unpack(mu[:PACKED]), unpack(mw[:PACKED])
    return solve(jnp.where(odd, gu, gw), across, jnp.where(odd, gw, gu), offs)


def solve_kernel(step, layout, count, offs_ref, *refs):
    parts, refs = refs[:count], refs[count:]
    place = Place(layout)
    odd = place.odd
    offs = step_offsets(offs_ref, step)
    if step == 0:
        rotation_ref, *messages = refs
        gram = tree_sum([p[...] for p in parts])
        first, second = unpack_two(gram[B : 2 * B], gram[2 * B : 2 * B + 1])
        angles, rotation, first, second = solve(first, gram[:B], second, offs)
        past = ()
    else:
        mu_ref, mw_ref, rotation_ref, *messages = refs
        mu, mw = mu_ref[...], mw_ref[...]
        gram = tree_sum([p[...] for p in parts])
        angles, rotation, first, second = cross_solve(gram, odd, mu, mw, offs)
        past = older(odd, mu, mw)
    rotation_ref[...] = rotation
    packed = pack(first), pack(second)
    for message, gives_first in zip(messages, place.gives_first):
        message[:PACKED, :] = jnp.where(gives_first, *packed)
        write_record(message, PACKED, angles)
        at = PACKED + RECORD
        for history in past:
            message[at : at + history.shape[0], :] = history
            at += history.shape[0]


def solved(step, layout, offsets, parts, messages=()):
    small = PACKED + RECORD
    if step:
        small += 2 * (messages[0].shape[0] - PACKED)
    kernel = functools.partial(solve_kernel, step, layout, len(parts))
    shapes = [(2 * B, 2 * B), (small, B), (small, B)]
    return call(kernel, shapes, (offsets, *parts, *messages))


def turn_kernel(ways, layout, ordered, rotation_ref, near_ref, far_ref, *refs):
    count = 1 if ordered else 2
    xs, outs = refs[:count], list(refs[count:])
    place = Place(layout)
    rows = outs[0].shape[0] - base_excess(ways, near_ref)
    x = jnp.concatenate([x_ref[:rows, :] for x_ref in xs], axis=1)
    rotation = rotation_ref[...]
    if not ordered:
        swapped = jnp.concatenate([rotation[B:], rotation[:B]], axis=0)
        rotation = jnp.where(place.odd, rotation, swapped)
    if len(outs) == 1:
        rotation = jnp.where(place.gives_first[0], rotation[:, :B], rotation[:, B:])
    x = product(x, rotation)
    messages = [m for m, way in zip((near_ref, far_ref), ways) if way != RAW]
    sides = [g for g, way in zip(place.gives_first, ways) if way != RAW]
    kept = [way for way in ways if way != RAW]
    for out, message, gives_first, way in zip(outs, messages, sides, kept):
        if way == JOINED:
            out[rows:, :] = message[...]
        if len(outs) == 1:
            out[:rows, :] = x
            continue

        @pl.when(gives_first)
        def _():
            out[:rows, :] = x[:, :B]

        @pl.when(jnp.logical_not(gives_first))
        def _():
            out[:rows, :] = x[:, B:]


def base_excess(ways, message):
    way = next(w for w in ways if w != RAW)
    return message.shape[0] if way == JOINED else 0


def turned(rows, ways, layout, rotation, near, far, *xs):
    shapes = [(base_of(way, rows, near), B) for way in ways if way != RAW]
    kernel = functools.partial(turn_kernel, ways, layout, len(xs) == 1)
    return call(kernel, shapes, (rotation, near, far, *xs))


def half_rotation(angles, offs, take_first):
    halves = [rotate(top, low, angles, offs) for top, low in identity_halves()]
    return jnp.concatenate([jnp.where(take_first, top, low) for top, low in halves], axis=0)


def arrive_kernel(block_ref, u_ref, w_ref, own_ref, x_ref, gram_ref, mw_ref):
    rows = x_ref.shape[0]
    place = Place(crossed)
    own = place.stays
    mw_ref[...] = jnp.where(own, own_ref[rows:, :], w_ref[rows:, :])

    def put(first, block):
        @pl.when(first)
        def _():
            x_ref[:, :B] = block

        @pl.when(jnp.logical_not(first))
        def _():
            x_ref[:, B:] = block

    put(place.odd, block_ref[...])
    even = jnp.logical_not(place.odd)

    @pl.when(own)
    def _():
        put(even, own_ref[:rows, :])

    @pl.when(jnp.logical_not(own))
    def _():
        put(even, w_ref[:rows, :])

    gram_ref[...] = transposed_dot(x_ref[:, :B], x_ref[:, B:])


def arrive(block, u, w, own):
    rows = block.shape[0]
    shapes = [(rows, 2 * B), (B, B), u.shape]
    return call(arrive_kernel, shapes, (block, u, w, own))


def ahead_kernel(u_ref, raw_ref, out_ref):
    out_ref[...] = transposed_dot(u_ref[: raw_ref.shape[0], :], raw_ref[...])


def ahead(u, raw):
    return call(ahead_kernel, [(B, 2 * B)], (u, raw))[0]


def arrive_raw_kernel(step, rows, offs_ref, u_ref, w_ref, own_ref, ahead_ref, *refs):
    half_ref, gram_ref, mu_ref, mw_ref = refs
    place = Place(crossed)
    own = place.edge
    mu_ref[...] = u_ref[rows:, :]
    mw_ref[...] = jnp.where(own, own_ref[...], w_ref[...])
    at = slice(PACKED, PACKED + RECORD)
    angles = read_record(jnp.where(own, own_ref[at, :], w_ref[at, :]))
    takes_first = jnp.logical_or(jnp.logical_not(place.odd), place.slot == place.pairs - 1)
    half = half_rotation(angles, step_offsets(offs_ref, step), takes_first)
    half_ref[...] = half
    gram = product(ahead_ref[...], half)
    gram_ref[...] = jnp.where(place.odd, gram, gram.T)


def arrive_raw(step, rows, offsets, u, w, own, products):
    kernel = functools.partial(arrive_raw_kernel, step, rows)
    shapes = [(2 * B, B), (B, B), w.shape, w.shape]
    return call(kernel, shapes, (offsets, u, w, own, products))


def outer_block_kernel(raw_ref, half_ref, out_ref):
    out_ref[...] = product(raw_ref[...], half_ref[...])


def outer_block(raw, half):
    return call(outer_block_kernel, [(raw.shape[0], B)], (raw, half))[0]


def ready_kernel(step, offs_ref, u_ref, block_ref, raw_ref, out_ref):
    place = Place(crossed)

    @pl.when(place.same)
    def _():
        takes_first = jnp.logical_and(place.odd, place.slot != 1)
        angles = read_record(u_ref[PACKED : PACKED + RECORD, :])
        half = half_rotation(angles, step_offsets(offs_ref, step), takes_first)
        out_ref[...] = product(raw_ref[...], half)

    @pl.when(jnp.logical_not(place.same))
    def _():
        out_ref[...] = block_ref[...]


def ready(step, offsets, u, block, raw):
    kernel = functools.partial(ready_kernel, step)
    return call(kernel, [block.shape], (offsets, u, block, raw))[0]


def last_gram_kernel(rows, u_ref, w_ref, own_ref, out_ref):
    own = Place(given).stays

    @pl.when(own)
    def _():
        out_ref[...] = transposed_dot(u_ref[:rows, :], own_ref[:rows, :])

    @pl.when(jnp.logical_not(own))
    def _():
        out_ref[...] = transposed_dot(u_ref[:rows, :], w_ref[:rows, :])


def last_gram(rows, messages):
    return call(functools.partial(last_gram_kernel, rows), [(B, B)], messages)[0]


def settle_kernel(u_ref, w_ref, own_ref, x_ref, mu_ref, mw_ref):
    rows = x_ref.shape[0]
    place = Place(given)
    odd, own = place.odd, place.stays
    u, w = u_ref[...], jnp.where(own, own_ref[...], w_ref[...])
    x_ref[:, :B] = jnp.where(odd, u[:rows], w[:rows])
    x_ref[:, B:] = jnp.where(odd, w[:rows], u[:rows])
    mu_ref[...] = u[rows:]
    mw_ref[...] = w[rows:]


def settle(rows, messages):
    small = messages[0].shape[0] - rows
    shapes = [(rows, 2 * B), (small, B), (small, B)]
    return call(settle_kernel, shapes, messages)


def came_from(slot, is_first, pairs):
    if is_first:
        return jnp.where(slot == 0, 0, slot - 1), slot != 1
    last = slot == pairs - 1
    return jnp.where(last, slot, slot + 1), last


def vectors_kernel(offs_ref, mu_ref, mw_ref, out_ref):
    place = Place(given)
    slot, pairs, part, odd = place.slot, place.pairs, place.part, place.odd
    held_slots = out_ref.shape[0] // (2 * B)
    unit = jnp.where(eye_mask(), 1.0, 0.0)
    zero = jnp.zeros_like(unit)
    pasts = older(odd, mu_ref[...], mw_ref[...])
    nodes = [
        (unit, *came_from(slot, is_first, pairs), past, at)
        for is_first, past, at in ((True, pasts[0], 0), (False, pasts[1], B))
    ]
    for step in reversed(range(STEPS - 1)):
        offs = step_offsets(offs_ref, step)
        below = []
        for block, node, was_first, past, at in nodes:
            top, low = rotate_back(
                jnp.where(was_first, block, zero),
                jnp.where(was_first, zero, block),
                read_record(past[:RECORD]),
                offs,
            )
            if step == 0:
                below.append((top, low, node, at))
                continue
            half = (past.shape[0] - RECORD) // 2
            top_past, low_past = past[RECORD : RECORD + half], past[RECORD + half :]
            below.append((top, *came_from(node, True, pairs), top_past, at))
            below.append((low, *came_from(node, False, pairs), low_past, at))
        nodes = below
    out_ref[...] = jnp.zeros_like(out_ref)
    for top, low, node, column in nodes:

        @pl.when(node // held_slots == part)
        def _():
            at = pl.multiple_of((node - part * held_slots) * (2 * B), 2 * B)
            out_ref[pl.ds(at, B), column : column + B] += top.T
            out_ref[pl.ds(at + B, B), column : column + B] += low.T


def vectors_before_last(height, offsets, messages):
    return call(vectors_kernel, [(height, 2 * B)], (offsets, *messages))[0]


def last_kernel(count, offs_ref, *refs):
    parts, refs = refs[:count], refs[count:]
    mu_ref, mw_ref, x_ref, v_ref, x_out, v_out, x_held, v_held, sems = refs
    odd = Place(given).odd
    gram = tree_sum([p[...] for p in parts])
    across = jnp.where(odd, gram, gram.T)
    offs = step_offsets(offs_ref, STEPS - 1)
    _, rotation, _, _ = cross_solve(across, odd, mu_ref[...], mw_ref[...], offs)
    copies = []

    def put(source, held, out, at):
        held[at, :] = product(source[at, :], rotation)
        copies.append(pltpu.make_async_copy(held.at[at], out.at[at], sems.at[len(copies)]))
        copies[-1].start()

    size = x_ref.shape[0] // PIECES
    for i in range(PIECES):
        put(x_ref, x_held, x_out, pl.ds(i * size, size))
    put(v_ref, v_held, v_out, pl.ds(0, v_ref.shape[0]))
    for copy in copies:
        copy.wait()


def last_step(offsets, parts, messages, x, v):
    outside = pl.BlockSpec(memory_space=pl.ANY)
    return pl.pallas_call(
        functools.partial(last_kernel, len(parts)),
        out_shape=tuple(jax.ShapeDtypeStruct(a.shape, jnp.float32) for a in (x, v)),
        in_specs=[VMEM] * (len(parts) + 5),
        out_specs=(outside, outside),
        scratch_shapes=[pltpu.VMEM(a.shape, jnp.float32) for a in (x, v)]
        + [pltpu.SemaphoreType.DMA((PIECES + 1,))],
        compiler_params=PARAMS,
    )(offsets, *parts, *messages, x, v)


def in_stages(partial, layout):
    distance, count = 1, lax.axis_size("row")
    while 2 * distance < count:
        partial = partial + send(partial, layout, layout, other_part(distance))
        distance *= 2
    if distance < count:
        return [partial, send(partial, layout, layout, other_part(distance))]
    return [partial]


def at_once(partial, layout):
    others = range(1, lax.axis_size("row"))
    return [partial] + [send(partial, layout, layout, other_part(d)) for d in others]


def body(whitened, offsets):
    rows, width = whitened.shape
    height = lax.axis_size("pair") * width // lax.axis_size("row")

    raw = send(whitened, given, crossed, inner)
    terms = in_stages(whole_gram(whitened), given)
    rotation, near, far = solved(0, given, offsets, terms)
    u = send(near, given, crossed, inner)
    block, far = turned(rows, (EITHER, JOINED), given, rotation, near, far, whitened)
    w = send(far, given, crossed, outer)
    block = send(block, given, given, other_part(1))
    block = ready(0, offsets, u, block, raw)
    x, cross, mw = arrive(block, u, w, far)

    raw = send(x, crossed, crossed, outer, swap=False)
    terms = at_once(cross, crossed)
    rotation, near, far = solved(1, crossed, offsets, terms, (u, mw))
    w = send(far, crossed, crossed, outer)
    (near,) = turned(rows, (JOINED, RAW), crossed, rotation, near, far, x)
    u = send(near, crossed, crossed, inner)
    half, cross, mu, mw = arrive_raw(1, rows, offsets, u, w, far, ahead(u, raw))
    block = outer_block(raw, half)

    terms = at_once(cross, crossed)
    rotation, near, far = solved(2, crossed, offsets, terms, (mu, mw))
    near, far = turned(rows, (JOINED, JOINED), crossed, rotation, near, far, u, block)
    w = send(far, crossed, given, outer)
    u = send(near, crossed, given, inner)
    terms = in_stages(last_gram(rows, (u, w, far)), given)
    x, mu, mw = settle(rows, (u, w, far))
    vectors = vectors_before_last(height, offsets, (mu, mw))
    return last_step(offsets, terms, (mu, mw), x, vectors)


def solution(mesh):
    in_specs = (P("row", "pair"), P())
    out_specs = (P("row", "pair"), P("row", "pair"))
    return jax.shard_map(body, mesh=mesh, in_specs=in_specs, out_specs=out_specs, check_vma=False)
```

```python
import functools

import jax
import jax.numpy as jnp
from jax import lax
from jax.experimental import pallas as pl
from jax.experimental.pallas import tpu as pltpu
from jax.sharding import PartitionSpec as P

B = 128
ROUNDS = 4
STEPS = 4
RECORD = 2 * ROUNDS
PIECES = 4
HALF = B // 2
PACKED = HALF + 8
AXES = ("pair", "row")
PARAMS = pltpu.CompilerParams(vmem_limit_bytes=40 * 1024 * 1024)
VMEM = pl.BlockSpec(memory_space=pltpu.VMEM)


def given(slot, part):
    return slot, part


def crossed(slot, part):
    return (slot & ~1) | (part & 1), (part & ~1) | (slot & 1)


def route(source, target, change, swap=True):
    pairs, rows = lax.axis_size("pair"), lax.axis_size("row")
    line = []
    for slot in range(pairs):
        for part in range(rows):
            a = source(slot, part)
            b = target(*change(slot, part, pairs))
            if swap and a == b:
                b = a[0], a[1] ^ (rows // 2)
            line.append((a[0] * rows + a[1], b[0] * rows + b[1]))
    return line


def inner(slot, part, pairs):
    return slot ^ 1, part


def outer(slot, part, pairs):
    if slot == 0 or slot == pairs - 1:
        return slot, part
    return (slot + 1 if slot & 1 else slot - 1), part


def send(x, source, target, change, swap=True):
    return lax.ppermute(x, AXES, route(source, target, change, swap))


def other_part(distance):
    return lambda slot, part, pairs: (slot, part ^ distance)


def eye_mask():
    shape = (B, B)
    return lax.broadcasted_iota(jnp.int32, shape, 0) == lax.broadcasted_iota(jnp.int32, shape, 1)


def identity_halves():
    unit = jnp.where(eye_mask(), 1.0, 0.0)
    return [(unit, jnp.zeros_like(unit)), (jnp.zeros_like(unit), unit)]


def diagonal(mask, block):
    return jnp.sum(jnp.where(mask, block, 0.0), axis=0, keepdims=True)


def as_column(mask, row):
    return jnp.sum(jnp.where(mask, jnp.broadcast_to(row, (B, B)), 0.0), axis=1, keepdims=True)


def solve(first, across, second, offs):
    mask = eye_mask()
    distance = (index((B, B), 1) - index((B, B), 0)) & (B - 1)
    angles = []
    turns = identity_halves()
    a, d = diagonal(mask, first), diagonal(mask, second)
    held = 0
    for r in range(ROUNDS):
        turn, ahead = (held - offs[r]) & (B - 1), (offs[r] - held) & (B - 1)
        held = offs[r]
        c0 = pltpu.roll(diagonal(distance == ahead, across), turn, 1)
        d = pltpu.roll(d, turn, 1)
        across = pltpu.roll(across, turn, 1)
        second = pltpu.roll(pltpu.roll(second, turn, 1), turn, 0)
        turns = [(top, pltpu.roll(low, turn, 1)) for top, low in turns]
        h = 0.5 * (d - a)
        radius = jnp.sqrt(h * h + c0 * c0)
        sg = jnp.where(h >= 0, 1.0, -1.0)
        t = -sg * c0 / (jnp.abs(h) + radius + 1e-06 * (a + d))
        c = lax.rsqrt(1.0 + t * t)
        s = t * c
        angles.append((c, s))
        cc, sc = as_column(mask, c), as_column(mask, s)
        below = across.T
        first1 = first * c + across * s
        across1 = across * c - first * s
        below1 = below * c + second * s
        second1 = second * c - below * s
        first = cc * first1 + sc * below1
        across = cc * across1 + sc * second1
        second = cc * second1 - sc * across1
        moved = s * (s * (d - a) + 2.0 * (c * c0))
        a, d = a + moved, d - moved
        turns = [(c * top + s * low, c * low - s * top) for top, low in turns]
    first = jnp.where(mask, jnp.broadcast_to(a, (B, B)), first)
    second = jnp.where(mask, jnp.broadcast_to(d, (B, B)), second)
    second = pltpu.roll(pltpu.roll(second, held, 1), held, 0)
    turns = [(top, pltpu.roll(low, held, 1)) for top, low in turns]
    rotation = jnp.concatenate([jnp.concatenate(t, axis=1) for t in turns], axis=0)
    return angles, rotation, first, second


def rotate(first, second, angles, offs):
    held = 0
    for r in range(ROUNDS):
        c, s = angles[r]
        second = pltpu.roll(second, (held - offs[r]) & (B - 1), 1)
        held = offs[r]
        first, second = c * first + s * second, c * second - s * first
    return first, pltpu.roll(second, held, 1)


def rotate_back(first, second, angles, offs):
    held = 0
    for r in reversed(range(ROUNDS)):
        c, s = angles[r]
        second = pltpu.roll(second, (held - offs[r]) & (B - 1), 1)
        held = offs[r]
        first, second = c * first - s * second, s * first + c * second
    return first, pltpu.roll(second, held, 1)


def read_record(rows):
    return [(rows[r : r + 1], rows[ROUNDS + r : ROUNDS + r + 1]) for r in range(ROUNDS)]


def write_record(ref, at, angles):
    for r, (c, s) in enumerate(angles):
        ref[at + r : at + r + 1, :] = c
        ref[at + ROUNDS + r : at + ROUNDS + r + 1, :] = s


def index(shape, axis):
    return lax.broadcasted_iota(jnp.int32, shape, axis)


def pack(block):
    shape = (HALF, B)
    low = jnp.logical_and(index(shape, 1) < HALF, index(shape, 0) > index(shape, 1))
    rows = jnp.where(low, pltpu.roll(block[HALF:], HALF, 1), block[:HALF])
    return jnp.concatenate([rows, jnp.broadcast_to(diagonal(eye_mask(), block), (8, B))], axis=0)


def unpack(packed):
    rows, diag = packed[:HALF], packed[HALF : HALF + 1]
    turned = jnp.concatenate([rows, rows], axis=0).T
    shape = (HALF, B)
    i, j = index(shape, 0), index(shape, 1)
    left = j < HALF
    top = jnp.where(jnp.logical_and(left, i > j), turned[:HALF], rows)
    right = jnp.where(i > j - HALF, pltpu.roll(rows, HALF, 1), turned[:HALF])
    right = jnp.where(i == j - HALF, jnp.broadcast_to(diag, shape), right)
    return jnp.concatenate([top, jnp.where(left, turned[HALF:], right)], axis=0)


def pack_two(first, second):
    rows, cols = index((B, B), 0), index((B, B), 1)
    return [
        jnp.where(rows <= cols, first, second),
        jnp.broadcast_to(diagonal(eye_mask(), second), (8, B)),
    ]


def unpack_two(block, diag):
    rows, cols = index((B, B), 0), index((B, B), 1)
    turned = block.T
    second = jnp.where(rows > cols, block, turned)
    second = jnp.where(rows == cols, jnp.broadcast_to(diag, (B, B)), second)
    return jnp.where(rows <= cols, block, turned), second


def tree_sum(parts):
    parts = list(parts)
    while len(parts) > 1:
        parts = [parts[i] + parts[i + 1] for i in range(0, len(parts), 2)]
    return parts[0]


def split(x):
    high = x.astype(jnp.bfloat16)
    return high, (x - high.astype(jnp.float32)).astype(jnp.bfloat16)


def product(x, rotation):
    xh, xl = split(x)
    rh, rl = split(rotation)

    def dot(a, b):
        return jnp.dot(a, b, preferred_element_type=jnp.float32)

    return (dot(xl, rh) + dot(xh, rl)) + dot(xh, rh)


def step_offsets(offs_ref, step):
    return [offs_ref[step, r] for r in range(ROUNDS)]


def transposed_dot(left, right):
    lh, ll = split(left)
    rh, rl = split(right)

    def dot(a, b):
        dims = (((0,), (0,)), ((), ()))
        return lax.dot_general(a, b, dims, preferred_element_type=jnp.float32)

    return (dot(ll, rh) + dot(lh, rl)) + dot(lh, rh)


JOINED, RAW, EITHER = range(3)


def call(kernel, out_shapes, arrays):
    return pl.pallas_call(
        kernel,
        out_shape=tuple(jax.ShapeDtypeStruct(shape, jnp.float32) for shape in out_shapes),
        in_specs=[VMEM] * len(arrays),
        out_specs=tuple(VMEM for _ in out_shapes),
        compiler_params=PARAMS,
    )(*arrays)


class Place:
    def __init__(self, layout):
        pair, row = lax.axis_index("pair"), lax.axis_index("row")
        self.pairs = lax.axis_size("pair")
        self.slot, self.part = layout(pair, row)
        self.odd = (self.slot & 1) == 1
        self.edge = jnp.logical_or(self.slot == 0, self.slot == self.pairs - 1)
        self.gives_first = (
            jnp.logical_and(jnp.logical_not(self.odd), self.slot != 0),
            jnp.logical_or(self.odd, self.slot == 0),
        )
        self.same = ((pair ^ row) & 1) == 0
        self.stays = jnp.logical_and(self.edge, self.same)


def whole_gram_kernel(x_ref, out_ref):
    x = x_ref[...]
    gram = transposed_dot(x, x)
    squares = jnp.sum(x * x, axis=0, keepdims=True)
    mask = eye_mask()
    first = jnp.where(mask, jnp.broadcast_to(squares[:, :B], (B, B)), gram[:B, :B])
    second = jnp.where(mask, jnp.broadcast_to(squares[:, B:], (B, B)), gram[B:, B:])
    packed, diag = pack_two(first, second)
    out_ref[:B, :] = gram[:B, B:]
    out_ref[B : 2 * B, :] = packed
    out_ref[2 * B :, :] = diag


def whole_gram(x):
    return call(whole_gram_kernel, [(2 * B + 8, B)], (x,))[0]


def base_of(way, rows, message):
    return rows + (message.shape[0] if way == JOINED else 0)


def older(odd, mu, mw):
    hu, hw = mu[PACKED:], mw[PACKED:]
    return jnp.where(odd, hu, hw), jnp.where(odd, hw, hu)


def cross_solve(across, odd, mu, mw, offs):
    gu, gw = unpack(mu[:PACKED]), unpack(mw[:PACKED])
    return solve(jnp.where(odd, gu, gw), across, jnp.where(odd, gw, gu), offs)


def solve_kernel(step, layout, count, offs_ref, *refs):
    parts, refs = refs[:count], refs[count:]
    place = Place(layout)
    odd = place.odd
    offs = step_offsets(offs_ref, step)
    if step == 0:
        rotation_ref, *messages = refs
        gram = tree_sum([p[...] for p in parts])
        first, second = unpack_two(gram[B : 2 * B], gram[2 * B : 2 * B + 1])
        angles, rotation, first, second = solve(first, gram[:B], second, offs)
        past = ()
    else:
        mu_ref, mw_ref, rotation_ref, *messages = refs
        mu, mw = mu_ref[...], mw_ref[...]
        gram = tree_sum([p[...] for p in parts])
        angles, rotation, first, second = cross_solve(gram, odd, mu, mw, offs)
        past = older(odd, mu, mw)
    rotation_ref[...] = rotation
    packed = pack(first), pack(second)
    for message, gives_first in zip(messages, place.gives_first):
        message[:PACKED, :] = jnp.where(gives_first, *packed)
        write_record(message, PACKED, angles)
        at = PACKED + RECORD
        for history in past:
            message[at : at + history.shape[0], :] = history
            at += history.shape[0]


def solved(step, layout, offsets, parts, messages=()):
    small = PACKED + RECORD
    if step:
        small += 2 * (messages[0].shape[0] - PACKED)
    kernel = functools.partial(solve_kernel, step, layout, len(parts))
    shapes = [(2 * B, 2 * B), (small, B), (small, B)]
    return call(kernel, shapes, (offsets, *parts, *messages))


def turn_kernel(ways, layout, ordered, rotation_ref, near_ref, far_ref, *refs):
    count = 1 if ordered else 2
    xs, outs = refs[:count], list(refs[count:])
    place = Place(layout)
    rows = outs[0].shape[0] - base_excess(ways, near_ref)
    x = jnp.concatenate([x_ref[:rows, :] for x_ref in xs], axis=1)
    rotation = rotation_ref[...]
    if not ordered:
        swapped = jnp.concatenate([rotation[B:], rotation[:B]], axis=0)
        rotation = jnp.where(place.odd, rotation, swapped)
    if len(outs) == 1:
        side = place.gives_first[0 if ways[1] == RAW else 1]
        rotation = jnp.where(side, rotation[:, :B], rotation[:, B:])
    x = product(x, rotation)
    messages = [m for m, way in zip((near_ref, far_ref), ways) if way != RAW]
    sides = [g for g, way in zip(place.gives_first, ways) if way != RAW]
    kept = [way for way in ways if way != RAW]
    for out, message, gives_first, way in zip(outs, messages, sides, kept):
        if way == JOINED:
            out[rows:, :] = message[...]
        if len(outs) == 1:
            out[:rows, :] = x
            continue

        @pl.when(gives_first)
        def _():
            out[:rows, :] = x[:, :B]

        @pl.when(jnp.logical_not(gives_first))
        def _():
            out[:rows, :] = x[:, B:]


def base_excess(ways, message):
    way = next(w for w in ways if w != RAW)
    return message.shape[0] if way == JOINED else 0


def turned(rows, ways, layout, rotation, near, far, *xs):
    shapes = [(base_of(way, rows, near), B) for way in ways if way != RAW]
    kernel = functools.partial(turn_kernel, ways, layout, len(xs) == 1)
    return call(kernel, shapes, (rotation, near, far, *xs))


def half_rotation(angles, offs, take_first):
    halves = [rotate(top, low, angles, offs) for top, low in identity_halves()]
    return jnp.concatenate([jnp.where(take_first, top, low) for top, low in halves], axis=0)


def arrive_kernel(block_ref, w_ref, own_ref, x_ref, mw_ref):
    rows = x_ref.shape[0]
    place = Place(crossed)
    own = place.stays
    mw_ref[...] = jnp.where(own, own_ref[rows:, :], w_ref[rows:, :])

    def put(first, block):
        @pl.when(first)
        def _():
            x_ref[:, :B] = block

        @pl.when(jnp.logical_not(first))
        def _():
            x_ref[:, B:] = block

    put(place.odd, block_ref[...])
    even = jnp.logical_not(place.odd)

    @pl.when(own)
    def _():
        put(even, own_ref[:rows, :])

    @pl.when(jnp.logical_not(own))
    def _():
        put(even, w_ref[:rows, :])


def arrive(block, w, own):
    rows = block.shape[0]
    shapes = [(rows, 2 * B), (w.shape[0] - rows, B)]
    return call(arrive_kernel, shapes, (block, w, own))


def pair_gram_kernel(x_ref, out_ref):
    out_ref[...] = transposed_dot(x_ref[:, :B], x_ref[:, B:])


def pair_gram(x):
    return call(pair_gram_kernel, [(B, B)], (x,))[0]


def ahead_kernel(u_ref, raw_ref, out_ref):
    out_ref[...] = transposed_dot(u_ref[: raw_ref.shape[0], :], raw_ref[...])


def ahead(u, raw):
    return call(ahead_kernel, [(B, 2 * B)], (u, raw))[0]


def arrive_raw_kernel(step, rows, offs_ref, u_ref, w_ref, own_ref, ahead_ref, *refs):
    half_ref, gram_ref, mu_ref, mw_ref = refs
    place = Place(crossed)
    own = place.edge
    mu_ref[...] = u_ref[rows:, :]
    mw_ref[...] = jnp.where(own, own_ref[...], w_ref[...])
    at = slice(PACKED, PACKED + RECORD)
    angles = read_record(jnp.where(own, own_ref[at, :], w_ref[at, :]))
    takes_first = jnp.logical_or(jnp.logical_not(place.odd), place.slot == place.pairs - 1)
    half = half_rotation(angles, step_offsets(offs_ref, step), takes_first)
    half_ref[...] = half
    gram = product(ahead_ref[...], half)
    gram_ref[...] = jnp.where(place.odd, gram, gram.T)


def arrive_raw(step, rows, offsets, u, w, own, products):
    kernel = functools.partial(arrive_raw_kernel, step, rows)
    shapes = [(2 * B, B), (B, B), w.shape, w.shape]
    return call(kernel, shapes, (offsets, u, w, own, products))


def outer_block_kernel(raw_ref, half_ref, out_ref):
    out_ref[...] = product(raw_ref[...], half_ref[...])


def outer_block(raw, half):
    return call(outer_block_kernel, [(raw.shape[0], B)], (raw, half))[0]


def ready_kernel(step, offs_ref, u_ref, block_ref, raw_ref, out_ref):
    place = Place(crossed)

    @pl.when(place.same)
    def _():
        takes_first = jnp.logical_and(place.odd, place.slot != 1)
        angles = read_record(u_ref[PACKED : PACKED + RECORD, :])
        half = half_rotation(angles, step_offsets(offs_ref, step), takes_first)
        out_ref[...] = product(raw_ref[...], half)

    @pl.when(jnp.logical_not(place.same))
    def _():
        out_ref[...] = block_ref[...]


def ready(step, offsets, u, block, raw):
    kernel = functools.partial(ready_kernel, step)
    return call(kernel, [block.shape], (offsets, u, block, raw))[0]


def last_gram_kernel(rows, u_ref, w_ref, own_ref, out_ref):
    own = Place(given).stays

    @pl.when(own)
    def _():
        out_ref[...] = transposed_dot(u_ref[:rows, :], own_ref[:rows, :])

    @pl.when(jnp.logical_not(own))
    def _():
        out_ref[...] = transposed_dot(u_ref[:rows, :], w_ref[:rows, :])


def last_gram(rows, messages):
    return call(functools.partial(last_gram_kernel, rows), [(B, B)], messages)[0]


def settle_kernel(u_ref, w_ref, own_ref, x_ref, mu_ref, mw_ref):
    rows = x_ref.shape[0]
    place = Place(given)
    odd, own = place.odd, place.stays
    u, w = u_ref[...], jnp.where(own, own_ref[...], w_ref[...])
    x_ref[:, :B] = jnp.where(odd, u[:rows], w[:rows])
    x_ref[:, B:] = jnp.where(odd, w[:rows], u[:rows])
    mu_ref[...] = u[rows:]
    mw_ref[...] = w[rows:]


def settle(rows, messages):
    small = messages[0].shape[0] - rows
    shapes = [(rows, 2 * B), (small, B), (small, B)]
    return call(settle_kernel, shapes, messages)


def came_from(slot, is_first, pairs):
    if is_first:
        return jnp.where(slot == 0, 0, slot - 1), slot != 1
    last = slot == pairs - 1
    return jnp.where(last, slot, slot + 1), last


def vectors_kernel(offs_ref, mu_ref, mw_ref, out_ref):
    place = Place(given)
    slot, pairs, part, odd = place.slot, place.pairs, place.part, place.odd
    held_slots = out_ref.shape[0] // (2 * B)
    unit = jnp.where(eye_mask(), 1.0, 0.0)
    zero = jnp.zeros_like(unit)
    pasts = older(odd, mu_ref[...], mw_ref[...])
    nodes = [
        (unit, *came_from(slot, is_first, pairs), past, at)
        for is_first, past, at in ((True, pasts[0], 0), (False, pasts[1], B))
    ]
    for step in reversed(range(STEPS - 1)):
        offs = step_offsets(offs_ref, step)
        below = []
        for block, node, was_first, past, at in nodes:
            top, low = rotate_back(
                jnp.where(was_first, block, zero),
                jnp.where(was_first, zero, block),
                read_record(past[:RECORD]),
                offs,
            )
            if step == 0:
                below.append((top, low, node, at))
                continue
            half = (past.shape[0] - RECORD) // 2
            top_past, low_past = past[RECORD : RECORD + half], past[RECORD + half :]
            below.append((top, *came_from(node, True, pairs), top_past, at))
            below.append((low, *came_from(node, False, pairs), low_past, at))
        nodes = below
    out_ref[...] = jnp.zeros_like(out_ref)
    for top, low, node, column in nodes:

        @pl.when(node // held_slots == part)
        def _():
            at = pl.multiple_of((node - part * held_slots) * (2 * B), 2 * B)
            out_ref[pl.ds(at, B), column : column + B] += top.T
            out_ref[pl.ds(at + B, B), column : column + B] += low.T


def vectors_before_last(height, offsets, messages):
    return call(vectors_kernel, [(height, 2 * B)], (offsets, *messages))[0]


def last_kernel(count, offs_ref, *refs):
    parts, refs = refs[:count], refs[count:]
    mu_ref, mw_ref, x_ref, v_ref, x_out, v_out, x_held, v_held, sems = refs
    odd = Place(given).odd
    gram = tree_sum([p[...] for p in parts])
    across = jnp.where(odd, gram, gram.T)
    offs = step_offsets(offs_ref, STEPS - 1)
    _, rotation, _, _ = cross_solve(across, odd, mu_ref[...], mw_ref[...], offs)
    copies = []

    def put(source, held, out, at):
        held[at, :] = product(source[at, :], rotation)
        copies.append(pltpu.make_async_copy(held.at[at], out.at[at], sems.at[len(copies)]))
        copies[-1].start()

    size = x_ref.shape[0] // PIECES
    for i in range(PIECES):
        put(x_ref, x_held, x_out, pl.ds(i * size, size))
    put(v_ref, v_held, v_out, pl.ds(0, v_ref.shape[0]))
    for copy in copies:
        copy.wait()


def last_step(offsets, parts, messages, x, v):
    outside = pl.BlockSpec(memory_space=pl.ANY)
    return pl.pallas_call(
        functools.partial(last_kernel, len(parts)),
        out_shape=tuple(jax.ShapeDtypeStruct(a.shape, jnp.float32) for a in (x, v)),
        in_specs=[VMEM] * (len(parts) + 5),
        out_specs=(outside, outside),
        scratch_shapes=[pltpu.VMEM(a.shape, jnp.float32) for a in (x, v)]
        + [pltpu.SemaphoreType.DMA((PIECES + 1,))],
        compiler_params=PARAMS,
    )(offsets, *parts, *messages, x, v)


def in_stages(partial, layout):
    distance, count = 1, lax.axis_size("row")
    while 2 * distance < count:
        partial = partial + send(partial, layout, layout, other_part(distance))
        distance *= 2
    if distance < count:
        return [partial, send(partial, layout, layout, other_part(distance))]
    return [partial]


def at_once(partial, layout):
    others = range(1, lax.axis_size("row"))
    return [partial] + [send(partial, layout, layout, other_part(d)) for d in others]


def body(whitened, offsets):
    rows, width = whitened.shape
    height = lax.axis_size("pair") * width // lax.axis_size("row")

    raw = send(whitened, given, crossed, inner)
    terms = in_stages(whole_gram(whitened), given)
    rotation, near, far = solved(0, given, offsets, terms)
    u = send(near, given, crossed, inner)
    (block,) = turned(rows, (EITHER, RAW), given, rotation, near, far, whitened)
    (far,) = turned(rows, (RAW, JOINED), given, rotation, near, far, whitened)
    w = send(far, given, crossed, outer)
    block = send(block, given, given, other_part(1))
    block = ready(0, offsets, u, block, raw)
    x, mw = arrive(block, w, far)

    raw = send(x, crossed, crossed, outer, swap=False)
    terms = at_once(pair_gram(x), crossed)
    rotation, near, far = solved(1, crossed, offsets, terms, (u, mw))
    w = send(far, crossed, crossed, outer)
    (near,) = turned(rows, (JOINED, RAW), crossed, rotation, near, far, x)
    u = send(near, crossed, crossed, inner)
    half, cross, mu, mw = arrive_raw(1, rows, offsets, u, w, far, ahead(u, raw))
    block = outer_block(raw, half)

    terms = at_once(cross, crossed)
    rotation, near, far = solved(2, crossed, offsets, terms, (mu, mw))
    (joined,) = turned(rows, (RAW, JOINED), crossed, rotation, near, far, u, block)
    (near,) = turned(rows, (JOINED, RAW), crossed, rotation, near, far, u, block)
    far = joined
    w = send(far, crossed, given, outer)
    u = send(near, crossed, given, inner)
    terms = in_stages(last_gram(rows, (u, w, far)), given)
    x, mu, mw = settle(rows, (u, w, far))
    vectors = vectors_before_last(height, offsets, (mu, mw))
    return last_step(offsets, terms, (mu, mw), x, vectors)


def solution(mesh):
    in_specs = (P("row", "pair"), P())
    out_specs = (P("row", "pair"), P("row", "pair"))
    return jax.shard_map(body, mesh=mesh, in_specs=in_specs, out_specs=out_specs, check_vma=False)
```

```python
import functools

import jax
import jax.numpy as jnp
from jax import lax
from jax.experimental import pallas as pl
from jax.experimental.pallas import tpu as pltpu
from jax.sharding import PartitionSpec as P

B = 128
ROUNDS = 4
STEPS = 4
RECORD = 2 * ROUNDS
PIECES = 4
HALF = B // 2
PACKED = HALF + 8
AXES = ("pair", "row")
PARAMS = pltpu.CompilerParams(vmem_limit_bytes=40 * 1024 * 1024)
VMEM = pl.BlockSpec(memory_space=pltpu.VMEM)


def given(slot, part):
    return slot, part


def crossed(slot, part):
    return (slot & ~1) | (part & 1), (part & ~1) | (slot & 1)


def route(source, target, change, swap=True):
    pairs, rows = lax.axis_size("pair"), lax.axis_size("row")
    line = []
    for slot in range(pairs):
        for part in range(rows):
            a = source(slot, part)
            b = target(*change(slot, part, pairs))
            if swap and a == b:
                b = a[0], a[1] ^ (rows // 2)
            line.append((a[0] * rows + a[1], b[0] * rows + b[1]))
    return line


def inner(slot, part, pairs):
    return slot ^ 1, part


def outer(slot, part, pairs):
    if slot == 0 or slot == pairs - 1:
        return slot, part
    return (slot + 1 if slot & 1 else slot - 1), part


def send(x, source, target, change, swap=True):
    return lax.ppermute(x, AXES, route(source, target, change, swap))


def other_part(distance):
    return lambda slot, part, pairs: (slot, part ^ distance)


def eye_mask():
    shape = (B, B)
    return lax.broadcasted_iota(jnp.int32, shape, 0) == lax.broadcasted_iota(jnp.int32, shape, 1)


def identity_halves():
    unit = jnp.where(eye_mask(), 1.0, 0.0)
    return [(unit, jnp.zeros_like(unit)), (jnp.zeros_like(unit), unit)]


def diagonal(mask, block):
    return jnp.sum(jnp.where(mask, block, 0.0), axis=0, keepdims=True)


def as_column(mask, row):
    return jnp.sum(jnp.where(mask, jnp.broadcast_to(row, (B, B)), 0.0), axis=1, keepdims=True)


def solve(first, across, second, offs):
    mask = eye_mask()
    distance = (index((B, B), 1) - index((B, B), 0)) & (B - 1)
    angles = []
    turns = identity_halves()
    a, d = diagonal(mask, first), diagonal(mask, second)
    held = 0
    for r in range(ROUNDS):
        turn, ahead = (held - offs[r]) & (B - 1), (offs[r] - held) & (B - 1)
        held = offs[r]
        c0 = pltpu.roll(diagonal(distance == ahead, across), turn, 1)
        d = pltpu.roll(d, turn, 1)
        across = pltpu.roll(across, turn, 1)
        second = pltpu.roll(pltpu.roll(second, turn, 1), turn, 0)
        turns = [(top, pltpu.roll(low, turn, 1)) for top, low in turns]
        h = 0.5 * (d - a)
        radius = jnp.sqrt(h * h + c0 * c0)
        sg = jnp.where(h >= 0, 1.0, -1.0)
        t = -sg * c0 / (jnp.abs(h) + radius + 1e-06 * (a + d))
        c = lax.rsqrt(1.0 + t * t)
        s = t * c
        angles.append((c, s))
        cc, sc = as_column(mask, c), as_column(mask, s)
        below = across.T
        first1 = first * c + across * s
        across1 = across * c - first * s
        below1 = below * c + second * s
        second1 = second * c - below * s
        first = cc * first1 + sc * below1
        across = cc * across1 + sc * second1
        second = cc * second1 - sc * across1
        moved = s * (s * (d - a) + 2.0 * (c * c0))
        a, d = a + moved, d - moved
        turns = [(c * top + s * low, c * low - s * top) for top, low in turns]
    first = jnp.where(mask, jnp.broadcast_to(a, (B, B)), first)
    second = jnp.where(mask, jnp.broadcast_to(d, (B, B)), second)
    second = pltpu.roll(pltpu.roll(second, held, 1), held, 0)
    turns = [(top, pltpu.roll(low, held, 1)) for top, low in turns]
    rotation = jnp.concatenate([jnp.concatenate(t, axis=1) for t in turns], axis=0)
    return angles, rotation, first, second


def rotate(first, second, angles, offs):
    held = 0
    for r in range(ROUNDS):
        c, s = angles[r]
        second = pltpu.roll(second, (held - offs[r]) & (B - 1), 1)
        held = offs[r]
        first, second = c * first + s * second, c * second - s * first
    return first, pltpu.roll(second, held, 1)


def rotate_back(first, second, angles, offs):
    held = 0
    for r in reversed(range(ROUNDS)):
        c, s = angles[r]
        second = pltpu.roll(second, (held - offs[r]) & (B - 1), 1)
        held = offs[r]
        first, second = c * first - s * second, s * first + c * second
    return first, pltpu.roll(second, held, 1)


def read_record(rows):
    return [(rows[r : r + 1], rows[ROUNDS + r : ROUNDS + r + 1]) for r in range(ROUNDS)]


def write_record(ref, at, angles):
    for r, (c, s) in enumerate(angles):
        ref[at + r : at + r + 1, :] = c
        ref[at + ROUNDS + r : at + ROUNDS + r + 1, :] = s


def index(shape, axis):
    return lax.broadcasted_iota(jnp.int32, shape, axis)


def pack(block):
    shape = (HALF, B)
    low = jnp.logical_and(index(shape, 1) < HALF, index(shape, 0) > index(shape, 1))
    rows = jnp.where(low, pltpu.roll(block[HALF:], HALF, 1), block[:HALF])
    return jnp.concatenate([rows, jnp.broadcast_to(diagonal(eye_mask(), block), (8, B))], axis=0)


def unpack(packed):
    rows, diag = packed[:HALF], packed[HALF : HALF + 1]
    turned = jnp.concatenate([rows, rows], axis=0).T
    shape = (HALF, B)
    i, j = index(shape, 0), index(shape, 1)
    left = j < HALF
    top = jnp.where(jnp.logical_and(left, i > j), turned[:HALF], rows)
    right = jnp.where(i > j - HALF, pltpu.roll(rows, HALF, 1), turned[:HALF])
    right = jnp.where(i == j - HALF, jnp.broadcast_to(diag, shape), right)
    return jnp.concatenate([top, jnp.where(left, turned[HALF:], right)], axis=0)


def pack_two(first, second):
    rows, cols = index((B, B), 0), index((B, B), 1)
    return [
        jnp.where(rows <= cols, first, second),
        jnp.broadcast_to(diagonal(eye_mask(), second), (8, B)),
    ]


def unpack_two(block, diag):
    rows, cols = index((B, B), 0), index((B, B), 1)
    turned = block.T
    second = jnp.where(rows > cols, block, turned)
    second = jnp.where(rows == cols, jnp.broadcast_to(diag, (B, B)), second)
    return jnp.where(rows <= cols, block, turned), second


def tree_sum(parts):
    parts = list(parts)
    while len(parts) > 1:
        parts = [parts[i] + parts[i + 1] for i in range(0, len(parts), 2)]
    return parts[0]


def split(x):
    high = x.astype(jnp.bfloat16)
    return high, (x - high.astype(jnp.float32)).astype(jnp.bfloat16)


def product(x, rotation):
    xh, xl = split(x)
    rh, rl = split(rotation)

    def dot(a, b):
        return jnp.dot(a, b, preferred_element_type=jnp.float32)

    return (dot(xl, rh) + dot(xh, rl)) + dot(xh, rh)


def step_offsets(offs_ref, step):
    return [offs_ref[step, r] for r in range(ROUNDS)]


def transposed_dot(left, right):
    lh, ll = split(left)
    rh, rl = split(right)

    def dot(a, b):
        dims = (((0,), (0,)), ((), ()))
        return lax.dot_general(a, b, dims, preferred_element_type=jnp.float32)

    return (dot(ll, rh) + dot(lh, rl)) + dot(lh, rh)


JOINED, RAW, EITHER = range(3)


def call(kernel, out_shapes, arrays):
    return pl.pallas_call(
        kernel,
        out_shape=tuple(jax.ShapeDtypeStruct(shape, jnp.float32) for shape in out_shapes),
        in_specs=[VMEM] * len(arrays),
        out_specs=tuple(VMEM for _ in out_shapes),
        compiler_params=PARAMS,
    )(*arrays)


class Place:
    def __init__(self, layout):
        pair, row = lax.axis_index("pair"), lax.axis_index("row")
        self.pairs = lax.axis_size("pair")
        self.slot, self.part = layout(pair, row)
        self.odd = (self.slot & 1) == 1
        self.edge = jnp.logical_or(self.slot == 0, self.slot == self.pairs - 1)
        self.gives_first = (
            jnp.logical_and(jnp.logical_not(self.odd), self.slot != 0),
            jnp.logical_or(self.odd, self.slot == 0),
        )
        self.same = ((pair ^ row) & 1) == 0
        self.stays = jnp.logical_and(self.edge, self.same)


def whole_gram_kernel(x_ref, out_ref):
    x = x_ref[...]
    gram = transposed_dot(x, x)
    squares = jnp.sum(x * x, axis=0, keepdims=True)
    mask = eye_mask()
    first = jnp.where(mask, jnp.broadcast_to(squares[:, :B], (B, B)), gram[:B, :B])
    second = jnp.where(mask, jnp.broadcast_to(squares[:, B:], (B, B)), gram[B:, B:])
    packed, diag = pack_two(first, second)
    out_ref[:B, :] = gram[:B, B:]
    out_ref[B : 2 * B, :] = packed
    out_ref[2 * B :, :] = diag


def whole_gram(x):
    return call(whole_gram_kernel, [(2 * B + 8, B)], (x,))[0]


def base_of(way, rows, message):
    return rows + (message.shape[0] if way == JOINED else 0)


def older(odd, mu, mw):
    hu, hw = mu[PACKED:], mw[PACKED:]
    return jnp.where(odd, hu, hw), jnp.where(odd, hw, hu)


def cross_solve(across, odd, mu, mw, offs):
    gu, gw = unpack(mu[:PACKED]), unpack(mw[:PACKED])
    return solve(jnp.where(odd, gu, gw), across, jnp.where(odd, gw, gu), offs)


def solve_kernel(step, layout, count, offs_ref, *refs):
    parts, refs = refs[:count], refs[count:]
    place = Place(layout)
    odd = place.odd
    offs = step_offsets(offs_ref, step)
    if step == 0:
        rotation_ref, *messages = refs
        gram = tree_sum([p[...] for p in parts])
        first, second = unpack_two(gram[B : 2 * B], gram[2 * B : 2 * B + 1])
        angles, rotation, first, second = solve(first, gram[:B], second, offs)
        past = ()
    else:
        mu_ref, mw_ref, rotation_ref, *messages = refs
        mu, mw = mu_ref[...], mw_ref[...]
        gram = tree_sum([p[...] for p in parts])
        angles, rotation, first, second = cross_solve(gram, odd, mu, mw, offs)
        past = older(odd, mu, mw)
    rotation_ref[...] = rotation
    packed = pack(first), pack(second)
    for message, gives_first in zip(messages, place.gives_first):
        message[:PACKED, :] = jnp.where(gives_first, *packed)
        write_record(message, PACKED, angles)
        at = PACKED + RECORD
        for history in past:
            message[at : at + history.shape[0], :] = history
            at += history.shape[0]


def solved(step, layout, offsets, parts, messages=()):
    small = PACKED + RECORD
    if step:
        small += 2 * (messages[0].shape[0] - PACKED)
    kernel = functools.partial(solve_kernel, step, layout, len(parts))
    shapes = [(2 * B, 2 * B), (small, B), (small, B)]
    return call(kernel, shapes, (offsets, *parts, *messages))


def turn_kernel(ways, layout, ordered, rows, left_out, rotation_ref, near_ref, far_ref, *refs):
    count = 1 if ordered else 2
    xs, outs = refs[:count], list(refs[count:])
    place = Place(layout)
    x = jnp.concatenate([x_ref[:rows, :] for x_ref in xs], axis=1)
    rotation = rotation_ref[...]
    if not ordered:
        swapped = jnp.concatenate([rotation[B:], rotation[:B]], axis=0)
        rotation = jnp.where(place.odd, rotation, swapped)
    if len(outs) == 1:
        side = place.gives_first[0 if ways[1] == RAW else 1]
        rotation = jnp.where(side, rotation[:, :B], rotation[:, B:])
    x = product(x, rotation)
    messages = [m for m, way in zip((near_ref, far_ref), ways) if way != RAW]
    sides = [g for g, way in zip(place.gives_first, ways) if way != RAW]
    kept = [way for way in ways if way != RAW]
    for out, message, gives_first, way in zip(outs, messages, sides, kept):
        start = left_out if message is far_ref else 0
        size = rows - start
        if way == JOINED:
            out[size:, :] = message[...]
        if len(outs) == 1:
            out[:size, :] = x[start:]
            continue

        @pl.when(gives_first)
        def _():
            out[:size, :] = x[start:, :B]

        @pl.when(jnp.logical_not(gives_first))
        def _():
            out[:size, :] = x[start:, B:]


def turned(rows, ways, layout, rotation, near, far, *xs, left_out=0):
    sizes = [base_of(way, rows, near) for way in ways if way != RAW]
    if ways[1] != RAW:
        sizes[-1] -= left_out
    kernel = functools.partial(turn_kernel, ways, layout, len(xs) == 1, rows, left_out)
    return call(kernel, [(size, B) for size in sizes], (rotation, near, far, *xs))


def half_rotation(angles, offs, take_first):
    halves = [rotate(top, low, angles, offs) for top, low in identity_halves()]
    return jnp.concatenate([jnp.where(take_first, top, low) for top, low in halves], axis=0)


def arrive_kernel(block_ref, w_ref, own_ref, x_ref, mw_ref):
    rows = x_ref.shape[0]
    place = Place(crossed)
    own = place.stays
    mw_ref[...] = jnp.where(own, own_ref[rows:, :], w_ref[rows:, :])

    def put(first, block):
        @pl.when(first)
        def _():
            x_ref[:, :B] = block

        @pl.when(jnp.logical_not(first))
        def _():
            x_ref[:, B:] = block

    put(place.odd, block_ref[...])
    even = jnp.logical_not(place.odd)

    @pl.when(own)
    def _():
        put(even, own_ref[:rows, :])

    @pl.when(jnp.logical_not(own))
    def _():
        put(even, w_ref[:rows, :])


def arrive(block, w, own):
    rows = block.shape[0]
    shapes = [(rows, 2 * B), (w.shape[0] - rows, B)]
    return call(arrive_kernel, shapes, (block, w, own))


def top_rows_kernel(x_ref, out_ref):
    out_ref[...] = x_ref[: out_ref.shape[0], :]


def top_rows(x, size):
    return call(top_rows_kernel, [(size, x.shape[1])], (x,))[0]


def pair_gram_kernel(x_ref, out_ref):
    out_ref[...] = transposed_dot(x_ref[:, :B], x_ref[:, B:])


def pair_gram(x):
    return call(pair_gram_kernel, [(B, B)], (x,))[0]


def ahead_kernel(u_ref, raw_ref, out_ref):
    out_ref[...] = transposed_dot(u_ref[: raw_ref.shape[0], :], raw_ref[...])


def ahead(u, raw):
    return call(ahead_kernel, [(B, 2 * B)], (u, raw))[0]


def arrive_raw_kernel(step, rows, offs_ref, u_ref, w_ref, own_ref, ahead_ref, *refs):
    half_ref, gram_ref, mu_ref, mw_ref = refs
    place = Place(crossed)
    own = place.edge
    mu_ref[...] = u_ref[rows:, :]
    rest = w_ref.shape[0] - mw_ref.shape[0]
    mw_ref[...] = jnp.where(own, own_ref[rest:, :], w_ref[rest:, :])
    at = slice(rest + PACKED, rest + PACKED + RECORD)
    angles = read_record(jnp.where(own, own_ref[at, :], w_ref[at, :]))
    takes_first = jnp.logical_or(jnp.logical_not(place.odd), place.slot == place.pairs - 1)
    half = half_rotation(angles, step_offsets(offs_ref, step), takes_first)
    half_ref[...] = half
    tail = jnp.where(own, own_ref[:rest, :], w_ref[:rest, :])
    gram = product(ahead_ref[...], half) + transposed_dot(u_ref[rows - rest : rows, :], tail)
    gram_ref[...] = jnp.where(place.odd, gram, gram.T)


def arrive_raw(step, rows, offsets, u, w, own, products):
    kernel = functools.partial(arrive_raw_kernel, step, rows)
    small = (u.shape[0] - rows, B)
    return call(kernel, [(2 * B, B), (B, B), small, small], (offsets, u, w, own, products))


def outer_block_kernel(raw_ref, half_ref, w_ref, own_ref, out_ref):
    size = raw_ref.shape[0]
    rest = out_ref.shape[0] - size
    out_ref[:size, :] = product(raw_ref[...], half_ref[...])
    out_ref[size:, :] = jnp.where(Place(crossed).edge, own_ref[:rest, :], w_ref[:rest, :])


def outer_block(rows, raw, half, w, own):
    return call(outer_block_kernel, [(rows, B)], (raw, half, w, own))[0]


def ready_kernel(step, offs_ref, u_ref, block_ref, raw_ref, out_ref):
    place = Place(crossed)

    @pl.when(place.same)
    def _():
        takes_first = jnp.logical_and(place.odd, place.slot != 1)
        angles = read_record(u_ref[PACKED : PACKED + RECORD, :])
        half = half_rotation(angles, step_offsets(offs_ref, step), takes_first)
        out_ref[...] = product(raw_ref[...], half)

    @pl.when(jnp.logical_not(place.same))
    def _():
        out_ref[...] = block_ref[...]


def ready(step, offsets, u, block, raw):
    kernel = functools.partial(ready_kernel, step)
    return call(kernel, [block.shape], (offsets, u, block, raw))[0]


def last_gram_kernel(rows, u_ref, w_ref, own_ref, out_ref):
    own = Place(given).stays

    @pl.when(own)
    def _():
        out_ref[...] = transposed_dot(u_ref[:rows, :], own_ref[:rows, :])

    @pl.when(jnp.logical_not(own))
    def _():
        out_ref[...] = transposed_dot(u_ref[:rows, :], w_ref[:rows, :])


def last_gram(rows, messages):
    return call(functools.partial(last_gram_kernel, rows), [(B, B)], messages)[0]


def settle_kernel(u_ref, w_ref, own_ref, x_ref, mu_ref, mw_ref):
    rows = x_ref.shape[0]
    place = Place(given)
    odd, own = place.odd, place.stays
    u, w = u_ref[...], jnp.where(own, own_ref[...], w_ref[...])
    x_ref[:, :B] = jnp.where(odd, u[:rows], w[:rows])
    x_ref[:, B:] = jnp.where(odd, w[:rows], u[:rows])
    mu_ref[...] = u[rows:]
    mw_ref[...] = w[rows:]


def settle(rows, messages):
    small = messages[0].shape[0] - rows
    shapes = [(rows, 2 * B), (small, B), (small, B)]
    return call(settle_kernel, shapes, messages)


def came_from(slot, is_first, pairs):
    if is_first:
        return jnp.where(slot == 0, 0, slot - 1), slot != 1
    last = slot == pairs - 1
    return jnp.where(last, slot, slot + 1), last


def vectors_kernel(offs_ref, mu_ref, mw_ref, out_ref):
    place = Place(given)
    slot, pairs, part, odd = place.slot, place.pairs, place.part, place.odd
    held_slots = out_ref.shape[0] // (2 * B)
    unit = jnp.where(eye_mask(), 1.0, 0.0)
    zero = jnp.zeros_like(unit)
    pasts = older(odd, mu_ref[...], mw_ref[...])
    nodes = [
        (unit, *came_from(slot, is_first, pairs), past, at)
        for is_first, past, at in ((True, pasts[0], 0), (False, pasts[1], B))
    ]
    for step in reversed(range(STEPS - 1)):
        offs = step_offsets(offs_ref, step)
        below = []
        for block, node, was_first, past, at in nodes:
            top, low = rotate_back(
                jnp.where(was_first, block, zero),
                jnp.where(was_first, zero, block),
                read_record(past[:RECORD]),
                offs,
            )
            if step == 0:
                below.append((top, low, node, at))
                continue
            half = (past.shape[0] - RECORD) // 2
            top_past, low_past = past[RECORD : RECORD + half], past[RECORD + half :]
            below.append((top, *came_from(node, True, pairs), top_past, at))
            below.append((low, *came_from(node, False, pairs), low_past, at))
        nodes = below
    out_ref[...] = jnp.zeros_like(out_ref)
    for top, low, node, column in nodes:

        @pl.when(node // held_slots == part)
        def _():
            at = pl.multiple_of((node - part * held_slots) * (2 * B), 2 * B)
            out_ref[pl.ds(at, B), column : column + B] += top.T
            out_ref[pl.ds(at + B, B), column : column + B] += low.T


def vectors_before_last(height, offsets, messages):
    return call(vectors_kernel, [(height, 2 * B)], (offsets, *messages))[0]


def last_kernel(count, offs_ref, *refs):
    parts, refs = refs[:count], refs[count:]
    mu_ref, mw_ref, x_ref, v_ref, x_out, v_out, x_held, v_held, sems = refs
    odd = Place(given).odd
    gram = tree_sum([p[...] for p in parts])
    across = jnp.where(odd, gram, gram.T)
    offs = step_offsets(offs_ref, STEPS - 1)
    _, rotation, _, _ = cross_solve(across, odd, mu_ref[...], mw_ref[...], offs)
    copies = []

    def put(source, held, out, at):
        held[at, :] = product(source[at, :], rotation)
        copies.append(pltpu.make_async_copy(held.at[at], out.at[at], sems.at[len(copies)]))
        copies[-1].start()

    size = x_ref.shape[0] // PIECES
    for i in range(PIECES):
        put(x_ref, x_held, x_out, pl.ds(i * size, size))
    put(v_ref, v_held, v_out, pl.ds(0, v_ref.shape[0]))
    for copy in copies:
        copy.wait()


def last_step(offsets, parts, messages, x, v):
    outside = pl.BlockSpec(memory_space=pl.ANY)
    return pl.pallas_call(
        functools.partial(last_kernel, len(parts)),
        out_shape=tuple(jax.ShapeDtypeStruct(a.shape, jnp.float32) for a in (x, v)),
        in_specs=[VMEM] * (len(parts) + 5),
        out_specs=(outside, outside),
        scratch_shapes=[pltpu.VMEM(a.shape, jnp.float32) for a in (x, v)]
        + [pltpu.SemaphoreType.DMA((PIECES + 1,))],
        compiler_params=PARAMS,
    )(offsets, *parts, *messages, x, v)


def in_stages(partial, layout):
    distance, count = 1, lax.axis_size("row")
    while 2 * distance < count:
        partial = partial + send(partial, layout, layout, other_part(distance))
        distance *= 2
    if distance < count:
        return [partial, send(partial, layout, layout, other_part(distance))]
    return [partial]


def at_once(partial, layout):
    others = range(1, lax.axis_size("row"))
    return [partial] + [send(partial, layout, layout, other_part(d)) for d in others]


def body(whitened, offsets):
    rows, width = whitened.shape
    height = lax.axis_size("pair") * width // lax.axis_size("row")

    raw = send(whitened, given, crossed, inner)
    terms = in_stages(whole_gram(whitened), given)
    rotation, near, far = solved(0, given, offsets, terms)
    u = send(near, given, crossed, inner)
    (block,) = turned(rows, (EITHER, RAW), given, rotation, near, far, whitened)
    (far,) = turned(rows, (RAW, JOINED), given, rotation, near, far, whitened)
    w = send(far, given, crossed, outer)
    block = send(block, given, given, other_part(1))
    block = ready(0, offsets, u, block, raw)
    x, mw = arrive(block, w, far)

    size = rows // 128 * 112
    raw = send(top_rows(x, size), crossed, crossed, outer, swap=False)
    terms = at_once(pair_gram(x), crossed)
    rotation, near, far = solved(1, crossed, offsets, terms, (u, mw))
    ways = (JOINED, JOINED)
    near, far = turned(rows, ways, crossed, rotation, near, far, x, left_out=size)
    w = send(far, crossed, crossed, outer)
    u = send(near, crossed, crossed, inner)
    half, cross, mu, mw = arrive_raw(1, rows, offsets, u, w, far, ahead(u, raw))
    block = outer_block(rows, raw, half, w, far)

    terms = at_once(cross, crossed)
    rotation, near, far = solved(2, crossed, offsets, terms, (mu, mw))
    (joined,) = turned(rows, (RAW, JOINED), crossed, rotation, near, far, u, block)
    (near,) = turned(rows, (JOINED, RAW), crossed, rotation, near, far, u, block)
    far = joined
    w = send(far, crossed, given, outer)
    u = send(near, crossed, given, inner)
    terms = in_stages(last_gram(rows, (u, w, far)), given)
    x, mu, mw = settle(rows, (u, w, far))
    vectors = vectors_before_last(height, offsets, (mu, mw))
    return last_step(offsets, terms, (mu, mw), x, vectors)


def solution(mesh):
    in_specs = (P("row", "pair"), P())
    out_specs = (P("row", "pair"), P("row", "pair"))
    return jax.shard_map(body, mesh=mesh, in_specs=in_specs, out_specs=out_specs, check_vma=False)
```

```python
import functools

import jax
import jax.numpy as jnp
from jax import lax
from jax.experimental import pallas as pl
from jax.experimental.pallas import tpu as pltpu
from jax.sharding import PartitionSpec as P

B = 128
ROUNDS = 4
STEPS = 4
RECORD = 2 * ROUNDS
PIECES = 8
HALF = B // 2
PACKED = HALF + 8
AXES = ("pair", "row")
PARAMS = pltpu.CompilerParams(vmem_limit_bytes=40 * 1024 * 1024)
VMEM = pl.BlockSpec(memory_space=pltpu.VMEM)


def given(slot, part):
    return slot, part


def crossed(slot, part):
    return (slot & ~1) | (part & 1), (part & ~1) | (slot & 1)


def route(source, target, change, swap=True):
    pairs, rows = lax.axis_size("pair"), lax.axis_size("row")
    line = []
    for slot in range(pairs):
        for part in range(rows):
            a = source(slot, part)
            b = target(*change(slot, part, pairs))
            if swap and a == b:
                b = a[0], a[1] ^ (rows // 2)
            line.append((a[0] * rows + a[1], b[0] * rows + b[1]))
    return line


def inner(slot, part, pairs):
    return slot ^ 1, part


def outer(slot, part, pairs):
    if slot == 0 or slot == pairs - 1:
        return slot, part
    return (slot + 1 if slot & 1 else slot - 1), part


def send(x, source, target, change, swap=True):
    return lax.ppermute(x, AXES, route(source, target, change, swap))


def other_part(distance):
    return lambda slot, part, pairs: (slot, part ^ distance)


def eye_mask():
    shape = (B, B)
    return lax.broadcasted_iota(jnp.int32, shape, 0) == lax.broadcasted_iota(jnp.int32, shape, 1)


def identity_halves():
    unit = jnp.where(eye_mask(), 1.0, 0.0)
    return [(unit, jnp.zeros_like(unit)), (jnp.zeros_like(unit), unit)]


def diagonal(mask, block):
    return jnp.sum(jnp.where(mask, block, 0.0), axis=0, keepdims=True)


def as_column(mask, row):
    return jnp.sum(jnp.where(mask, jnp.broadcast_to(row, (B, B)), 0.0), axis=1, keepdims=True)


def solve(first, across, second, offs):
    mask = eye_mask()
    distance = (index((B, B), 1) - index((B, B), 0)) & (B - 1)
    angles = []
    turns = identity_halves()
    a, d = diagonal(mask, first), diagonal(mask, second)
    held = 0
    for r in range(ROUNDS):
        turn, ahead = (held - offs[r]) & (B - 1), (offs[r] - held) & (B - 1)
        held = offs[r]
        c0 = pltpu.roll(diagonal(distance == ahead, across), turn, 1)
        d = pltpu.roll(d, turn, 1)
        across = pltpu.roll(across, turn, 1)
        second = pltpu.roll(pltpu.roll(second, turn, 1), turn, 0)
        turns = [(top, pltpu.roll(low, turn, 1)) for top, low in turns]
        h = 0.5 * (d - a)
        radius = jnp.sqrt(h * h + c0 * c0)
        sg = jnp.where(h >= 0, 1.0, -1.0)
        t = -sg * c0 / (jnp.abs(h) + radius + 1e-06 * (a + d))
        c = lax.rsqrt(1.0 + t * t)
        s = t * c
        angles.append((c, s))
        cc, sc = as_column(mask, c), as_column(mask, s)
        below = across.T
        first1 = first * c + across * s
        across1 = across * c - first * s
        below1 = below * c + second * s
        second1 = second * c - below * s
        first = cc * first1 + sc * below1
        across = cc * across1 + sc * second1
        second = cc * second1 - sc * across1
        moved = s * (s * (d - a) + 2.0 * (c * c0))
        a, d = a + moved, d - moved
        turns = [(c * top + s * low, c * low - s * top) for top, low in turns]
    first = jnp.where(mask, jnp.broadcast_to(a, (B, B)), first)
    second = jnp.where(mask, jnp.broadcast_to(d, (B, B)), second)
    second = pltpu.roll(pltpu.roll(second, held, 1), held, 0)
    turns = [(top, pltpu.roll(low, held, 1)) for top, low in turns]
    rotation = jnp.concatenate([jnp.concatenate(t, axis=1) for t in turns], axis=0)
    return angles, rotation, first, second


def rotate(first, second, angles, offs):
    held = 0
    for r in range(ROUNDS):
        c, s = angles[r]
        second = pltpu.roll(second, (held - offs[r]) & (B - 1), 1)
        held = offs[r]
        first, second = c * first + s * second, c * second - s * first
    return first, pltpu.roll(second, held, 1)


def rotate_back(first, second, angles, offs):
    held = 0
    for r in reversed(range(ROUNDS)):
        c, s = angles[r]
        second = pltpu.roll(second, (held - offs[r]) & (B - 1), 1)
        held = offs[r]
        first, second = c * first - s * second, s * first + c * second
    return first, pltpu.roll(second, held, 1)


def read_record(rows):
    return [(rows[r : r + 1], rows[ROUNDS + r : ROUNDS + r + 1]) for r in range(ROUNDS)]


def write_record(ref, at, angles):
    for r, (c, s) in enumerate(angles):
        ref[at + r : at + r + 1, :] = c
        ref[at + ROUNDS + r : at + ROUNDS + r + 1, :] = s


def index(shape, axis):
    return lax.broadcasted_iota(jnp.int32, shape, axis)


def pack(block):
    shape = (HALF, B)
    low = jnp.logical_and(index(shape, 1) < HALF, index(shape, 0) > index(shape, 1))
    rows = jnp.where(low, pltpu.roll(block[HALF:], HALF, 1), block[:HALF])
    return jnp.concatenate([rows, jnp.broadcast_to(diagonal(eye_mask(), block), (8, B))], axis=0)


def unpack(packed):
    rows, diag = packed[:HALF], packed[HALF : HALF + 1]
    turned = jnp.concatenate([rows, rows], axis=0).T
    shape = (HALF, B)
    i, j = index(shape, 0), index(shape, 1)
    left = j < HALF
    top = jnp.where(jnp.logical_and(left, i > j), turned[:HALF], rows)
    right = jnp.where(i > j - HALF, pltpu.roll(rows, HALF, 1), turned[:HALF])
    right = jnp.where(i == j - HALF, jnp.broadcast_to(diag, shape), right)
    return jnp.concatenate([top, jnp.where(left, turned[HALF:], right)], axis=0)


def pack_two(first, second):
    rows, cols = index((B, B), 0), index((B, B), 1)
    return [
        jnp.where(rows <= cols, first, second),
        jnp.broadcast_to(diagonal(eye_mask(), second), (8, B)),
    ]


def unpack_two(block, diag):
    rows, cols = index((B, B), 0), index((B, B), 1)
    turned = block.T
    second = jnp.where(rows > cols, block, turned)
    second = jnp.where(rows == cols, jnp.broadcast_to(diag, (B, B)), second)
    return jnp.where(rows <= cols, block, turned), second


def tree_sum(parts):
    parts = list(parts)
    while len(parts) > 1:
        parts = [parts[i] + parts[i + 1] for i in range(0, len(parts), 2)]
    return parts[0]


def split(x):
    high = x.astype(jnp.bfloat16)
    return high, (x - high.astype(jnp.float32)).astype(jnp.bfloat16)


def product(x, rotation):
    xh, xl = split(x)
    rh, rl = split(rotation)

    def dot(a, b):
        return jnp.dot(a, b, preferred_element_type=jnp.float32)

    return (dot(xl, rh) + dot(xh, rl)) + dot(xh, rh)


def step_offsets(offs_ref, step):
    return [offs_ref[step, r] for r in range(ROUNDS)]


def transposed_dot(left, right):
    lh, ll = split(left)
    rh, rl = split(right)

    def dot(a, b):
        dims = (((0,), (0,)), ((), ()))
        return lax.dot_general(a, b, dims, preferred_element_type=jnp.float32)

    return (dot(ll, rh) + dot(lh, rl)) + dot(lh, rh)


JOINED, RAW, EITHER = range(3)


def call(kernel, out_shapes, arrays):
    return pl.pallas_call(
        kernel,
        out_shape=tuple(jax.ShapeDtypeStruct(shape, jnp.float32) for shape in out_shapes),
        in_specs=[VMEM] * len(arrays),
        out_specs=tuple(VMEM for _ in out_shapes),
        compiler_params=PARAMS,
    )(*arrays)


class Place:
    def __init__(self, layout):
        pair, row = lax.axis_index("pair"), lax.axis_index("row")
        self.pairs = lax.axis_size("pair")
        self.slot, self.part = layout(pair, row)
        self.odd = (self.slot & 1) == 1
        self.edge = jnp.logical_or(self.slot == 0, self.slot == self.pairs - 1)
        self.gives_first = (
            jnp.logical_and(jnp.logical_not(self.odd), self.slot != 0),
            jnp.logical_or(self.odd, self.slot == 0),
        )
        self.same = ((pair ^ row) & 1) == 0
        self.stays = jnp.logical_and(self.edge, self.same)


def whole_gram_kernel(x_ref, out_ref):
    x = x_ref[...]
    gram = transposed_dot(x, x)
    squares = jnp.sum(x * x, axis=0, keepdims=True)
    mask = eye_mask()
    first = jnp.where(mask, jnp.broadcast_to(squares[:, :B], (B, B)), gram[:B, :B])
    second = jnp.where(mask, jnp.broadcast_to(squares[:, B:], (B, B)), gram[B:, B:])
    packed, diag = pack_two(first, second)
    out_ref[:B, :] = gram[:B, B:]
    out_ref[B : 2 * B, :] = packed
    out_ref[2 * B :, :] = diag


def whole_gram(x):
    return call(whole_gram_kernel, [(2 * B + 8, B)], (x,))[0]


def base_of(way, rows, message):
    return rows + (message.shape[0] if way == JOINED else 0)


def older(odd, mu, mw):
    hu, hw = mu[PACKED:], mw[PACKED:]
    return jnp.where(odd, hu, hw), jnp.where(odd, hw, hu)


def cross_solve(across, odd, mu, mw, offs):
    gu, gw = unpack(mu[:PACKED]), unpack(mw[:PACKED])
    return solve(jnp.where(odd, gu, gw), across, jnp.where(odd, gw, gu), offs)


def solve_kernel(step, layout, count, offs_ref, *refs):
    parts, refs = refs[:count], refs[count:]
    place = Place(layout)
    odd = place.odd
    offs = step_offsets(offs_ref, step)
    if step == 0:
        rotation_ref, *messages = refs
        gram = tree_sum([p[...] for p in parts])
        first, second = unpack_two(gram[B : 2 * B], gram[2 * B : 2 * B + 1])
        angles, rotation, first, second = solve(first, gram[:B], second, offs)
        past = ()
    else:
        mu_ref, mw_ref, rotation_ref, *messages = refs
        mu, mw = mu_ref[...], mw_ref[...]
        gram = tree_sum([p[...] for p in parts])
        angles, rotation, first, second = cross_solve(gram, odd, mu, mw, offs)
        past = older(odd, mu, mw)
    rotation_ref[...] = rotation
    packed = pack(first), pack(second)
    for message, gives_first in zip(messages, place.gives_first):
        message[:PACKED, :] = jnp.where(gives_first, *packed)
        write_record(message, PACKED, angles)
        at = PACKED + RECORD
        for history in past:
            message[at : at + history.shape[0], :] = history
            at += history.shape[0]


def solved(step, layout, offsets, parts, messages=()):
    small = PACKED + RECORD
    if step:
        small += 2 * (messages[0].shape[0] - PACKED)
    kernel = functools.partial(solve_kernel, step, layout, len(parts))
    shapes = [(2 * B, 2 * B), (small, B), (small, B)]
    return call(kernel, shapes, (offsets, *parts, *messages))


def turn_kernel(ways, layout, ordered, rows, left_out, rotation_ref, near_ref, far_ref, *refs):
    count = 1 if ordered else 2
    xs, outs = refs[:count], list(refs[count:])
    place = Place(layout)
    x = jnp.concatenate([x_ref[:rows, :] for x_ref in xs], axis=1)
    rotation = rotation_ref[...]
    if not ordered:
        swapped = jnp.concatenate([rotation[B:], rotation[:B]], axis=0)
        rotation = jnp.where(place.odd, rotation, swapped)
    if len(outs) == 1:
        side = place.gives_first[0 if ways[1] == RAW else 1]
        rotation = jnp.where(side, rotation[:, :B], rotation[:, B:])
    x = product(x, rotation)
    messages = [m for m, way in zip((near_ref, far_ref), ways) if way != RAW]
    sides = [g for g, way in zip(place.gives_first, ways) if way != RAW]
    kept = [way for way in ways if way != RAW]
    for out, message, gives_first, way in zip(outs, messages, sides, kept):
        start = left_out if message is far_ref else 0
        size = rows - start
        if way == JOINED:
            out[size:, :] = message[...]
        if len(outs) == 1:
            out[:size, :] = x[start:]
            continue

        @pl.when(gives_first)
        def _():
            out[:size, :] = x[start:, :B]

        @pl.when(jnp.logical_not(gives_first))
        def _():
            out[:size, :] = x[start:, B:]


def turned(rows, ways, layout, rotation, near, far, *xs, left_out=0):
    sizes = [base_of(way, rows, near) for way in ways if way != RAW]
    if ways[1] != RAW:
        sizes[-1] -= left_out
    kernel = functools.partial(turn_kernel, ways, layout, len(xs) == 1, rows, left_out)
    return call(kernel, [(size, B) for size in sizes], (rotation, near, far, *xs))


def half_rotation(angles, offs, take_first):
    halves = [rotate(top, low, angles, offs) for top, low in identity_halves()]
    return jnp.concatenate([jnp.where(take_first, top, low) for top, low in halves], axis=0)


def arrive_kernel(block_ref, w_ref, own_ref, x_ref, mw_ref):
    rows = x_ref.shape[0]
    place = Place(crossed)
    own = place.stays
    mw_ref[...] = jnp.where(own, own_ref[rows:, :], w_ref[rows:, :])

    def put(first, block):
        @pl.when(first)
        def _():
            x_ref[:, :B] = block

        @pl.when(jnp.logical_not(first))
        def _():
            x_ref[:, B:] = block

    put(place.odd, block_ref[...])
    even = jnp.logical_not(place.odd)

    @pl.when(own)
    def _():
        put(even, own_ref[:rows, :])

    @pl.when(jnp.logical_not(own))
    def _():
        put(even, w_ref[:rows, :])


def arrive(block, w, own):
    rows = block.shape[0]
    shapes = [(rows, 2 * B), (w.shape[0] - rows, B)]
    return call(arrive_kernel, shapes, (block, w, own))


def top_rows_kernel(x_ref, out_ref):
    out_ref[...] = x_ref[: out_ref.shape[0], :]


def top_rows(x, size):
    return call(top_rows_kernel, [(size, x.shape[1])], (x,))[0]


def pair_gram_kernel(x_ref, out_ref):
    out_ref[...] = transposed_dot(x_ref[:, :B], x_ref[:, B:])


def pair_gram(x):
    return call(pair_gram_kernel, [(B, B)], (x,))[0]


def ahead_kernel(u_ref, raw_ref, out_ref):
    out_ref[...] = transposed_dot(u_ref[: raw_ref.shape[0], :], raw_ref[...])


def ahead(u, raw):
    return call(ahead_kernel, [(B, 2 * B)], (u, raw))[0]


def arrive_raw_kernel(step, rows, offs_ref, u_ref, w_ref, own_ref, ahead_ref, *refs):
    half_ref, gram_ref, mu_ref, mw_ref = refs
    place = Place(crossed)
    own = place.edge
    mu_ref[...] = u_ref[rows:, :]
    rest = w_ref.shape[0] - mw_ref.shape[0]
    mw_ref[...] = jnp.where(own, own_ref[rest:, :], w_ref[rest:, :])
    at = slice(rest + PACKED, rest + PACKED + RECORD)
    angles = read_record(jnp.where(own, own_ref[at, :], w_ref[at, :]))
    takes_first = jnp.logical_or(jnp.logical_not(place.odd), place.slot == place.pairs - 1)
    half = half_rotation(angles, step_offsets(offs_ref, step), takes_first)
    half_ref[...] = half
    tail = jnp.where(own, own_ref[:rest, :], w_ref[:rest, :])
    gram = product(ahead_ref[...], half) + transposed_dot(u_ref[rows - rest : rows, :], tail)
    gram_ref[...] = jnp.where(place.odd, gram, gram.T)


def arrive_raw(step, rows, offsets, u, w, own, products):
    kernel = functools.partial(arrive_raw_kernel, step, rows)
    small = (u.shape[0] - rows, B)
    return call(kernel, [(2 * B, B), (B, B), small, small], (offsets, u, w, own, products))


def outer_block_kernel(raw_ref, half_ref, w_ref, own_ref, out_ref):
    size = raw_ref.shape[0]
    rest = out_ref.shape[0] - size
    out_ref[:size, :] = product(raw_ref[...], half_ref[...])
    out_ref[size:, :] = jnp.where(Place(crossed).edge, own_ref[:rest, :], w_ref[:rest, :])


def outer_block(rows, raw, half, w, own):
    return call(outer_block_kernel, [(rows, B)], (raw, half, w, own))[0]


def ready_kernel(step, offs_ref, u_ref, block_ref, raw_ref, out_ref):
    place = Place(crossed)

    @pl.when(place.same)
    def _():
        takes_first = jnp.logical_and(place.odd, place.slot != 1)
        angles = read_record(u_ref[PACKED : PACKED + RECORD, :])
        half = half_rotation(angles, step_offsets(offs_ref, step), takes_first)
        out_ref[...] = product(raw_ref[...], half)

    @pl.when(jnp.logical_not(place.same))
    def _():
        out_ref[...] = block_ref[...]


def ready(step, offsets, u, block, raw):
    kernel = functools.partial(ready_kernel, step)
    return call(kernel, [block.shape], (offsets, u, block, raw))[0]


def last_gram_kernel(rows, u_ref, w_ref, own_ref, out_ref):
    own = Place(given).stays

    @pl.when(own)
    def _():
        out_ref[...] = transposed_dot(u_ref[:rows, :], own_ref[:rows, :])

    @pl.when(jnp.logical_not(own))
    def _():
        out_ref[...] = transposed_dot(u_ref[:rows, :], w_ref[:rows, :])


def last_gram(rows, messages):
    return call(functools.partial(last_gram_kernel, rows), [(B, B)], messages)[0]


def settle_kernel(u_ref, w_ref, own_ref, x_ref, mu_ref, mw_ref):
    rows = x_ref.shape[0]
    place = Place(given)
    odd, own = place.odd, place.stays
    u, w = u_ref[...], jnp.where(own, own_ref[...], w_ref[...])
    x_ref[:, :B] = jnp.where(odd, u[:rows], w[:rows])
    x_ref[:, B:] = jnp.where(odd, w[:rows], u[:rows])
    mu_ref[...] = u[rows:]
    mw_ref[...] = w[rows:]


def settle(rows, messages):
    small = messages[0].shape[0] - rows
    shapes = [(rows, 2 * B), (small, B), (small, B)]
    return call(settle_kernel, shapes, messages)


def came_from(slot, is_first, pairs):
    if is_first:
        return jnp.where(slot == 0, 0, slot - 1), slot != 1
    last = slot == pairs - 1
    return jnp.where(last, slot, slot + 1), last


def vectors_kernel(offs_ref, mu_ref, mw_ref, out_ref):
    place = Place(given)
    slot, pairs, part, odd = place.slot, place.pairs, place.part, place.odd
    held_slots = out_ref.shape[0] // (2 * B)
    unit = jnp.where(eye_mask(), 1.0, 0.0)
    zero = jnp.zeros_like(unit)
    pasts = older(odd, mu_ref[...], mw_ref[...])
    nodes = [
        (unit, *came_from(slot, is_first, pairs), past, at)
        for is_first, past, at in ((True, pasts[0], 0), (False, pasts[1], B))
    ]
    for step in reversed(range(STEPS - 1)):
        offs = step_offsets(offs_ref, step)
        below = []
        for block, node, was_first, past, at in nodes:
            top, low = rotate_back(
                jnp.where(was_first, block, zero),
                jnp.where(was_first, zero, block),
                read_record(past[:RECORD]),
                offs,
            )
            if step == 0:
                below.append((top, low, node, at))
                continue
            half = (past.shape[0] - RECORD) // 2
            top_past, low_past = past[RECORD : RECORD + half], past[RECORD + half :]
            below.append((top, *came_from(node, True, pairs), top_past, at))
            below.append((low, *came_from(node, False, pairs), low_past, at))
        nodes = below
    out_ref[...] = jnp.zeros_like(out_ref)
    for top, low, node, column in nodes:

        @pl.when(node // held_slots == part)
        def _():
            at = pl.multiple_of((node - part * held_slots) * (2 * B), 2 * B)
            out_ref[pl.ds(at, B), column : column + B] += top.T
            out_ref[pl.ds(at + B, B), column : column + B] += low.T


def vectors_before_last(height, offsets, messages):
    return call(vectors_kernel, [(height, 2 * B)], (offsets, *messages))[0]


def last_kernel(count, offs_ref, *refs):
    parts, refs = refs[:count], refs[count:]
    mu_ref, mw_ref, x_ref, v_ref, x_out, v_out, x_held, v_held, sems = refs
    odd = Place(given).odd
    gram = tree_sum([p[...] for p in parts])
    across = jnp.where(odd, gram, gram.T)
    offs = step_offsets(offs_ref, STEPS - 1)
    _, rotation, _, _ = cross_solve(across, odd, mu_ref[...], mw_ref[...], offs)
    copies = []

    def put(source, held, out, at):
        held[at, :] = product(source[at, :], rotation)
        copies.append(pltpu.make_async_copy(held.at[at], out.at[at], sems.at[len(copies)]))
        copies[-1].start()

    size = x_ref.shape[0] // PIECES
    for i in range(PIECES):
        put(x_ref, x_held, x_out, pl.ds(i * size, size))
    put(v_ref, v_held, v_out, pl.ds(0, v_ref.shape[0]))
    for copy in copies:
        copy.wait()


def last_step(offsets, parts, messages, x, v):
    outside = pl.BlockSpec(memory_space=pl.ANY)
    return pl.pallas_call(
        functools.partial(last_kernel, len(parts)),
        out_shape=tuple(jax.ShapeDtypeStruct(a.shape, jnp.float32) for a in (x, v)),
        in_specs=[VMEM] * (len(parts) + 5),
        out_specs=(outside, outside),
        scratch_shapes=[pltpu.VMEM(a.shape, jnp.float32) for a in (x, v)]
        + [pltpu.SemaphoreType.DMA((PIECES + 1,))],
        compiler_params=PARAMS,
    )(offsets, *parts, *messages, x, v)


def in_stages(partial, layout):
    distance, count = 1, lax.axis_size("row")
    while 2 * distance < count:
        partial = partial + send(partial, layout, layout, other_part(distance))
        distance *= 2
    if distance < count:
        return [partial, send(partial, layout, layout, other_part(distance))]
    return [partial]


def at_once(partial, layout):
    others = range(1, lax.axis_size("row"))
    return [partial] + [send(partial, layout, layout, other_part(d)) for d in others]


def body(whitened, offsets):
    rows, width = whitened.shape
    height = lax.axis_size("pair") * width // lax.axis_size("row")

    raw = send(whitened, given, crossed, inner)
    terms = in_stages(whole_gram(whitened), given)
    rotation, near, far = solved(0, given, offsets, terms)
    u = send(near, given, crossed, inner)
    (block,) = turned(rows, (EITHER, RAW), given, rotation, near, far, whitened)
    (far,) = turned(rows, (RAW, JOINED), given, rotation, near, far, whitened)
    w = send(far, given, crossed, outer)
    block = send(block, given, given, other_part(1))
    block = ready(0, offsets, u, block, raw)
    x, mw = arrive(block, w, far)

    size = rows // 128 * 112
    raw = send(top_rows(x, size), crossed, crossed, outer, swap=False)
    terms = at_once(pair_gram(x), crossed)
    rotation, near, far = solved(1, crossed, offsets, terms, (u, mw))
    ways = (JOINED, JOINED)
    near, far = turned(rows, ways, crossed, rotation, near, far, x, left_out=size)
    w = send(far, crossed, crossed, outer)
    u = send(near, crossed, crossed, inner)
    half, cross, mu, mw = arrive_raw(1, rows, offsets, u, w, far, ahead(u, raw))
    block = outer_block(rows, raw, half, w, far)

    terms = at_once(cross, crossed)
    rotation, near, far = solved(2, crossed, offsets, terms, (mu, mw))
    (joined,) = turned(rows, (RAW, JOINED), crossed, rotation, near, far, u, block)
    (near,) = turned(rows, (JOINED, RAW), crossed, rotation, near, far, u, block)
    far = joined
    w = send(far, crossed, given, outer)
    u = send(near, crossed, given, inner)
    terms = in_stages(last_gram(rows, (u, w, far)), given)
    x, mu, mw = settle(rows, (u, w, far))
    vectors = vectors_before_last(height, offsets, (mu, mw))
    return last_step(offsets, terms, (mu, mw), x, vectors)


def solution(mesh):
    in_specs = (P("row", "pair"), P())
    out_specs = (P("row", "pair"), P("row", "pair"))
    return jax.shard_map(body, mesh=mesh, in_specs=in_specs, out_specs=out_specs, check_vma=False)
```
